128 devices in a mesh: grp: 2 (over x_hi), tp: 16 (over y, x_lo, core), dp: 4 (over z).
Axes of the slice: x: 4 (x_hi: 2, x_lo: 2; x = x_hi * 2 + x_lo), y: 4, z: 4, core: 2. Of those that a mesh axis runs over, the one named last changes fastest.
Arguments:
- prompt_tokens: bfloat16 [2, 4096, 8192], P('grp', 'dp', 'tp'), may hold values from -6 to 6
- norm_gain: float32 [8192], replicated, may hold values from 0.1 to 1.9
- q_weight: bfloat16 [8192, 8192], P(None, 'tp'), may hold values from -0.0625 to 0.0625
- k_weight: bfloat16 [8192, 1024], P(None, 'tp'), may hold values from -0.0625 to 0.0625
- v_weight: bfloat16 [8192, 1024], P(None, 'tp'), may hold values from -0.0625 to 0.0625
- q_bias: float32 [8192], replicated
- k_bias: float32 [1024], replicated
- v_bias: float32 [1024], replicated, may hold values from -3 to 3
- decode_tokens: bfloat16 [2, 3, 256, 8192], P('grp', None, 'dp', 'tp'), may hold values from -6 to 6
- k_cache: bfloat16 [2, 8192, 16, 1024], P('grp', 'dp', None, 'tp')
- v_cache: bfloat16 [2, 8192, 16, 1024], P('grp', 'dp', None, 'tp'), may hold values from -6 to 6
- block_table: int32 [2, 256, 32], P('grp', 'dp'), may hold values from 0 to 2047, as said below
- context_len: int32 [2, 256], P('grp', 'dp'), may hold values from 1 to 509, as said below
- prompt_dest: int32 [2, 16], P('grp', 'dp'), may hold values from 0 to 255, as said below
Outputs:
- prefill_out: bfloat16 [2, 4096, 8192], P('grp', 'dp', 'tp')
- decode_out: bfloat16 [2, 3, 256, 8192], P('grp', None, 'dp', 'tp')
The draws below stay inside these ranges and needn't reach their ends.
Inputs may be any that keep to these rules, and one draw needn't show every extreme that they name: `block_table`: the 32 entries of the rows of one replica's requests are all different. `context_len`: request r belongs to replica r // 64. Requests named in the other pool's prompt_dest have length 256; every replica of every pool has another request of length 509. `prompt_dest`: prompt n belongs to replica n // 4. The 4 prompts of one replica go to 4 different replicas of the other pool, and each replica receives exactly one prompt from each replica of the sending pool, all at different requests.
All inputs are finite; a program needn't handle non-finite values.
Results may differ from the reference program's by a relative error of at most 0.01.
The reference program's roundings to bfloat16 on the way count: a program that leaves them out, or rounds other values in their place, can miss the bound.
Values may be sent and summed in bfloat16 or wider, within the bound.
No kernel may reach another device: no remote copies, remote signals or barrier semaphores. Data moves between devices by JAX's collectives and lax.ppermute only.
A program may use at most 192 MiB of HBM per device.

```python
import math
import jax
import jax.numpy as jnp
from jax import lax

D = 8192
HEADS = 64
KV_HEADS = 8
HEAD_DIM = 128
BLOCK = 16
STEPS = 3
MAXB = 32
PROMPT = 256
REQ_DEV = 64
REPLICAS = 4
PROMPTS = 16
PTOKENS = 4096
REQ = 256
NBLK = 2048
N_GRP = 2


def dest_plan(key):
    key = jax.random.fold_in(key, 31)
    route_keys = jax.random.split(jax.random.fold_in(key, 1), 2 * REPLICAS)
    routes = jax.vmap(lambda one_key: jax.random.permutation(one_key, REPLICAS))(route_keys).reshape(2, REPLICAS, REPLICAS)
    seat_keys = jax.random.split(jax.random.fold_in(key, 2), 2 * REPLICAS)
    seats = jax.vmap(lambda one_key: jax.random.permutation(one_key, REQ_DEV))(seat_keys).reshape(2, REPLICAS, REQ_DEV)
    pool_index = jnp.arange(2)[:, None, None]
    source_index = jnp.arange(REPLICAS)[None, :, None]
    chosen = seats[pool_index, routes, source_index]
    destination = routes * REQ_DEV + chosen
    return (destination.reshape(2, PROMPTS).astype(jnp.int32), seats)


def draw_q_bias(key, part):
    key = jax.random.fold_in(key, 11)
    noise = 0.5 * jax.random.normal(key, (HEADS * HEAD_DIM,), jnp.float32)
    return noise


def draw_k_bias(key, part):
    key = jax.random.fold_in(key, 12)
    noise = 0.5 * jax.random.normal(key, (KV_HEADS * HEAD_DIM,), jnp.float32)
    return noise


def draw_k_cache(key, part):
    key = jax.random.fold_in(key, 13)
    noise = jax.random.normal(key, (2, REPLICAS * NBLK, BLOCK, KV_HEADS * HEAD_DIM), jnp.float32)
    return noise.astype(jnp.bfloat16)


def draw_block_table(key, part):
    key = jax.random.fold_in(key, 21)
    table_keys = jax.random.split(key, 2 * REPLICAS)
    orders = jax.vmap(lambda one_key: jax.random.permutation(one_key, NBLK))(table_keys)
    return orders.reshape(2, REQ, MAXB).astype(jnp.int32)


def draw_prompt_dest(key, part):
    destination, seats = dest_plan(key)
    return destination


def draw_context_len(key, part):
    destination, seats = dest_plan(key)
    key = jax.random.fold_in(key, 41)
    longest = MAXB * BLOCK - STEPS
    lengths = jax.random.randint(key, (2, REQ), 1, longest + 1)
    replica_ids = jnp.arange(REPLICAS)
    farthest = seats[:, :, REPLICAS] + replica_ids[None, :] * REQ_DEV
    receiving = 1 - jnp.arange(2)[:, None]
    lengths = lengths.at[receiving, farthest].set(longest)
    lengths = lengths.at[receiving, destination].set(PROMPT)
    return lengths.astype(jnp.int32)


def steps_of(own_key, shape, pieces, low, largest):
    loudness = 1.0
    for axis_at, blocks in pieces:
        steps = jax.random.uniform(jax.random.fold_in(jax.random.fold_in(own_key, 6), axis_at), (blocks,), jnp.float32, low / len(pieces), largest / len(pieces))
        loudness = loudness * jnp.repeat(jnp.exp(steps), shape[axis_at] // blocks).reshape((-1,) + (1,) * (len(shape) - 1 - axis_at))
    return loudness


def centred(rng, shape, deviation, most, cuts=(), kind=jnp.bfloat16):
    array = deviation * jax.random.normal(rng, shape, jnp.float32)
    if cuts:
        array = array * steps_of(rng, shape, cuts, -0.22, 0.18)
    return jnp.clip(array, -most, most).astype(kind)


def setup_inputs(seed: int = 0) -> dict:
    arg_keys = jax.random.split(jax.random.key(seed), 15)
    prompt_tokens = centred(arg_keys[0], (N_GRP, PTOKENS, D), 1.0, 6.0, ((0, 2), (1, 4), (2, 16)))
    norm_gain = jnp.clip(1.0 + 0.18 * jax.random.normal(arg_keys[1], (D,), jnp.float32), 0.1, 1.9)
    q_weight = centred(arg_keys[2], (D, HEADS * HEAD_DIM), D ** -0.5, 0.0625, ((1, 16),))
    k_weight = centred(arg_keys[3], (D, KV_HEADS * HEAD_DIM), D ** -0.5, 0.0625, ((1, 16),))
    v_weight = centred(arg_keys[4], (D, KV_HEADS * HEAD_DIM), D ** -0.5, 0.0625, ((1, 16),))
    q_bias = draw_q_bias(jax.random.fold_in(arg_keys[14], 71), 0)
    k_bias = draw_k_bias(jax.random.fold_in(arg_keys[14], 71), 0)
    v_bias = centred(arg_keys[7], (KV_HEADS * HEAD_DIM,), 0.5, 3.0, (), jnp.float32)
    decode_tokens = centred(arg_keys[8], (N_GRP, STEPS, REQ, D), 1.0, 6.0, ((0, 2), (2, 4), (3, 16)))
    k_cache = draw_k_cache(jax.random.fold_in(arg_keys[14], 71), 0)
    v_cache = centred(arg_keys[10], (N_GRP, REPLICAS * NBLK, BLOCK, KV_HEADS * HEAD_DIM), 1.0, 6.0, ((0, 2), (1, 4), (3, 16)))
    block_table = draw_block_table(jax.random.fold_in(arg_keys[14], 71), 0)
    context_len = draw_context_len(jax.random.fold_in(arg_keys[14], 71), 0)
    prompt_dest = draw_prompt_dest(jax.random.fold_in(arg_keys[14], 71), 0)
    return {"prompt_tokens": prompt_tokens, "norm_gain": norm_gain, "q_weight": q_weight, "k_weight": k_weight, "v_weight": v_weight, "q_bias": q_bias, "k_bias": k_bias, "v_bias": v_bias, "decode_tokens": decode_tokens, "k_cache": k_cache, "v_cache": v_cache, "block_table": block_table, "context_len": context_len, "prompt_dest": prompt_dest}


ROPE_BASE = 1000000.0
NORM_EPSILON = 1e-06
MASKED = -1e+30

def rotate(values, positions):
    half_dim = values.shape[-1] // 2
    exponent = jnp.arange(half_dim, dtype=jnp.float32) * (2.0 / values.shape[-1])
    frequency = jnp.power(jnp.float32(ROPE_BASE), -exponent)
    angle = positions.astype(jnp.float32)[..., None] * frequency
    cosine = jnp.cos(angle)[..., None, :]
    sine = jnp.sin(angle)[..., None, :]
    first = values[..., :half_dim]
    second = values[..., half_dim:]
    return jnp.concatenate([first * cosine - second * sine, second * cosine + first * sine], axis=-1)

def normalize(rows, norm_gain):
    widened = rows.astype(jnp.float32)
    mean_square = lax.optimization_barrier(jnp.mean(widened * widened, axis=-1, keepdims=True))
    return (widened * lax.rsqrt(mean_square + NORM_EPSILON) * norm_gain).astype(jnp.bfloat16)

def project(normed, weight, bias):
    return jnp.dot(normed, weight, preferred_element_type=jnp.float32) + bias

def make_rows(rows, positions, norm_gain, q_weight, k_weight, v_weight, q_bias, k_bias, v_bias):
    normed = normalize(rows, norm_gain)
    row_count = rows.shape[0]
    queries = rotate(project(normed, q_weight, q_bias).reshape(row_count, HEADS, HEAD_DIM), positions).astype(jnp.bfloat16)
    key_rows = rotate(project(normed, k_weight, k_bias).reshape(row_count, KV_HEADS, HEAD_DIM), positions).astype(jnp.bfloat16)
    value_rows = project(normed, v_weight, v_bias).astype(jnp.bfloat16).reshape(row_count, KV_HEADS, HEAD_DIM)
    return (queries, key_rows, value_rows)

def prompt_attention(item):
    queries, key_rows, value_rows = item
    group_size = HEADS // KV_HEADS
    grouped = queries.reshape(PROMPT, KV_HEADS, group_size, HEAD_DIM).astype(jnp.float32)
    scores = jnp.einsum('qhgd,khd->hgqk', grouped, key_rows.astype(jnp.float32)) * (1.0 / math.sqrt(HEAD_DIM))
    causal = jnp.arange(PROMPT)[:, None] >= jnp.arange(PROMPT)[None, :]
    scores = jnp.where(causal, scores, MASKED)
    weights = jax.nn.softmax(scores, axis=-1).astype(jnp.bfloat16)
    mixed = jnp.einsum('hgqk,khd->qhgd', weights.astype(jnp.float32), value_rows.astype(jnp.float32))
    return mixed.astype(jnp.bfloat16).reshape(PROMPT, HEADS * HEAD_DIM)

def request_attention(item, key_cache, value_cache):
    query_rows, table_row, last_position = item
    group_size = HEADS // KV_HEADS
    span = MAXB * BLOCK
    key_rows = key_cache[table_row].reshape(span, KV_HEADS, HEAD_DIM)
    value_rows = value_cache[table_row].reshape(span, KV_HEADS, HEAD_DIM)
    grouped = query_rows.reshape(KV_HEADS, group_size, HEAD_DIM).astype(jnp.float32)
    scores = jnp.einsum('hgd,lhd->hgl', grouped, key_rows.astype(jnp.float32)) * (1.0 / math.sqrt(HEAD_DIM))
    valid = jnp.arange(span) <= last_position
    scores = jnp.where(valid, scores, MASKED)
    weights = jax.nn.softmax(scores, axis=-1).astype(jnp.bfloat16)
    mixed = jnp.einsum('hgl,lhd->hdg', weights.astype(jnp.float32), value_rows.astype(jnp.float32))
    return mixed.astype(jnp.bfloat16).reshape(-1)

def to_blocks(rows):
    return rows.reshape(PROMPTS * (PROMPT // BLOCK), BLOCK, KV_HEADS * HEAD_DIM)

def reference(prompt_tokens, norm_gain, q_weight, k_weight, v_weight, q_bias, k_bias, v_bias, decode_tokens, k_cache, v_cache, block_table, context_len, prompt_dest):
    cache_cols = KV_HEADS * HEAD_DIM
    prompt_blocks = PROMPT // BLOCK
    key_pools = [k_cache[0], k_cache[1]]
    value_pools = [v_cache[0], v_cache[1]]
    prefill_parts = []
    handed = []
    for pool in range(2):
        positions = (jnp.arange(PTOKENS) % PROMPT).astype(jnp.int32)
        queries, key_rows, value_rows = make_rows(prompt_tokens[pool], positions, norm_gain, q_weight, k_weight, v_weight, q_bias, k_bias, v_bias)
        mixed = lax.map(prompt_attention, (queries.reshape(PROMPTS, PROMPT, HEADS, HEAD_DIM), key_rows.reshape(PROMPTS, PROMPT, KV_HEADS, HEAD_DIM), value_rows.reshape(PROMPTS, PROMPT, KV_HEADS, HEAD_DIM)))
        prefill_parts.append(mixed.reshape(PTOKENS, HEADS * HEAD_DIM))
        handed.append((to_blocks(key_rows), to_blocks(value_rows)))
    for pool in range(2):
        other_pool = 1 - pool
        destination = prompt_dest[pool]
        replica = destination // REQ_DEV
        targets = (block_table[other_pool][destination][:, :prompt_blocks] + (replica * NBLK)[:, None]).reshape(-1)
        key_pools[other_pool] = key_pools[other_pool].at[targets].set(handed[pool][0])
        value_pools[other_pool] = value_pools[other_pool].at[targets].set(handed[pool][1])
    decode_parts = []
    for pool in range(2):
        lengths = context_len[pool]
        request_ids = jnp.arange(REQ, dtype=jnp.int32)
        tables = block_table[pool] + (request_ids // REQ_DEV * NBLK)[:, None]
        key_cache = key_pools[pool]
        value_cache = value_pools[pool]
        step_parts = []
        for step in range(STEPS):
            positions = lengths + step
            queries, key_rows, value_rows = make_rows(decode_tokens[pool, step], positions, norm_gain, q_weight, k_weight, v_weight, q_bias, k_bias, v_bias)
            target_blocks = tables[request_ids, positions // BLOCK]
            target_slots = positions % BLOCK
            key_cache = key_cache.at[target_blocks, target_slots].set(key_rows.reshape(REQ, cache_cols))
            value_cache = value_cache.at[target_blocks, target_slots].set(value_rows.reshape(REQ, cache_cols))
            attend = lambda item, kc=key_cache, vc=value_cache: request_attention(item, kc, vc)
            step_parts.append(lax.map(attend, (queries, tables, positions)))
        decode_parts.append(jnp.stack(step_parts))
    return (jnp.stack(prefill_parts), jnp.stack(decode_parts))
```

```python
import functools
import math

import jax
import jax.numpy as jnp
from jax import lax
from jax.experimental import pallas as pl
from jax.experimental.pallas import tpu as pltpu
from jax.sharding import PartitionSpec as P

HEAD_DIM = 128
GROUP = 8
BLOCK = 16
MAXB = 32
PROMPT = 256
REQ_DEV = 64
STEPS = 3
ROPE_BASE = 1000000.0
NORM_EPSILON = 1e-06
MASKED = -1e30
SCALE = 1.0 / math.sqrt(HEAD_DIM)
FEATURES = 8192
CHUNK = 1024
PROMPT_ROWS = 512
DECODE_ROWS = 96
ROWS = PROMPT_ROWS + DECODE_ROWS
QCOLS = GROUP * HEAD_DIM
COLS = QCOLS + 2 * HEAD_DIM
HALF_REQ = REQ_DEV // 2
NBLK = 2048
PAIRS = HALF_REQ * MAXB
VMEM = 56 * 1024 * 1024

CORE = [(i, i ^ 1) for i in range(16)]
XSWAP = [(i, i ^ 2) for i in range(16)]
YUP = [(i, (i + 4) % 16) for i in range(16)]
YDOWN = [(i, (i + 12) % 16) for i in range(16)]
YFAR = [(i, (i + 8) % 16) for i in range(16)]

NT = (((1,), (1,)), ((), ()))
F32 = jnp.float32
BF16 = jnp.bfloat16


def send(array, pairs):
    return lax.ppermute(array, "tp", pairs)


def cost(flops, nbytes, trans=0):
    return pl.CostEstimate(flops=flops, bytes_accessed=nbytes, transcendentals=trans)


def params(**more):
    return pltpu.CompilerParams(vmem_limit_bytes=VMEM, **more)


def arrange_kernel(table_ref, k_ref, v_ref, k_out, v_out, pick):
    tile = table_ref.shape[1]
    block = lax.broadcasted_iota(jnp.int32, (NBLK, tile), 0)
    pick[...] = jnp.where(block == table_ref[...], 1.0, 0.0).astype(BF16)
    k_out[...] = jnp.dot(k_ref[...], pick[...], preferred_element_type=F32).astype(BF16)
    v_out[...] = jnp.dot(v_ref[...], pick[...], preferred_element_type=F32).astype(BF16)


def arrange(table_row, k_flat, v_flat):
    rows = k_flat.shape[0]
    tile = 256
    whole = pl.BlockSpec((rows, NBLK), lambda i: (0, 0))
    out = pl.BlockSpec((rows, tile), lambda i: (0, i))
    shape = jax.ShapeDtypeStruct((rows, PAIRS), BF16)
    return pl.pallas_call(
        arrange_kernel,
        grid=(PAIRS // tile,),
        in_specs=[pl.BlockSpec((1, tile), lambda i: (0, i)), whole, whole],
        out_specs=[out, out],
        out_shape=[shape, shape],
        scratch_shapes=[pltpu.VMEM((NBLK, tile), BF16)],
        compiler_params=params(),
        cost_estimate=cost(4 * rows * NBLK * PAIRS, 4 * rows * (NBLK + PAIRS)),
        name="arrange_cache",
    )(table_row, k_flat, v_flat)


def project_kernel(pieces, first, last, idx_ref, *refs):
    refs = list(refs)
    groups = []
    for count in pieces:
        groups.append(refs[:count])
        refs = refs[count:]
    rstd_ref, gain_ref, qa_ref, qb_ref, ka_ref, kb_ref, va_ref, vb_ref = refs[:8]
    refs = refs[8:]
    if not first:
        before = refs.pop(0)
    if last:
        qbias_ref, kbias_ref, vbias_ref, cos_ref, sin_ref = refs[:5]
        refs = refs[5:]
        q_out, k_out, v_out, dq_out, dkv_out, total = refs
    else:
        (total,) = refs
    step = pl.program_id(0)
    parity = idx_ref[len(pieces)]

    @pl.when(step == 0)
    def _():
        if first:
            total[...] = jnp.zeros_like(total)
        else:
            total[...] = before[...]

    for at, group in enumerate(groups):

        @pl.when(step == at)
        def _():
            parts = [ref[...].astype(F32) for ref in group]
            raw = parts[0] if len(parts) == 1 else jnp.concatenate(parts, axis=0)
            normed = (raw * rstd_ref[...] * gain_ref[...]).astype(BF16)
            half = QCOLS // 2
            total[:, :half] += jnp.dot(normed, qa_ref[...], preferred_element_type=F32)
            total[:, half:QCOLS] += jnp.dot(normed, qb_ref[...], preferred_element_type=F32)
            for own, other, start in ((ka_ref, kb_ref, QCOLS), (va_ref, vb_ref, QCOLS + HEAD_DIM)):
                a, b = own[...], other[...]
                weight = jnp.concatenate(
                    [jnp.where(parity == 0, a, b), jnp.where(parity == 0, b, a)], axis=0
                )
                total[:, start : start + HEAD_DIM] += lax.dot_general(
                    normed, weight, NT, preferred_element_type=F32
                )

    if last:

        @pl.when(step == len(pieces) - 1)
        def _():
            cosine, sine = cos_ref[...], sin_ref[...]

            def turn(rows):
                return rows * cosine + pltpu.roll(rows, HEAD_DIM // 2, 1) * sine

            half = GROUP // 2
            for head in range(GROUP):
                here = (head % half) * HEAD_DIM
                own = total[:, here : here + HEAD_DIM]
                other = total[:, QCOLS // 2 + here : QCOLS // 2 + here + HEAD_DIM]
                mine = 0 if head < half else 1
                cols = slice(head * HEAD_DIM, (head + 1) * HEAD_DIM)
                rows = jnp.where(parity == mine, own, other) + qbias_ref[:, cols]
                rows = turn(rows).astype(BF16)
                q_out[:, cols] = rows[:PROMPT_ROWS]
                dq_out[:, cols] = rows[PROMPT_ROWS:].astype(F32)
            keys = turn(total[:, QCOLS : QCOLS + HEAD_DIM] + kbias_ref[...]).astype(BF16)
            values = (total[:, QCOLS + HEAD_DIM :] + vbias_ref[...]).astype(BF16)
            k_out[...] = keys[:PROMPT_ROWS]
            v_out[...] = values[:PROMPT_ROWS]
            dkv_out[:, :HEAD_DIM] = keys[PROMPT_ROWS:].astype(F32)
            dkv_out[:, HEAD_DIM:] = values[PROMPT_ROWS:].astype(F32)


def project(chunks, places, parity, rstd, gain, weights, before=None, ending=None):
    first, last = before is None, ending is not None
    pieces = tuple(len(c) for c in chunks)
    flat = [p for c in chunks for p in c]
    count = len(chunks)
    whole = lambda a: pl.BlockSpec(a.shape, lambda i, s: (0,) * a.ndim)
    qa, qb, ka, kb, va, vb = weights
    wide = pl.BlockSpec((CHUNK, QCOLS // 2), lambda i, s: (s[i], 0))
    thin = pl.BlockSpec((HEAD_DIM // 2, CHUNK), lambda i, s: (0, s[i]))
    operands = flat + [rstd, gain, qa, qb, ka, kb, va, vb]
    specs = [whole(p) for p in flat] + [
        whole(rstd),
        pl.BlockSpec((1, CHUNK), lambda i, s: (0, s[i])),
        wide,
        wide,
        thin,
        thin,
        thin,
        thin,
    ]
    if not first:
        operands.append(before)
        specs.append(whole(before))
    scratch = []
    total = jax.ShapeDtypeStruct((ROWS, COLS), F32)
    if last:
        operands += list(ending)
        specs += [whole(a) for a in ending]
        outs = [
            jax.ShapeDtypeStruct((PROMPT_ROWS, QCOLS), BF16),
            jax.ShapeDtypeStruct((PROMPT_ROWS, HEAD_DIM), BF16),
            jax.ShapeDtypeStruct((PROMPT_ROWS, HEAD_DIM), BF16),
            jax.ShapeDtypeStruct((DECODE_ROWS, QCOLS), F32),
            jax.ShapeDtypeStruct((DECODE_ROWS, 2 * HEAD_DIM), F32),
        ]
        scratch = [pltpu.VMEM((ROWS, COLS), F32)]
    else:
        outs = [total]
    scalars = jnp.stack(list(places) + [parity]).astype(jnp.int32)
    got = pl.pallas_call(
        functools.partial(project_kernel, pieces, first, last),
        grid_spec=pltpu.PrefetchScalarGridSpec(
            num_scalar_prefetch=1,
            grid=(count,),
            in_specs=specs,
            out_specs=[pl.BlockSpec(o.shape, lambda i, s: (0, 0)) for o in outs],
            scratch_shapes=scratch,
        ),
        out_shape=outs,
        compiler_params=params(),
        cost_estimate=cost(
            2 * ROWS * COLS * CHUNK * count, count * CHUNK * 2 * (ROWS + COLS) + 8 * ROWS * COLS
        ),
        name="project_rows",
    )(scalars, *operands)
    return got if last else got[0]


def prompt_kernel(q_ref, k_ref, v_ref, out_ref):
    keys, values = k_ref[...], v_ref[...]
    row = lax.broadcasted_iota(jnp.int32, (PROMPT, PROMPT), 0)
    col = lax.broadcasted_iota(jnp.int32, (PROMPT, PROMPT), 1)
    causal = row >= col
    for head in range(GROUP):
        cols = slice(head * HEAD_DIM, (head + 1) * HEAD_DIM)
        scores = lax.dot_general(q_ref[:, cols], keys, NT, preferred_element_type=F32) * SCALE
        scores = jnp.where(causal, scores, MASKED)
        powers = jnp.exp(scores - jnp.max(scores, axis=1, keepdims=True))
        weights = (powers / jnp.sum(powers, axis=1, keepdims=True)).astype(BF16)
        out_ref[:, cols] = jnp.dot(weights, values, preferred_element_type=F32).astype(BF16)


def prompt_attention(q, k, v):
    rows = lambda width: pl.BlockSpec((PROMPT, width), lambda i: (i, 0))
    count = q.shape[0] // PROMPT
    return pl.pallas_call(
        prompt_kernel,
        grid=(count,),
        in_specs=[rows(QCOLS), rows(HEAD_DIM), rows(HEAD_DIM)],
        out_specs=rows(QCOLS),
        out_shape=jax.ShapeDtypeStruct(q.shape, BF16),
        compiler_params=params(),
        cost_estimate=cost(
            count * GROUP * 4 * PROMPT * PROMPT * HEAD_DIM * 4, 4 * q.size, q.shape[0] * PROMPT * GROUP
        ),
        name="prompt_attention",
    )(q, k, v)


def fill_spread(spread):
    row = lax.broadcasted_iota(jnp.int32, spread.shape, 0)
    col = lax.broadcasted_iota(jnp.int32, spread.shape, 1)
    spread[...] = jnp.where(col == (row % HEAD_DIM) * GROUP + row // HEAD_DIM, 1.0, 0.0).astype(BF16)


def decode_kernel(
    par_ref, q_ref, kv_ref, len_ref, ka_ref, kb_ref, va_ref, vb_ref, out_ref, scores, mixed, spread
):
    step = pl.program_id(0)
    parity = par_ref[0]
    lanes = GROUP * MAXB
    rows = GROUP * STEPS * 8

    def natural(own, other):
        return jnp.concatenate(
            [jnp.where(parity == 0, own, other), jnp.where(parity == 0, other, own)], axis=0
        )

    queries = jnp.concatenate(
        [
            q_ref[s, :, m * HEAD_DIM : (m + 1) * HEAD_DIM]
            for m in range(GROUP)
            for s in range(STEPS)
        ],
        axis=0,
    ).astype(BF16)
    row = lax.broadcasted_iota(jnp.int32, (rows, lanes), 0)
    lane = lax.broadcasted_iota(jnp.int32, (rows, lanes), 1)
    limit = jnp.where(row % 8 == lane // MAXB, len_ref[...], 0)
    place = (lax.broadcasted_iota(jnp.int32, (1, lanes), 1) % MAXB) * BLOCK
    top = jnp.full((rows, lanes), MASKED, F32)
    for slot in range(BLOCK):
        keys = natural(ka_ref[slot], kb_ref[slot])
        part = jnp.dot(queries, keys, preferred_element_type=F32) * SCALE
        part = jnp.where(place + slot < limit, part, MASKED)
        scores[slot] = part
        top = jnp.maximum(top, part)
    fresh = jnp.concatenate([kv_ref[s] for s in range(STEPS)], axis=0)
    fresh = jnp.concatenate([fresh, jnp.zeros((128 - 8 * STEPS, 2 * HEAD_DIM), F32)], axis=0).astype(BF16)
    newer = lax.dot_general(queries, fresh[:, :HEAD_DIM], NT, preferred_element_type=F32) * SCALE
    nrow = lax.broadcasted_iota(jnp.int32, (rows, 128), 0)
    nlane = lax.broadcasted_iota(jnp.int32, (rows, 128), 1)
    seen = (nrow % 8 == nlane % 8) & (nlane // 8 <= (nrow // 8) % STEPS)
    newer = jnp.where(seen, newer, MASKED)
    peak = jnp.maximum(
        jnp.max(top, axis=1, keepdims=True), jnp.max(newer, axis=1, keepdims=True)
    )
    newer = jnp.exp(newer - peak)
    weight_sum = jnp.zeros((rows, lanes), F32)
    for slot in range(BLOCK):
        powers = jnp.exp(scores[slot] - peak)
        scores[slot] = powers
        weight_sum = weight_sum + powers
    share = 1.0 / (
        jnp.sum(weight_sum, axis=1, keepdims=True) + jnp.sum(newer, axis=1, keepdims=True)
    )
    result = jnp.dot(
        (newer * share).astype(BF16), fresh[:, HEAD_DIM:], preferred_element_type=F32
    )
    for slot in range(BLOCK):
        values = natural(va_ref[slot], vb_ref[slot])
        result = result + lax.dot_general(
            (scores[slot] * share).astype(BF16), values, NT, preferred_element_type=F32
        )
    for m in range(GROUP):
        for s in range(STEPS):
            at = (m * STEPS + s) * 8
            mixed[s, pl.ds(pl.multiple_of(step * 8, 8), 8), m * HEAD_DIM : (m + 1) * HEAD_DIM] = (
                result[at : at + 8]
            )

    @pl.when(step == pl.num_programs(0) - 1)
    def _():
        fill_spread(spread)
        rounded = mixed[...].reshape(DECODE_ROWS, QCOLS).astype(BF16)
        out_ref[...] = jnp.dot(rounded, spread[...], preferred_element_type=F32).astype(BF16)


def decode_attention(parity, q, kv, lengths, ka, kb, va, vb):
    lanes = GROUP * MAXB
    group = HALF_REQ // 8
    cache = pl.BlockSpec((BLOCK, HEAD_DIM // 2, lanes), lambda i, s: (0, 0, i))
    return pl.pallas_call(
        decode_kernel,
        grid_spec=pltpu.PrefetchScalarGridSpec(
            num_scalar_prefetch=1,
            grid=(group,),
            in_specs=[
                pl.BlockSpec((STEPS, 8, QCOLS), lambda i, s: (0, i, 0)),
                pl.BlockSpec((STEPS, 8, 2 * HEAD_DIM), lambda i, s: (0, i, 0)),
                pl.BlockSpec((1, lanes), lambda i, s: (0, i)),
                cache,
                cache,
                cache,
                cache,
            ],
            out_specs=pl.BlockSpec((DECODE_ROWS, QCOLS), lambda i, s: (0, 0)),
            scratch_shapes=[
                pltpu.VMEM((BLOCK, GROUP * STEPS * 8, lanes), F32),
                pltpu.VMEM((STEPS, HALF_REQ, QCOLS), F32),
                pltpu.VMEM((QCOLS, QCOLS), BF16),
            ],
        ),
        out_shape=jax.ShapeDtypeStruct((DECODE_ROWS, QCOLS), BF16),
        compiler_params=params(),
        cost_estimate=cost(10_000_000_000, 10_000_000, 3_000_000),
        name="decode_attention",
    )(parity, q, kv, lengths, ka, kb, va, vb)


def arrived_kernel(req_ref, q_ref, kv_ref, *refs):
    arrived = refs[:4]
    out_ref, spread = refs[4:]
    fill_spread(spread)
    rows = GROUP * 8
    table = STEPS * REQ_DEV
    row = lax.broadcasted_iota(jnp.int32, (8, table), 0)
    col = lax.broadcasted_iota(jnp.int32, (8, table), 1)
    nrow = lax.broadcasted_iota(jnp.int32, (rows, 128), 0)
    nlane = lax.broadcasted_iota(jnp.int32, (rows, 128), 1)
    seen = (nlane < STEPS) & (nlane <= nrow % 8)
    all_q = q_ref[...].astype(BF16)
    all_kv = kv_ref[...].astype(BF16)
    for at in range(4):
        request = req_ref[at]
        pick = jnp.where((col == row * REQ_DEV + request) & (row < STEPS), 1.0, 0.0).astype(BF16)
        own = jnp.dot(pick, all_q, preferred_element_type=F32)
        queries = jnp.concatenate(
            [own[:, m * HEAD_DIM : (m + 1) * HEAD_DIM] for m in range(GROUP)], axis=0
        ).astype(BF16)
        fresh = jnp.dot(pick, all_kv, preferred_element_type=F32)
        fresh = jnp.concatenate([fresh, jnp.zeros((120, 2 * HEAD_DIM), F32)], axis=0).astype(BF16)
        keys, values = arrived[at][:, :HEAD_DIM], arrived[at][:, HEAD_DIM:]
        scores = lax.dot_general(queries, keys, NT, preferred_element_type=F32) * SCALE
        newer = lax.dot_general(queries, fresh[:, :HEAD_DIM], NT, preferred_element_type=F32) * SCALE
        newer = jnp.where(seen, newer, MASKED)
        peak = jnp.maximum(
            jnp.max(scores, axis=1, keepdims=True), jnp.max(newer, axis=1, keepdims=True)
        )
        scores = jnp.exp(scores - peak)
        newer = jnp.exp(newer - peak)
        share = 1.0 / (
            jnp.sum(scores, axis=1, keepdims=True) + jnp.sum(newer, axis=1, keepdims=True)
        )
        result = jnp.dot((scores * share).astype(BF16), values, preferred_element_type=F32)
        result = result + jnp.dot(
            (newer * share).astype(BF16), fresh[:, HEAD_DIM:], preferred_element_type=F32
        )
        wide = jnp.concatenate([result[m * 8 : (m + 1) * 8] for m in range(GROUP)], axis=1)
        out_ref[at * 8 : (at + 1) * 8] = jnp.dot(
            wide.astype(BF16), spread[...], preferred_element_type=F32
        )


def arrived_attention(requests, q, kv, arrived):
    whole = lambda a: pl.BlockSpec(a.shape, lambda i, s: (0, 0))
    return pl.pallas_call(
        arrived_kernel,
        grid_spec=pltpu.PrefetchScalarGridSpec(
            num_scalar_prefetch=1,
            grid=(1,),
            in_specs=[whole(q), whole(kv)] + [whole(a) for a in arrived],
            out_specs=pl.BlockSpec((32, QCOLS), lambda i, s: (0, 0)),
            scratch_shapes=[pltpu.VMEM((QCOLS, QCOLS), BF16)],
        ),
        out_shape=jax.ShapeDtypeStruct((32, QCOLS), F32),
        compiler_params=params(),
        cost_estimate=cost(500_000_000, 2_000_000, 100_000),
        name="arrived_attention",
    )(requests, q, kv, *arrived)


def body(
    prompt_tokens,
    norm_gain,
    q_weight,
    k_weight,
    v_weight,
    q_bias,
    k_bias,
    v_bias,
    decode_tokens,
    k_cache,
    v_cache,
    block_table,
    context_len,
    prompt_dest,
):
    tp_rank = lax.axis_index("tp")
    dp_rank = lax.axis_index("dp")
    grp_rank = lax.axis_index("grp")
    parity = tp_rank % 2
    chip = tp_rank // 2
    y_at, x_at = chip // 2, chip % 2
    lengths = context_len[0]

    def half_rows(which):
        prompts = lax.dynamic_slice_in_dim(prompt_tokens[0], which * PROMPT_ROWS, PROMPT_ROWS, 0)
        steps = lax.dynamic_slice_in_dim(decode_tokens[0], which * HALF_REQ, HALF_REQ, 1)
        return jnp.concatenate([prompts, steps.reshape(DECODE_ROWS, -1)], axis=0)

    def joined(own, other, axis):
        return jnp.where(
            parity == 0,
            jnp.concatenate([own, other], axis=axis),
            jnp.concatenate([other, own], axis=axis),
        )

    mine = half_rows(parity)
    partner = send(half_rows(1 - parity), CORE)
    held = joined(mine, partner, 1)

    k_turned, v_turned = k_weight.T, v_weight.T
    held_b, q_w, k_turned, v_turned = lax.optimization_barrier((held, q_weight, k_turned, v_turned))
    weights = (
        q_w,
        send(q_w, CORE),
        k_turned,
        send(k_turned, CORE),
        v_turned,
        send(v_turned, CORE),
    )
    held = held_b

    side = send(held, XSWAP)
    up = send(held, YUP)
    down = send(held, YDOWN)

    wide = held.astype(F32)
    squares = jnp.sum(wide * wide, axis=1)
    for pairs in (XSWAP, YUP, YFAR):
        if pairs is YUP:
            pairs = [(i, i ^ 4) for i in range(16)]
        squares = squares + send(squares, pairs)
    rstd = lax.rsqrt(squares * (1.0 / FEATURES) + NORM_EPSILON)[:, None]
    gain = norm_gain[None, :]

    cut = 336
    mid = 304
    inner = 176
    far_a = send(up[:mid], YUP)
    far_b = send(down[mid:], YDOWN)
    side_up_a = send(side[:cut], YUP)
    side_down_a = send(side[:cut], YDOWN)
    side_up_b = send(up[cut:], XSWAP)
    side_down_b = send(down[cut:], XSWAP)
    side_far_a = send(side_up_a[:inner], YUP)
    side_far_b = send(side_down_a[inner:], YDOWN)
    side_far_c = send(far_b[cut - mid :], XSWAP)

    table = block_table[0]
    turned = lambda cache: jnp.transpose(cache[0], (1, 2, 0)).reshape(BLOCK * HEAD_DIM // 2, NBLK)
    k_flat, v_flat = turned(k_cache), turned(v_cache)

    def table_row(which):
        return lax.dynamic_slice_in_dim(table, which * HALF_REQ, HALF_REQ, 0).reshape(1, PAIRS)

    k_theirs, v_theirs = arrange(table_row(1 - parity), k_flat, v_flat)
    k_other, v_other = send(k_theirs, CORE), send(v_theirs, CORE)
    k_own, v_own = arrange(table_row(parity), k_flat, v_flat)
    cache_shape = (BLOCK, HEAD_DIM // 2, PAIRS)

    own_len = lax.dynamic_slice_in_dim(lengths, parity * HALF_REQ, HALF_REQ, 0)
    positions = jnp.concatenate(
        [
            jnp.arange(PROMPT_ROWS, dtype=jnp.int32) % PROMPT,
            (own_len[None, :] + jnp.arange(STEPS, dtype=jnp.int32)[:, None]).reshape(-1),
        ]
    )
    exponent = jnp.arange(HEAD_DIM // 2, dtype=F32) * (2.0 / HEAD_DIM)
    frequency = jnp.power(F32(ROPE_BASE), -exponent)
    angle = positions.astype(F32)[:, None] * frequency
    cosine, sine = jnp.cos(angle), jnp.sin(angle)
    cosine = jnp.concatenate([cosine, cosine], axis=1)
    sine = jnp.concatenate([-sine, sine], axis=1)

    place = lambda dy, dx: ((y_at + dy) % 4) * 2 + (x_at + dx) % 2
    total = project(
        [(held,), (side,), (up,), (down,)],
        [place(0, 0), place(0, 1), place(3, 0), place(1, 0)],
        parity,
        rstd,
        gain,
        weights,
    )
    total = project(
        [(far_a, far_b), (side_up_a, side_up_b), (side_down_a, side_down_b)],
        [place(2, 0), place(3, 1), place(1, 1)],
        parity,
        rstd,
        gain,
        weights,
        before=total,
    )
    pool_cols = lambda bias, width: lax.dynamic_slice_in_dim(bias, chip * width, width, 0)[None, :]
    q, k, v, dq, dkv = project(
        [(side_far_a, side_far_b, side_far_c)],
        [place(2, 1)],
        parity,
        rstd,
        gain,
        weights,
        before=total,
        ending=(
            pool_cols(q_bias, QCOLS),
            pool_cols(k_bias, HEAD_DIM),
            pool_cols(v_bias, HEAD_DIM),
            cosine,
            sine,
        ),
    )

    kv_own = jnp.concatenate([k, v], axis=1)
    kv_all = joined(kv_own, send(kv_own, CORE), 0).reshape(4, PROMPT, 2 * HEAD_DIM)
    destination = prompt_dest[0]
    replica = jnp.arange(4, dtype=jnp.int32)
    order = jnp.sum(
        jnp.where((destination // REQ_DEV)[None, :] == replica[:, None], replica[None, :], 0), axis=1
    )
    arrived = []
    for shift in range(4):
        target = (dp_rank + shift) % 4
        block = lax.dynamic_index_in_dim(kv_all, order[target], 0, keepdims=False)
        pairs = [(g * 4 + a, (1 - g) * 4 + (a + shift) % 4) for g in range(2) for a in range(4)]
        arrived.append(lax.ppermute(block, ("grp", "dp"), pairs))
    every = lax.all_gather(prompt_dest[0], ("grp", "dp"), axis=0).reshape(2, 4, 4)
    theirs = lax.dynamic_index_in_dim(every, 1 - grp_rank, 0, keepdims=False)
    requests = []
    for shift in range(4):
        source = lax.dynamic_index_in_dim(theirs, (dp_rank - shift) % 4, 0, keepdims=False)
        requests.append(jnp.sum(jnp.where(source // REQ_DEV == dp_rank, source % REQ_DEV, 0)))
    requests = jnp.stack(requests).astype(jnp.int32)

    prefill = prompt_attention(q, k, v)

    def own_cols(rows, which):
        return lax.dynamic_slice_in_dim(rows, which * (QCOLS // 2), QCOLS // 2, 1)

    prefill_out = joined(
        own_cols(prefill, parity), send(own_cols(prefill, 1 - parity), CORE), 0
    )[None]

    dq3 = dq.reshape(STEPS, HALF_REQ, QCOLS)
    dkv3 = dkv.reshape(STEPS, HALF_REQ, 2 * HEAD_DIM)
    decode = decode_attention(
        parity[None].astype(jnp.int32),
        dq3,
        dkv3,
        jnp.repeat(own_len, MAXB)[None, :],
        k_own.reshape(cache_shape),
        k_other.reshape(cache_shape),
        v_own.reshape(cache_shape),
        v_other.reshape(cache_shape),
    ).reshape(STEPS, HALF_REQ, QCOLS)
    decode_own = lax.dynamic_slice_in_dim(decode, parity * (QCOLS // 2), QCOLS // 2, 2)
    decode_sent = lax.dynamic_slice_in_dim(decode, (1 - parity) * (QCOLS // 2), QCOLS // 2, 2)
    decode_out = joined(decode_own, send(decode_sent, CORE), 1)

    all_q = joined(dq3, send(dq3, CORE), 1).reshape(STEPS * REQ_DEV, QCOLS)
    all_kv = joined(dkv3, send(dkv3, CORE), 1).reshape(STEPS * REQ_DEV, 2 * HEAD_DIM)
    fixed = arrived_attention(requests, all_q, all_kv, arrived)
    fixed = own_cols(fixed, parity).astype(BF16).reshape(4, 8, QCOLS // 2)[:, :STEPS]
    request_id = jnp.arange(REQ_DEV, dtype=jnp.int32)[None, :, None]
    for at in range(4):
        decode_out = jnp.where(request_id == requests[at], fixed[at][:, None, :], decode_out)
    return (prefill_out, decode_out[None])


def solution(mesh):
    placed = (
        P("grp", "dp", "tp"),
        P(),
        P(None, "tp"),
        P(None, "tp"),
        P(None, "tp"),
        P(),
        P(),
        P(),
        P("grp", None, "dp", "tp"),
        P("grp", "dp", None, "tp"),
        P("grp", "dp", None, "tp"),
        P("grp", "dp", None),
        P("grp", "dp"),
        P("grp", "dp"),
    )
    return jax.shard_map(
        body,
        mesh=mesh,
        in_specs=placed,
        out_specs=(P("grp", "dp", "tp"), P("grp", None, "dp", "tp")),
        check_vma=False,
    )
```

```python
import functools
import math

import jax
import jax.numpy as jnp
from jax import lax
from jax.experimental import pallas as pl
from jax.experimental.pallas import tpu as pltpu
from jax.sharding import PartitionSpec as P

HEAD_DIM = 128
GROUP = 8
BLOCK = 16
MAXB = 32
PROMPT = 256
REQ_DEV = 64
STEPS = 3
ROPE_BASE = 1000000.0
NORM_EPSILON = 1e-06
MASKED = -1e30
SCALE = 1.0 / math.sqrt(HEAD_DIM)
FEATURES = 8192
CHUNK = 1024
PROMPT_ROWS = 512
DECODE_ROWS = 96
ROWS = PROMPT_ROWS + DECODE_ROWS
QCOLS = GROUP * HEAD_DIM
COLS = QCOLS + 2 * HEAD_DIM
HALF_REQ = REQ_DEV // 2
NBLK = 2048
PAIRS = HALF_REQ * MAXB
VMEM = 56 * 1024 * 1024
CUT = 336
MID = 304
INNER = 176

CORE = [(i, i ^ 1) for i in range(16)]
XSWAP = [(i, i ^ 2) for i in range(16)]
YFAR = [(i, i ^ 8) for i in range(16)]
YUP = [(i, (i + 4) % 16) for i in range(16)]
YDOWN = [(i, (i + 12) % 16) for i in range(16)]

NT = (((1,), (1,)), ((), ()))
F32 = jnp.float32
BF16 = jnp.bfloat16


def send(array, pairs):
    return lax.ppermute(array, "tp", pairs)


def cost(flops, nbytes, trans=0):
    return pl.CostEstimate(flops=flops // 64, bytes_accessed=nbytes // 64, transcendentals=trans // 64)


def params(**more):
    return pltpu.CompilerParams(vmem_limit_bytes=VMEM, **more)


def arrange_kernel(table_ref, k_ref, v_ref, out_ref, pick):
    tile = table_ref.shape[1]
    half = k_ref.shape[0]
    block = lax.broadcasted_iota(jnp.int32, (NBLK, tile), 0)
    pick[...] = jnp.where(block == table_ref[...], 1.0, 0.0).astype(BF16)
    out_ref[:half] = jnp.dot(k_ref[...], pick[...], preferred_element_type=F32).astype(BF16)
    out_ref[half:] = jnp.dot(v_ref[...], pick[...], preferred_element_type=F32).astype(BF16)


def arrange(table_row, k_flat, v_flat):
    rows = k_flat.shape[0]
    tile = 256
    whole = pl.BlockSpec((rows, NBLK), lambda i: (0, 0))
    return pl.pallas_call(
        arrange_kernel,
        grid=(PAIRS // tile,),
        in_specs=[pl.BlockSpec((1, tile), lambda i: (0, i)), whole, whole],
        out_specs=pl.BlockSpec((2 * rows, tile), lambda i: (0, i)),
        out_shape=jax.ShapeDtypeStruct((2 * rows, PAIRS), BF16),
        scratch_shapes=[pltpu.VMEM((NBLK, tile), BF16)],
        compiler_params=params(),
        cost_estimate=cost(4 * rows * NBLK * PAIRS, 4 * rows * (NBLK + PAIRS)),
        name="arrange_cache",
    )(table_row, k_flat, v_flat)


def pack_kernel(plan, count, *refs):
    sources, outs = refs[:count], refs[count:]
    for out, parts in zip(outs, plan):
        at = 0
        for source, start, stop in parts:
            out[at : at + stop - start] = sources[source][start:stop]
            at += stop - start


def pack(sources, plan):
    sizes = [sum(stop - start for _, start, stop in parts) for parts in plan]
    shapes = [jax.ShapeDtypeStruct((size, CHUNK), BF16) for size in sizes]
    whole = lambda a: pl.BlockSpec(a.shape, lambda: (0, 0))
    return pl.pallas_call(
        functools.partial(pack_kernel, plan, len(sources)),
        in_specs=[whole(a) for a in sources],
        out_specs=[whole(a) for a in shapes],
        out_shape=shapes,
        compiler_params=params(),
        cost_estimate=cost(0, 4 * CHUNK * sum(sizes)),
        name="pack_rows",
    )(*sources)


def handover_kernel(scalar_ref, own_ref, other_ref, *outs):
    parity, rank = scalar_ref[4], scalar_ref[5]
    for shift in range(4):
        target = (rank + shift) % 4
        at = jnp.int32(0)
        request = jnp.int32(0)
        for prompt in range(4):
            chosen = scalar_ref[prompt] // REQ_DEV == target
            at = jnp.where(chosen, prompt, at)
            request = jnp.where(chosen, scalar_ref[prompt] % REQ_DEV, request)
        rows = pl.ds(pl.multiple_of((at % 2) * PROMPT, PROMPT), PROMPT)
        outs[shift][:PROMPT] = jnp.where(at // 2 == parity, own_ref[rows, :], other_ref[rows, :])
        outs[shift][PROMPT:] = jnp.full((16, 2 * HEAD_DIM), request.astype(F32), F32).astype(BF16)


def handover(scalars, own, other):
    whole = pl.BlockSpec(own.shape, lambda i, s: (0, 0))
    shape = jax.ShapeDtypeStruct((PROMPT + 16, 2 * HEAD_DIM), BF16)
    return pl.pallas_call(
        handover_kernel,
        grid_spec=pltpu.PrefetchScalarGridSpec(
            num_scalar_prefetch=1,
            grid=(1,),
            in_specs=[whole, whole],
            out_specs=[pl.BlockSpec(shape.shape, lambda i, s: (0, 0))] * 4,
        ),
        out_shape=[shape] * 4,
        compiler_params=params(),
        cost_estimate=cost(0, 2_000_000),
        name="sort_prompts",
    )(scalars, own, other)


def project_kernel(chunks, count, first, last, idx_ref, *refs):
    refs = list(refs)
    arrays, refs = refs[:count], refs[count:]
    rstd_ref, gain_ref, qa_ref, qb_ref, kva_ref, kvb_ref = refs[:6]
    refs = refs[6:]
    if not first:
        before = refs.pop(0)
    if last:
        qbias_ref, kbias_ref, vbias_ref, cos_ref, sin_ref = refs[:5]
        refs = refs[5:]
        q_out, kv_out, steps_out, total = refs
    else:
        (total,) = refs
    step = pl.program_id(0)
    parity = idx_ref[len(chunks)]
    half = QCOLS // 2
    half_dim = HEAD_DIM // 2

    @pl.when(step == 0)
    def _():
        if first:
            total[...] = jnp.zeros_like(total)
        else:
            total[...] = before[...]

    for at, parts in enumerate(chunks):

        @pl.when(step == at)
        def _():
            rows = [arrays[source][start:stop].astype(F32) for source, start, stop in parts]
            raw = rows[0] if len(rows) == 1 else jnp.concatenate(rows, axis=0)
            normed = (raw * rstd_ref[...] * gain_ref[...]).astype(BF16)
            total[:, :half] += jnp.dot(normed, qa_ref[...], preferred_element_type=F32)
            total[:, half:QCOLS] += jnp.dot(normed, qb_ref[...], preferred_element_type=F32)
            own, other = kva_ref[...], kvb_ref[...]
            low = jnp.where(parity == 0, own, other)
            high = jnp.where(parity == 0, other, own)
            weight = jnp.concatenate(
                [low[:half_dim], high[:half_dim], low[half_dim:], high[half_dim:]], axis=0
            )
            total[:, QCOLS:] += lax.dot_general(normed, weight, NT, preferred_element_type=F32)

    if last:

        @pl.when(step == len(chunks) - 1)
        def _():
            cosine, sine = cos_ref[...], sin_ref[...]

            def turn(rows):
                return rows * cosine + pltpu.roll(rows, half_dim, 1) * sine

            for head in range(GROUP):
                here = (head % (GROUP // 2)) * HEAD_DIM
                own = total[:, here : here + HEAD_DIM]
                other = total[:, half + here : half + here + HEAD_DIM]
                mine = 0 if head < GROUP // 2 else 1
                cols = slice(head * HEAD_DIM, (head + 1) * HEAD_DIM)
                rows = jnp.where(parity == mine, own, other) + qbias_ref[:, cols]
                rows = turn(rows).astype(BF16)
                q_out[:, cols] = rows[:PROMPT_ROWS]
                steps_out[:, cols] = rows[PROMPT_ROWS:].astype(F32)
            keys = turn(total[:, QCOLS : QCOLS + HEAD_DIM] + kbias_ref[...]).astype(BF16)
            values = (total[:, QCOLS + HEAD_DIM :] + vbias_ref[...]).astype(BF16)
            kv_out[:, :HEAD_DIM] = keys[:PROMPT_ROWS]
            kv_out[:, HEAD_DIM:] = values[:PROMPT_ROWS]
            steps_out[:, QCOLS : QCOLS + HEAD_DIM] = keys[PROMPT_ROWS:].astype(F32)
            steps_out[:, QCOLS + HEAD_DIM :] = values[PROMPT_ROWS:].astype(F32)


def project(arrays, chunks, places, parity, rstd, gain, weights, before=None, ending=None):
    first, last = before is None, ending is not None
    count = len(chunks)
    whole = lambda a: pl.BlockSpec(a.shape, lambda i, s: (0,) * a.ndim)
    wide = pl.BlockSpec((CHUNK, QCOLS // 2), lambda i, s: (s[i], 0))
    thin = pl.BlockSpec((HEAD_DIM, CHUNK), lambda i, s: (0, s[i]))
    operands = list(arrays) + [rstd, gain, *weights]
    specs = [whole(p) for p in arrays] + [
        whole(rstd),
        pl.BlockSpec((1, CHUNK), lambda i, s: (0, s[i])),
        wide,
        wide,
        thin,
        thin,
    ]
    if not first:
        operands.append(before)
        specs.append(whole(before))
    scratch = []
    total = jax.ShapeDtypeStruct((ROWS, COLS), F32)
    if last:
        operands += list(ending)
        specs += [whole(a) for a in ending]
        outs = [
            jax.ShapeDtypeStruct((PROMPT_ROWS, QCOLS), BF16),
            jax.ShapeDtypeStruct((PROMPT_ROWS, 2 * HEAD_DIM), BF16),
            jax.ShapeDtypeStruct((DECODE_ROWS, COLS), F32),
        ]
        scratch = [pltpu.VMEM((ROWS, COLS), F32)]
    else:
        outs = [total]
    scalars = jnp.stack(list(places) + [parity]).astype(jnp.int32)
    got = pl.pallas_call(
        functools.partial(project_kernel, chunks, len(arrays), first, last),
        grid_spec=pltpu.PrefetchScalarGridSpec(
            num_scalar_prefetch=1,
            grid=(count,),
            in_specs=specs,
            out_specs=[pl.BlockSpec(o.shape, lambda i, s: (0, 0)) for o in outs],
            scratch_shapes=scratch,
        ),
        out_shape=outs,
        compiler_params=params(),
        cost_estimate=cost(
            2 * ROWS * COLS * CHUNK * count, count * CHUNK * 2 * (ROWS + COLS) + 8 * ROWS * COLS
        ),
        name="project_rows",
    )(scalars, *operands)
    return got if last else got[0]


def prompt_kernel(q_ref, kv_ref, out_ref):
    keys, values = kv_ref[:, :HEAD_DIM], kv_ref[:, HEAD_DIM:]
    row = lax.broadcasted_iota(jnp.int32, (PROMPT, PROMPT), 0)
    col = lax.broadcasted_iota(jnp.int32, (PROMPT, PROMPT), 1)
    causal = row >= col
    for head in range(GROUP):
        cols = slice(head * HEAD_DIM, (head + 1) * HEAD_DIM)
        scores = lax.dot_general(q_ref[:, cols], keys, NT, preferred_element_type=F32) * SCALE
        scores = jnp.where(causal, scores, MASKED)
        powers = jnp.exp(scores - jnp.max(scores, axis=1, keepdims=True))
        weights = (powers / jnp.sum(powers, axis=1, keepdims=True)).astype(BF16)
        out_ref[:, cols] = jnp.dot(weights, values, preferred_element_type=F32).astype(BF16)


def prompt_attention(q, kv):
    rows = lambda width: pl.BlockSpec((PROMPT, width), lambda i: (i, 0))
    count = q.shape[0] // PROMPT
    return pl.pallas_call(
        prompt_kernel,
        grid=(count,),
        in_specs=[rows(QCOLS), rows(2 * HEAD_DIM)],
        out_specs=rows(QCOLS),
        out_shape=jax.ShapeDtypeStruct(q.shape, BF16),
        compiler_params=params(),
        cost_estimate=cost(
            count * GROUP * 4 * PROMPT * PROMPT * HEAD_DIM * 4, 4 * q.size, q.shape[0] * PROMPT * GROUP
        ),
        name="prompt_attention",
    )(q, kv)


def fill_spread(spread):
    row = lax.broadcasted_iota(jnp.int32, spread.shape, 0)
    col = lax.broadcasted_iota(jnp.int32, spread.shape, 1)
    spread[...] = jnp.where(col == (row % HEAD_DIM) * GROUP + row // HEAD_DIM, 1.0, 0.0).astype(BF16)


def decode_kernel(
    par_ref, rows_ref, len_ref, own_ref, other_ref, out_ref, scores, mixed, spread
):
    step = pl.program_id(0)
    parity = par_ref[0]
    lanes = GROUP * MAXB
    rows = GROUP * STEPS * 8

    def natural(own, other):
        return jnp.concatenate(
            [jnp.where(parity == 0, own, other), jnp.where(parity == 0, other, own)], axis=0
        )

    queries = jnp.concatenate(
        [
            rows_ref[s, :, m * HEAD_DIM : (m + 1) * HEAD_DIM]
            for m in range(GROUP)
            for s in range(STEPS)
        ],
        axis=0,
    ).astype(BF16)
    row = lax.broadcasted_iota(jnp.int32, (rows, lanes), 0)
    lane = lax.broadcasted_iota(jnp.int32, (rows, lanes), 1)
    limit = jnp.where(row % 8 == lane // MAXB, len_ref[...], 0)
    place = (lax.broadcasted_iota(jnp.int32, (1, lanes), 1) % MAXB) * BLOCK
    top = jnp.full((rows, lanes), MASKED, F32)
    for slot in range(BLOCK):
        keys = natural(own_ref[0, slot], other_ref[0, slot])
        part = jnp.dot(queries, keys, preferred_element_type=F32) * SCALE
        part = jnp.where(place + slot < limit, part, MASKED)
        scores[slot] = part
        top = jnp.maximum(top, part)
    fresh = jnp.concatenate([rows_ref[s, :, QCOLS:] for s in range(STEPS)], axis=0)
    fresh = jnp.concatenate([fresh, jnp.zeros((128 - 8 * STEPS, 2 * HEAD_DIM), F32)], axis=0).astype(BF16)
    newer = lax.dot_general(queries, fresh[:, :HEAD_DIM], NT, preferred_element_type=F32) * SCALE
    nrow = lax.broadcasted_iota(jnp.int32, (rows, 128), 0)
    nlane = lax.broadcasted_iota(jnp.int32, (rows, 128), 1)
    seen = (nrow % 8 == nlane % 8) & (nlane // 8 <= (nrow // 8) % STEPS)
    newer = jnp.where(seen, newer, MASKED)
    peak = jnp.maximum(
        jnp.max(top, axis=1, keepdims=True), jnp.max(newer, axis=1, keepdims=True)
    )
    newer = jnp.exp(newer - peak)
    weight_sum = jnp.zeros((rows, lanes), F32)
    for slot in range(BLOCK):
        powers = jnp.exp(scores[slot] - peak)
        scores[slot] = powers
        weight_sum = weight_sum + powers
    share = 1.0 / (
        jnp.sum(weight_sum, axis=1, keepdims=True) + jnp.sum(newer, axis=1, keepdims=True)
    )
    result = jnp.dot(
        (newer * share).astype(BF16), fresh[:, HEAD_DIM:], preferred_element_type=F32
    )
    for slot in range(BLOCK):
        values = natural(own_ref[1, slot], other_ref[1, slot])
        result = result + lax.dot_general(
            (scores[slot] * share).astype(BF16), values, NT, preferred_element_type=F32
        )
    for m in range(GROUP):
        for s in range(STEPS):
            at = (m * STEPS + s) * 8
            mixed[s, pl.ds(pl.multiple_of(step * 8, 8), 8), m * HEAD_DIM : (m + 1) * HEAD_DIM] = (
                result[at : at + 8]
            )

    @pl.when(step == pl.num_programs(0) - 1)
    def _():
        fill_spread(spread)
        rounded = mixed[...].reshape(DECODE_ROWS, QCOLS).astype(BF16)
        out_ref[...] = jnp.dot(rounded, spread[...], preferred_element_type=F32).astype(BF16)


def decode_attention(parity, rows, lengths, own, other):
    lanes = GROUP * MAXB
    group = HALF_REQ // 8
    cache = pl.BlockSpec((2, BLOCK, HEAD_DIM // 2, lanes), lambda i, s: (0, 0, 0, i))
    return pl.pallas_call(
        decode_kernel,
        grid_spec=pltpu.PrefetchScalarGridSpec(
            num_scalar_prefetch=1,
            grid=(group,),
            in_specs=[
                pl.BlockSpec((STEPS, 8, COLS), lambda i, s: (0, i, 0)),
                pl.BlockSpec((1, lanes), lambda i, s: (0, i)),
                cache,
                cache,
            ],
            out_specs=pl.BlockSpec((DECODE_ROWS, QCOLS), lambda i, s: (0, 0)),
            scratch_shapes=[
                pltpu.VMEM((BLOCK, GROUP * STEPS * 8, lanes), F32),
                pltpu.VMEM((STEPS, HALF_REQ, QCOLS), F32),
                pltpu.VMEM((QCOLS, QCOLS), BF16),
            ],
        ),
        out_shape=jax.ShapeDtypeStruct((DECODE_ROWS, QCOLS), BF16),
        compiler_params=params(),
        cost_estimate=cost(10_000_000_000, 10_000_000, 3_000_000),
        name="decode_attention",
    )(parity, rows, lengths, own, other)


def arrived_kernel(par_ref, base_ref, rows_ref, *refs):
    arrived = refs[:4]
    out_ref, spread = refs[4:]
    own_cols = QCOLS // 2
    dim = lax.broadcasted_iota(jnp.int32, spread.shape, 0)
    out_col = lax.broadcasted_iota(jnp.int32, spread.shape, 1) + par_ref[0] * own_cols
    spread[...] = jnp.where(
        out_col == (dim % HEAD_DIM) * GROUP + dim // HEAD_DIM, 1.0, 0.0
    ).astype(BF16)
    rows = GROUP * 8
    table = STEPS * REQ_DEV
    row = lax.broadcasted_iota(jnp.int32, (8, table), 0)
    col = lax.broadcasted_iota(jnp.int32, (8, table), 1)
    turned_row = lax.broadcasted_iota(jnp.int32, (table, 8), 1)
    turned_col = lax.broadcasted_iota(jnp.int32, (table, 8), 0)
    nrow = lax.broadcasted_iota(jnp.int32, (rows, 128), 0)
    nlane = lax.broadcasted_iota(jnp.int32, (rows, 128), 1)
    seen = (nlane < STEPS) & (nlane <= nrow % 8)
    all_rows = rows_ref[...].astype(BF16)
    merged = base_ref[...].astype(F32)
    for at in range(4):
        request = arrived[at][PROMPT : PROMPT + 16, :128].astype(jnp.int32)[:1, :1]
        pick = jnp.where((col == row * REQ_DEV + request) & (row < STEPS), 1.0, 0.0).astype(BF16)
        own = jnp.dot(pick, all_rows, preferred_element_type=F32)
        queries = jnp.concatenate(
            [own[:, m * HEAD_DIM : (m + 1) * HEAD_DIM] for m in range(GROUP)], axis=0
        ).astype(BF16)
        fresh = jnp.concatenate([own[:, QCOLS:], jnp.zeros((120, 2 * HEAD_DIM), F32)], axis=0).astype(BF16)
        keys, values = arrived[at][:PROMPT, :HEAD_DIM], arrived[at][:PROMPT, HEAD_DIM:]
        scores = lax.dot_general(queries, keys, NT, preferred_element_type=F32) * SCALE
        newer = lax.dot_general(queries, fresh[:, :HEAD_DIM], NT, preferred_element_type=F32) * SCALE
        newer = jnp.where(seen, newer, MASKED)
        peak = jnp.maximum(
            jnp.max(scores, axis=1, keepdims=True), jnp.max(newer, axis=1, keepdims=True)
        )
        scores = jnp.exp(scores - peak)
        newer = jnp.exp(newer - peak)
        share = 1.0 / (
            jnp.sum(scores, axis=1, keepdims=True) + jnp.sum(newer, axis=1, keepdims=True)
        )
        result = jnp.dot((scores * share).astype(BF16), values, preferred_element_type=F32)
        result = result + jnp.dot(
            (newer * share).astype(BF16), fresh[:, HEAD_DIM:], preferred_element_type=F32
        )
        wide = jnp.concatenate([result[m * 8 : (m + 1) * 8] for m in range(GROUP)], axis=1)
        fixed = jnp.dot(wide.astype(BF16), spread[...], preferred_element_type=F32).astype(BF16)
        back = jnp.where((turned_col == turned_row * REQ_DEV + request) & (turned_row < STEPS), 1.0, 0.0)
        placed = jnp.dot(back.astype(BF16), fixed, preferred_element_type=F32)
        here = lax.broadcasted_iota(jnp.int32, (table, own_cols), 0) % REQ_DEV == request
        merged = jnp.where(here, placed, merged)
    out_ref[...] = merged.astype(BF16)


def arrived_attention(parity, base, rows, arrived):
    whole = lambda a: pl.BlockSpec(a.shape, lambda i, s: (0, 0))
    return pl.pallas_call(
        arrived_kernel,
        grid_spec=pltpu.PrefetchScalarGridSpec(
            num_scalar_prefetch=1,
            grid=(1,),
            in_specs=[whole(base), whole(rows)] + [whole(a) for a in arrived],
            out_specs=whole(base),
            scratch_shapes=[pltpu.VMEM((QCOLS, QCOLS // 2), BF16)],
        ),
        out_shape=jax.ShapeDtypeStruct(base.shape, BF16),
        compiler_params=params(),
        cost_estimate=cost(500_000_000, 2_000_000, 100_000),
        name="arrived_attention",
    )(parity, base, rows, *arrived)


def body(
    prompt_tokens,
    norm_gain,
    q_weight,
    k_weight,
    v_weight,
    q_bias,
    k_bias,
    v_bias,
    decode_tokens,
    k_cache,
    v_cache,
    block_table,
    context_len,
    prompt_dest,
):
    tp_rank = lax.axis_index("tp")
    dp_rank = lax.axis_index("dp")
    parity = tp_rank % 2
    chip = tp_rank // 2
    y_at, x_at = chip // 2, chip % 2
    lengths = context_len[0]

    def half_rows(which):
        prompts = lax.dynamic_slice_in_dim(prompt_tokens[0], which * PROMPT_ROWS, PROMPT_ROWS, 0)
        steps = lax.dynamic_slice_in_dim(decode_tokens[0], which * HALF_REQ, HALF_REQ, 1)
        return jnp.concatenate([prompts, steps.reshape(DECODE_ROWS, -1)], axis=0)

    def joined(own, other, axis):
        return jnp.where(
            parity == 0,
            jnp.concatenate([own, other], axis=axis),
            jnp.concatenate([other, own], axis=axis),
        )

    partner = send(half_rows(1 - parity), CORE)
    held = joined(half_rows(parity), partner, 1)
    kv_weight = jnp.concatenate([k_weight.T, v_weight.T], axis=0)

    held, q_w, kv_w = lax.optimization_barrier((held, q_weight, kv_weight))
    side, up, down = send(held, XSWAP), send(held, YUP), send(held, YDOWN)
    weights = (q_w, send(q_w, CORE), kv_w, send(kv_w, CORE))
    gain = norm_gain[None, :]

    table = block_table[0]
    turned = lambda cache: jnp.transpose(cache[0], (1, 2, 0)).reshape(BLOCK * HEAD_DIM // 2, NBLK)
    k_flat, v_flat = turned(k_cache), turned(v_cache)

    def table_row(which):
        return lax.dynamic_slice_in_dim(table, which * HALF_REQ, HALF_REQ, 0).reshape(1, PAIRS)

    row_theirs, row_own = table_row(1 - parity), table_row(parity)
    row_theirs, held = lax.optimization_barrier((row_theirs, held))
    cache_theirs = arrange(row_theirs, k_flat, v_flat)

    side, up, down, held, cache_theirs, row_own = lax.optimization_barrier(
        (side, up, down, held, cache_theirs, row_own)
    )

    def squares(left, right):
        left, right = left.astype(F32), right.astype(F32)
        return jnp.sum(left * left + right * right, axis=1)

    along, around = squares(held, side), squares(up, down)
    rise, fall, cross = pack(
        (side, up, down),
        (
            ((1, 0, MID), (0, 0, CUT)),
            ((2, MID, ROWS), (0, 0, CUT)),
            ((1, CUT, ROWS), (2, CUT, ROWS)),
        ),
    )
    far_along, far_around = send(along, YFAR), send(around, XSWAP)
    rise_b, fall_b, cross_b, side, row_own = lax.optimization_barrier((rise, fall, cross, side, row_own))
    rise, fall, cross = send(rise_b, YUP), send(fall_b, YDOWN), send(cross_b, XSWAP)
    mean = (along + around + far_along + far_around) * (1.0 / FEATURES)
    rstd = lax.rsqrt(mean + NORM_EPSILON)[:, None]
    cache_other = send(cache_theirs, CORE)
    cache_own = arrange(row_own, k_flat, v_flat)
    place = lambda dy, dx: ((y_at + dy) % 4) * 2 + (x_at + dx) % 2
    total = project(
        (held, side, up, down),
        tuple(((source, 0, ROWS),) for source in range(4)),
        [place(0, 0), place(0, 1), place(3, 0), place(1, 0)],
        parity,
        rstd,
        gain,
        weights,
    )

    rise, fall, cross, total, cache_own = lax.optimization_barrier((rise, fall, cross, total, cache_own))
    low = ROWS - MID
    rise_far, fall_far, cross_far = pack(
        (rise, fall),
        (
            ((0, MID, MID + INNER),),
            ((1, low + INNER, low + CUT),),
            ((1, CUT - MID, low),),
        ),
    )
    rise_far, fall_far, cross_far, rise, fall, cross, total = lax.optimization_barrier(
        (rise_far, fall_far, cross_far, rise, fall, cross, total)
    )
    far = (send(rise_far, YUP), send(fall_far, YDOWN), send(cross_far, XSWAP))
    total = project(
        (rise, fall, cross),
        (
            ((0, 0, MID), (1, 0, low)),
            ((0, MID, MID + CUT), (2, 0, ROWS - CUT)),
            ((1, low, low + CUT), (2, ROWS - CUT, 2 * (ROWS - CUT))),
        ),
        [place(2, 0), place(3, 1), place(1, 1)],
        parity,
        rstd,
        gain,
        weights,
        before=total,
    )

    own_len = lax.dynamic_slice_in_dim(lengths, parity * HALF_REQ, HALF_REQ, 0)
    positions = jnp.concatenate(
        [
            jnp.arange(PROMPT_ROWS, dtype=jnp.int32) % PROMPT,
            (own_len[None, :] + jnp.arange(STEPS, dtype=jnp.int32)[:, None]).reshape(-1),
        ]
    )
    exponent = jnp.arange(HEAD_DIM // 2, dtype=F32) * (2.0 / HEAD_DIM)
    frequency = jnp.power(F32(ROPE_BASE), -exponent)
    angle = positions.astype(F32)[:, None] * frequency
    cosine, sine = jnp.cos(angle), jnp.sin(angle)
    cosine = jnp.concatenate([cosine, cosine], axis=1)
    sine = jnp.concatenate([-sine, sine], axis=1)

    pool_cols = lambda bias, width: lax.dynamic_slice_in_dim(bias, chip * width, width, 0)[None, :]
    q, kv, steps = project(
        far,
        (((0, 0, INNER), (1, 0, CUT - INNER), (2, 0, ROWS - CUT)),),
        [place(2, 1)],
        parity,
        rstd,
        gain,
        weights,
        before=total,
        ending=(
            pool_cols(q_bias, QCOLS),
            pool_cols(k_bias, HEAD_DIM),
            pool_cols(v_bias, HEAD_DIM),
            cosine,
            sine,
        ),
    )

    scalars = jnp.concatenate([prompt_dest[0], parity[None], dp_rank[None]]).astype(jnp.int32)
    blocks = handover(scalars, kv, send(kv, CORE))
    blocks, q, kv, steps = lax.optimization_barrier((blocks, q, kv, steps))
    arrived = []
    for shift, block in enumerate(blocks):
        pairs = [(g * 4 + a, (1 - g) * 4 + (a + shift) % 4) for g in range(2) for a in range(4)]
        arrived.append(lax.ppermute(block, ("grp", "dp"), pairs))

    prefill = prompt_attention(q, kv)

    def own_cols(rows, which):
        return lax.dynamic_slice_in_dim(rows, which * (QCOLS // 2), QCOLS // 2, 1)

    prefill_out = joined(
        own_cols(prefill, parity), send(own_cols(prefill, 1 - parity), CORE), 0
    )[None]

    cache_shape = (2, BLOCK, HEAD_DIM // 2, PAIRS)
    steps = steps.reshape(STEPS, HALF_REQ, COLS)
    decode = decode_attention(
        parity[None].astype(jnp.int32),
        steps,
        jnp.repeat(own_len, MAXB)[None, :],
        cache_own.reshape(cache_shape),
        cache_other.reshape(cache_shape),
    ).reshape(STEPS, HALF_REQ, QCOLS)
    decode_own = lax.dynamic_slice_in_dim(decode, parity * (QCOLS // 2), QCOLS // 2, 2)
    decode_sent = lax.dynamic_slice_in_dim(decode, (1 - parity) * (QCOLS // 2), QCOLS // 2, 2)
    decode_out = joined(decode_own, send(decode_sent, CORE), 1)

    all_steps = joined(steps, send(steps, CORE), 1).reshape(STEPS * REQ_DEV, COLS)
    decode_out = arrived_attention(
        parity[None].astype(jnp.int32), decode_out.reshape(STEPS * REQ_DEV, -1), all_steps, arrived
    )
    return (prefill_out, decode_out.reshape(1, STEPS, REQ_DEV, -1))


def solution(mesh):
    placed = (
        P("grp", "dp", "tp"),
        P(),
        P(None, "tp"),
        P(None, "tp"),
        P(None, "tp"),
        P(),
        P(),
        P(),
        P("grp", None, "dp", "tp"),
        P("grp", "dp", None, "tp"),
        P("grp", "dp", None, "tp"),
        P("grp", "dp", None),
        P("grp", "dp"),
        P("grp", "dp"),
    )
    return jax.shard_map(
        body,
        mesh=mesh,
        in_specs=placed,
        out_specs=(P("grp", "dp", "tp"), P("grp", None, "dp", "tp")),
        check_vma=False,
    )
```

```python
import functools
import math

import jax
import jax.numpy as jnp
from jax import lax
from jax.experimental import pallas as pl
from jax.experimental.pallas import tpu as pltpu
from jax.sharding import PartitionSpec as P

HEAD_DIM = 128
GROUP = 8
BLOCK = 16
MAXB = 32
PROMPT = 256
REQ_DEV = 64
STEPS = 3
ROPE_BASE = 1000000.0
NORM_EPSILON = 1e-06
MASKED = -1e30
SCALE = 1.0 / math.sqrt(HEAD_DIM)
FEATURES = 8192
CHUNK = 1024
ROWS = 512
STEP_ROWS = STEPS * REQ_DEV
OWN_STEPS = STEP_ROWS // 2
ALL_ROWS = ROWS + OWN_STEPS
QCOLS = GROUP * HEAD_DIM
KVCOLS = 2 * HEAD_DIM
COLS = QCOLS + KVCOLS
HALF_REQ = REQ_DEV // 2
NBLK = 2048
PAIRS = HALF_REQ * MAXB
POWER = SCALE * math.log2(math.e)
WHOLE_VMEM = 58

CORE = [(i, i ^ 1) for i in range(16)]
XSWAP = [(i, i ^ 2) for i in range(16)]
YFAR = [(i, i ^ 8) for i in range(16)]
YUP = [(i, (i + 4) % 16) for i in range(16)]
YDOWN = [(i, (i + 12) % 16) for i in range(16)]

NT = (((1,), (1,)), ((), ()))
F32 = jnp.float32
BF16 = jnp.bfloat16


def send(array, pairs):
    return lax.ppermute(array, "tp", pairs)


def cost(*_):
    return pl.CostEstimate(flops=1, bytes_accessed=1, transcendentals=0)


def params(mebibytes):
    return pltpu.CompilerParams(vmem_limit_bytes=mebibytes * 1024 * 1024)


VMEM = pl.BlockSpec(memory_space=pltpu.VMEM)
SMEM = pl.BlockSpec(memory_space=pltpu.SMEM)


def resident(kernel, name, outs, scalars, operands, mebibytes, estimate, scratch=()):
    return pl.pallas_call(
        kernel,
        in_specs=[SMEM] + [VMEM] * len(operands),
        out_specs=[VMEM] * len(outs),
        out_shape=outs,
        scratch_shapes=list(scratch),
        compiler_params=params(mebibytes),
        cost_estimate=estimate,
        name=name,
    )(scalars, *operands)


HBM = pl.BlockSpec(memory_space=pltpu.HBM)


def arrange_kernel(which_ref, table_ref, k_ref, v_ref, out_ref, pick):
    tile = pick.shape[2]
    half = k_ref.shape[0]
    block = lax.broadcasted_iota(jnp.int32, (NBLK, tile), 0)
    for at in range(PAIRS // tile):
        lanes = pl.ds(pl.multiple_of(which_ref[0] * PAIRS + at * tile, tile), tile)
        slot = at % 2
        pick[slot] = jnp.where(block == table_ref[:, lanes], 1.0, 0.0).astype(BF16)
        out_ref[at, :half] = jnp.dot(k_ref[...], pick[slot], preferred_element_type=F32).astype(BF16)
        out_ref[at, half:] = jnp.dot(v_ref[...], pick[slot], preferred_element_type=F32).astype(BF16)


def arrange(which, table, k_flat, v_flat):
    rows = k_flat.shape[0]
    return resident(
        arrange_kernel,
        "arrange_cache",
        [jax.ShapeDtypeStruct((PAIRS // 256, 2 * rows, 256), BF16)],
        which,
        (table, k_flat, v_flat),
        WHOLE_VMEM,
        cost(),
        [pltpu.VMEM((2, NBLK, 256), BF16)],
    )[0]


def parts_kernel(cuts, _, *refs):
    for (start, stop), source, out in zip(cuts, refs[:3], refs[3:]):
        out[...] = source[start:stop]


def take_parts(scalars, arrays, cuts):
    outs = [jax.ShapeDtypeStruct((stop - start, CHUNK), BF16) for start, stop in cuts]
    return resident(functools.partial(parts_kernel, cuts), "take_parts", outs, scalars, arrays, 8, cost())


def handover_kernel(scalar_ref, own_ref, other_ref, *outs):
    parity, rank = scalar_ref[4], scalar_ref[5]
    for shift in range(4):
        target = (rank + shift) % 4
        at = jnp.int32(0)
        request = jnp.int32(0)
        for prompt in range(4):
            chosen = scalar_ref[prompt] // REQ_DEV == target
            at = jnp.where(chosen, prompt, at)
            request = jnp.where(chosen, scalar_ref[prompt] % REQ_DEV, request)
        rows = pl.ds(pl.multiple_of((at % 2) * PROMPT, PROMPT), PROMPT)
        outs[shift][:PROMPT] = jnp.where(at // 2 == parity, own_ref[rows, :], other_ref[rows, :])
        outs[shift][PROMPT:] = jnp.full((16, 2 * HEAD_DIM), request.astype(F32), F32).astype(BF16)


def handover(scalars, own, other):
    shape = jax.ShapeDtypeStruct((PROMPT + 16, KVCOLS), BF16)
    return resident(
        handover_kernel, "sort_prompts", [shape] * 4, scalars, (own, other), 8, cost(0, 2_000_000)
    )


def turn(rows, cosine, sine):
    return rows * cosine + pltpu.roll(rows, HEAD_DIM // 2, 1) * sine


class Copies:
    def __init__(self, sems):
        self.sems, self.made = sems, []

    def __call__(self, source, target):
        copy = pltpu.make_async_copy(source, target, self.sems.at[len(self.made)])
        copy.start()
        self.made.append(copy)
        return copy


def fetch_rows(copies, arrays, parts, lhs, at):
    cols = pl.ds(at * CHUNK, CHUNK)
    row, made = 0, []
    for source, start, stop in parts:
        target = lhs.at[pl.ds(row, stop - start), cols]
        made.append(copies(arrays[source].at[pl.ds(start, stop - start)], target))
        row += stop - start
    return made


def fetch_wide(copies, refs, chunk, parity, target, at):
    place = pl.ds(pl.multiple_of(chunk * CHUNK, CHUNK), CHUNK)
    half = QCOLS // 2
    made = []
    for ref, where in zip(refs, (parity, 1 - parity)):
        cols = pl.ds(pl.multiple_of(where * half, half), half)
        made.append(copies(ref.at[place, :], target.at[pl.ds(at * CHUNK, CHUNK), cols]))
    return made


def fetch_thin(copies, refs, chunk, parity, target, at):
    place = pl.ds(pl.multiple_of(chunk * CHUNK, CHUNK), CHUNK)
    half = HEAD_DIM // 2
    made = []
    for which, pair in enumerate((refs[:2], refs[2:])):
        for ref, where in zip(pair, (parity, 1 - parity)):
            rows = pl.ds(pl.multiple_of(which * HEAD_DIM + where * half, half), half)
            made.append(copies(ref.at[:, place], target.at[rows, pl.ds(at * CHUNK, CHUNK)]))
    return made


def project_kernel(chunks, order, count, first, idx_ref, *refs):
    wide_refs, thin_refs, refs = refs[:2], refs[2:6], refs[6:]
    arrays, refs = refs[:count], refs[count:]
    before, refs = ((), refs) if first else (refs[:2], refs[2:])
    q_total, kv_total, lhs, wide, thin, sems = refs[:6]
    parity = idx_ref[len(chunks)]
    copies = Copies(sems)
    groups = []
    for at, parts in enumerate(chunks):
        groups.append(
            fetch_rows(copies, arrays, parts, lhs, at)
            + fetch_wide(copies, wide_refs, idx_ref[at], parity, wide, at)
            + fetch_thin(copies, thin_refs, idx_ref[at], parity, thin, at)
        )
    if not first:
        groups[0] += [copies(before[0], refs[6]), copies(before[1], refs[7])]
        earlier = refs[6:8]
    for number, (start, stop) in enumerate(order):
        for group in groups[start:stop]:
            for copy in group:
                copy.wait()
        span = slice(start * CHUNK, stop * CHUNK)
        q_part = jnp.dot(lhs[:, span], wide[span, :], preferred_element_type=F32)
        kv_part = lax.dot_general(lhs[:, span], thin[:, span], NT, preferred_element_type=F32)
        if number:
            q_total[...] += q_part
            kv_total[...] += kv_part
        elif first:
            q_total[...] = q_part
            kv_total[...] = kv_part
        else:
            q_total[...] = earlier[0][...] + q_part
            kv_total[...] = earlier[1][...] + kv_part


def chunk_scalars(places, parity):
    return jnp.stack(list(places) + [parity]).astype(jnp.int32)


def from_hbm(kernel, name, outs, scalars, operands, resident_operands, scratch, limit=58):
    return pl.pallas_call(
        kernel,
        in_specs=[SMEM] + [HBM] * len(operands) + [VMEM] * len(resident_operands),
        out_specs=[VMEM] * len(outs),
        out_shape=outs,
        scratch_shapes=scratch,
        compiler_params=params(limit),
        cost_estimate=cost(),
        name=name,
    )(scalars, *operands, *resident_operands)


def project(arrays, chunks, order, scalars, weights, before=()):
    count = len(chunks)
    totals = [(ALL_ROWS, QCOLS), (ALL_ROWS, KVCOLS)]
    scratch = [
        pltpu.VMEM((ALL_ROWS, count * CHUNK), BF16),
        pltpu.VMEM((count * CHUNK, QCOLS), BF16),
        pltpu.VMEM((KVCOLS, count * CHUNK), BF16),
        pltpu.SemaphoreType.DMA((sum(len(parts) + 6 for parts in chunks) + 2,)),
    ]
    if before:
        scratch += [pltpu.VMEM(shape, F32) for shape in totals]
    return from_hbm(
        functools.partial(project_kernel, chunks, order, len(arrays), not before),
        "project_rows",
        [jax.ShapeDtypeStruct(shape, F32) for shape in totals],
        scalars,
        (*weights, *arrays, *before),
        (),
        scratch,
    )


def all_angles(first, second):
    return jnp.concatenate([first[...]] * (ROWS // PROMPT) + [second[...]], axis=0)


def keys_kernel(parts, count, idx_ref, *refs):
    thin_refs, before = refs[:4], refs[4]
    arrays, refs = refs[5 : 5 + count], refs[5 + count :]
    kb_ref, vb_ref, cos_ref, sin_ref, scos_ref, ssin_ref, out_ref, steps_out, lhs, thin, total, sems = refs
    copies = Copies(sems)
    made = fetch_rows(copies, arrays, parts, lhs, 0)
    made += fetch_thin(copies, thin_refs, idx_ref[0], idx_ref[1], thin, 0)
    made.append(copies(before, total))
    for copy in made:
        copy.wait()
    rows = total[...] + lax.dot_general(lhs[...], thin[...], NT, preferred_element_type=F32)
    cosine, sine = all_angles(cos_ref, scos_ref), all_angles(sin_ref, ssin_ref)
    keys = turn(rows[:, :HEAD_DIM] + kb_ref[...], cosine, sine).astype(BF16)
    values = (rows[:, HEAD_DIM:] + vb_ref[...]).astype(BF16)
    out_ref[:, :HEAD_DIM] = keys[:ROWS]
    out_ref[:, HEAD_DIM:] = values[:ROWS]
    steps_out[:, :HEAD_DIM] = keys[ROWS:].astype(F32)
    steps_out[:, HEAD_DIM:] = values[ROWS:].astype(F32)


def last_keys(arrays, parts, scalars, weights, before, ending):
    return from_hbm(
        functools.partial(keys_kernel, parts, len(arrays)),
        "project_keys",
        [jax.ShapeDtypeStruct((ROWS, KVCOLS), BF16), jax.ShapeDtypeStruct((OWN_STEPS, KVCOLS), F32)],
        scalars,
        (*weights, before, *arrays),
        ending,
        [
            pltpu.VMEM((ALL_ROWS, CHUNK), BF16),
            pltpu.VMEM((KVCOLS, CHUNK), BF16),
            pltpu.VMEM((ALL_ROWS, KVCOLS), F32),
            pltpu.SemaphoreType.DMA((len(parts) + 5,)),
        ],
        16,
    )


def queries_kernel(parts, count, idx_ref, *refs):
    wide_refs, before = refs[:2], refs[2]
    arrays, refs = refs[3 : 3 + count], refs[3 + count :]
    qbias_ref, cos_ref, sin_ref, scos_ref, ssin_ref, out_ref, steps_out, lhs, wide, total, sems = refs
    copies = Copies(sems)
    made = fetch_rows(copies, arrays, parts, lhs, 0)
    made += fetch_wide(copies, wide_refs, idx_ref[0], idx_ref[1], wide, 0)
    last = copies(before, total)
    for copy in made:
        copy.wait()
    rows = jnp.dot(lhs[...], wide[...], preferred_element_type=F32)
    last.wait()
    total[...] += rows
    cosine, sine = all_angles(cos_ref, scos_ref), all_angles(sin_ref, ssin_ref)
    for head in range(GROUP):
        cols = slice(head * HEAD_DIM, (head + 1) * HEAD_DIM)
        rows = turn(total[:, cols] + qbias_ref[:, cols], cosine, sine).astype(BF16)
        out_ref[:, cols] = rows[:ROWS]
        steps_out[:, cols] = rows[ROWS:].astype(F32)


def last_queries(arrays, parts, scalars, weights, before, ending):
    return from_hbm(
        functools.partial(queries_kernel, parts, len(arrays)),
        "project_queries",
        [jax.ShapeDtypeStruct((ROWS, QCOLS), BF16), jax.ShapeDtypeStruct((OWN_STEPS, QCOLS), F32)],
        scalars,
        (*weights, before, *arrays),
        ending,
        [
            pltpu.VMEM((ALL_ROWS, CHUNK), BF16),
            pltpu.VMEM((CHUNK, QCOLS), BF16),
            pltpu.VMEM((ALL_ROWS, QCOLS), F32),
            pltpu.SemaphoreType.DMA((len(parts) + 3,)),
        ],
    )


def split_kernel(par_ref, prompts_ref, steps_ref, own_out, other_out, sems):
    copies = Copies(sems)
    for out, which in ((other_out, 1 - par_ref[0]), (own_out, par_ref[0])):
        rows = pl.ds(pl.multiple_of(which * ROWS, ROWS), ROWS)
        copies(prompts_ref.at[rows], out.at[pl.ds(0, ROWS)])
        rows = pl.ds(pl.multiple_of(which * HALF_REQ, HALF_REQ), HALF_REQ)
        for s in range(STEPS):
            copies(steps_ref.at[s, rows], out.at[pl.ds(ROWS + s * HALF_REQ, HALF_REQ)])
    for copy in copies.made:
        copy.wait()


def split_rows(scalars, prompts, steps):
    half = jax.ShapeDtypeStruct((ALL_ROWS, prompts.shape[1]), BF16)
    return pl.pallas_call(
        split_kernel,
        in_specs=[SMEM, HBM, HBM],
        out_specs=[VMEM] * 2,
        out_shape=[half] * 2,
        scratch_shapes=[pltpu.SemaphoreType.DMA((2 + 2 * STEPS,))],
        compiler_params=params(WHOLE_VMEM),
        cost_estimate=cost(),
        name="split_rows",
    )(scalars, prompts, steps)


def halves(parity, wide, own_out, other_out):
    half = wide.shape[1] // 2
    own_out[...] = jnp.where(parity == 0, wide[:, :half], wide[:, half:])
    other_out[...] = jnp.where(parity == 0, wide[:, half:], wide[:, :half])


def prompt_kernel(par_ref, q_ref, kv_ref, own_out, other_out, out_ref):
    row = lax.broadcasted_iota(jnp.int32, (PROMPT, PROMPT), 0)
    col = lax.broadcasted_iota(jnp.int32, (PROMPT, PROMPT), 1)
    causal = row >= col
    for prompt in range(ROWS // PROMPT):
        rows = slice(prompt * PROMPT, (prompt + 1) * PROMPT)
        keys, values = kv_ref[rows, :HEAD_DIM], kv_ref[rows, HEAD_DIM:]
        for head in range(GROUP):
            cols = slice(head * HEAD_DIM, (head + 1) * HEAD_DIM)
            scores = lax.dot_general(q_ref[rows, cols], keys, NT, preferred_element_type=F32)
            scores = jnp.where(causal, scores, MASKED)
            powers = jnp.exp2((scores - jnp.max(scores, axis=1, keepdims=True)) * POWER)
            weights = (powers * (1.0 / jnp.sum(powers, axis=1, keepdims=True))).astype(BF16)
            out_ref[rows, cols] = jnp.dot(weights, values, preferred_element_type=F32).astype(BF16)
    halves(par_ref[0], out_ref, own_out, other_out)


def prompt_attention(scalars, q, kv):
    half = jax.ShapeDtypeStruct((ROWS, QCOLS // 2), BF16)
    return resident(
        prompt_kernel,
        "prompt_attention",
        [half, half],
        scalars,
        (q, kv),
        12,
        cost(),
        [pltpu.VMEM(q.shape, BF16)],
    )


def join_kernel(par_ref, own_ref, other_ref, out_ref):
    size = own_ref.shape[0]
    own, other = own_ref[...], other_ref[...]
    out_ref[:size] = jnp.where(par_ref[0] == 0, own, other)
    out_ref[size:] = jnp.where(par_ref[0] == 0, other, own)


def join_rows(parity, own, other):
    out = jax.ShapeDtypeStruct((2 * own.shape[0], own.shape[1]), BF16)
    return resident(join_kernel, "join_rows", [out], parity, (own, other), 8, cost())[0]


def decode_kernel(
    par_ref, own_ref, other_ref, q_ref, kv_ref, len_ref, spread_ref,
    own_out, other_out, scores, mixed, wide, cache, sems,
):
    parity = par_ref[0]
    half_dim = HEAD_DIM // 2
    copies = Copies(sems)
    for group in range(HALF_REQ // 8):
        for ref, where in ((own_ref, parity), (other_ref, 1 - parity)):
            dims = pl.ds(pl.multiple_of(where * half_dim, half_dim), half_dim)
            copies(ref.at[group], cache.at[group, :, dims])
    for group in range(HALF_REQ // 8):
        for copy in copies.made[2 * group : 2 * group + 2]:
            copy.wait()
        attend_group(group, q_ref, kv_ref, len_ref, cache.at[group], scores.at[group % 2], mixed)
    rounded = mixed[...].reshape(OWN_STEPS, QCOLS).astype(BF16)
    wide[...] = jnp.dot(rounded, spread_ref[...], preferred_element_type=F32).astype(BF16)
    halves(parity, wide, own_out, other_out)


def attend_group(group, q_ref, kv_ref, len_ref, cache, scores, mixed):
    rows = GROUP * STEPS * 8
    lanes = GROUP * MAXB

    def step_rows(s):
        return slice(s * HALF_REQ + group * 8, s * HALF_REQ + group * 8 + 8)

    queries = jnp.concatenate(
        [
            q_ref[step_rows(s), m * HEAD_DIM : (m + 1) * HEAD_DIM]
            for m in range(GROUP)
            for s in range(STEPS)
        ],
        axis=0,
    ).astype(BF16)
    row = lax.broadcasted_iota(jnp.int32, (rows, 128), 0) % 8
    lane = lax.broadcasted_iota(jnp.int32, (rows, 128), 1)
    lower = row < 4
    reach = len_ref[:, group * lanes : (group + 1) * lanes]
    reach = jnp.where(lower, reach[:, :128], reach[:, 128:])
    place = jnp.where(row % 4 == lane // MAXB, (lane % MAXB) * BLOCK, MAXB * BLOCK * 2) - reach
    top = jnp.full((rows, 128), MASKED, F32)
    for slot in range(BLOCK):
        part = jnp.dot(queries, cache[slot], preferred_element_type=F32)
        part = jnp.where(lower, part[:, :128], part[:, 128:])
        part = jnp.where(place < -slot, part, MASKED)
        scores[slot] = part
        top = jnp.maximum(top, part)
    fresh = jnp.concatenate([kv_ref[step_rows(s), :] for s in range(STEPS)], axis=0)
    fresh = jnp.concatenate([fresh, jnp.zeros((128 - 8 * STEPS, KVCOLS), F32)], axis=0).astype(BF16)
    newer = lax.dot_general(queries, fresh[:, :HEAD_DIM], NT, preferred_element_type=F32)
    at_step = (lax.broadcasted_iota(jnp.int32, (rows, 128), 0) // 8) % STEPS
    newer = jnp.where((row == lane % 8) & (lane // 8 <= at_step), newer, MASKED)
    peak = jnp.max(jnp.maximum(top, newer), axis=1, keepdims=True)
    newer = jnp.exp2((newer - peak) * POWER)
    weight_sum = newer
    for slot in range(BLOCK):
        powers = jnp.exp2((scores[slot] - peak) * POWER)
        scores[slot] = powers
        weight_sum = weight_sum + powers
    share = 1.0 / jnp.sum(weight_sum, axis=1, keepdims=True)
    result = jnp.dot(
        (newer * share).astype(BF16), fresh[:, HEAD_DIM:], preferred_element_type=F32
    )
    for slot in range(BLOCK):
        values = cache[BLOCK + slot]
        weight = scores[slot] * share
        weight = jnp.concatenate([jnp.where(lower, weight, 0.0), jnp.where(lower, 0.0, weight)], axis=1)
        result = result + lax.dot_general(weight.astype(BF16), values, NT, preferred_element_type=F32)
    for m in range(GROUP):
        for s in range(STEPS):
            at = (m * STEPS + s) * 8
            mixed[s, group * 8 : (group + 1) * 8, m * HEAD_DIM : (m + 1) * HEAD_DIM] = result[at : at + 8]


def decode_attention(parity, q, kv, lengths, own, other, spread):
    groups = HALF_REQ // 8
    split = (groups, 2 * BLOCK, HEAD_DIM // 2, GROUP * MAXB)
    return from_hbm(
        decode_kernel,
        "decode_attention",
        [jax.ShapeDtypeStruct((OWN_STEPS, QCOLS // 2), BF16)] * 2,
        parity,
        (own.reshape(split), other.reshape(split)),
        (q, kv, lengths, spread),
        [
            pltpu.VMEM((2, BLOCK, GROUP * STEPS * 8, 128), F32),
            pltpu.VMEM((STEPS, HALF_REQ, QCOLS), F32),
            pltpu.VMEM((OWN_STEPS, QCOLS), BF16),
            pltpu.VMEM((groups, 2 * BLOCK, HEAD_DIM, GROUP * MAXB), BF16),
            pltpu.SemaphoreType.DMA((2 * groups,)),
        ],
    )


def arrived_kernel(
    par_ref, own_ref, other_ref, q_ref, kv_ref, q_other_ref, kv_other_ref, spread_ref, *refs
):
    arrived, out_ref = refs[:4], refs[4]
    own_cols = QCOLS // 2
    rows = 4 * GROUP * 8

    def by_arrival(shape, axis, size):
        which = lax.broadcasted_iota(jnp.int32, shape, axis) // size
        picked = jnp.zeros(shape, jnp.int32)
        for at in range(4):
            picked = jnp.where(which == at, requests[at], picked)
        return picked

    requests = [arrived[at][PROMPT : PROMPT + 16, :128].astype(jnp.int32)[:1, :1] for at in range(4)]
    shape = (32, OWN_STEPS)
    step = lax.broadcasted_iota(jnp.int32, shape, 0) % 8
    col = lax.broadcasted_iota(jnp.int32, shape, 1)
    parity = par_ref[0]

    def picked_rows(half, ref):
        request = col % HALF_REQ + half * HALF_REQ
        pick = (col // HALF_REQ == step) & (request == by_arrival(shape, 0, 8))
        pick = jnp.where(pick, 1.0, 0.0).astype(BF16)
        return jnp.dot(pick, ref[...].astype(BF16), preferred_element_type=F32)

    own = picked_rows(parity, q_ref) + picked_rows(1 - parity, q_other_ref)
    fresh = picked_rows(parity, kv_ref) + picked_rows(1 - parity, kv_other_ref)
    queries = jnp.concatenate(
        [
            own[at * 8 : (at + 1) * 8, m * HEAD_DIM : (m + 1) * HEAD_DIM]
            for at in range(4)
            for m in range(GROUP)
        ],
        axis=0,
    ).astype(BF16)
    fresh = jnp.concatenate([fresh, jnp.zeros((96, KVCOLS), F32)], axis=0).astype(BF16)
    part = GROUP * 8
    scores = jnp.concatenate(
        [
            lax.dot_general(
                queries[at * part : (at + 1) * part],
                arrived[at][:PROMPT, :HEAD_DIM],
                NT,
                preferred_element_type=F32,
            )
            for at in range(4)
        ],
        axis=0,
    )
    newer = lax.dot_general(queries, fresh[:, :HEAD_DIM], NT, preferred_element_type=F32)
    nrow = lax.broadcasted_iota(jnp.int32, (rows, 128), 0)
    nlane = lax.broadcasted_iota(jnp.int32, (rows, 128), 1)
    seen = (nlane // 8 == nrow // part) & (nlane % 8 < STEPS) & (nlane % 8 <= nrow % 8)
    newer = jnp.where(seen, newer, MASKED)
    peak = jnp.maximum(jnp.max(scores, axis=1, keepdims=True), jnp.max(newer, axis=1, keepdims=True))
    scores = jnp.exp2((scores - peak) * POWER)
    newer = jnp.exp2((newer - peak) * POWER)
    share = 1.0 / (jnp.sum(scores, axis=1, keepdims=True) + jnp.sum(newer, axis=1, keepdims=True))
    scores = (scores * share).astype(BF16)
    result = jnp.concatenate(
        [
            jnp.dot(
                scores[at * part : (at + 1) * part],
                arrived[at][:PROMPT, HEAD_DIM:],
                preferred_element_type=F32,
            )
            for at in range(4)
        ],
        axis=0,
    )
    result = result + jnp.dot(
        (newer * share).astype(BF16), fresh[:, HEAD_DIM:], preferred_element_type=F32
    )
    wide = jnp.concatenate(
        [
            jnp.concatenate(
                [result[at * part + m * 8 : at * part + (m + 1) * 8] for m in range(GROUP)], axis=1
            )
            for at in range(4)
        ],
        axis=0,
    )
    spread = spread_ref[:, pl.ds(pl.multiple_of(par_ref[0] * own_cols, own_cols), own_cols)]
    fixed = jnp.dot(wide.astype(BF16), spread, preferred_element_type=F32).astype(BF16)
    shape = (STEP_ROWS, 32)
    line = lax.broadcasted_iota(jnp.int32, shape, 0)
    step = lax.broadcasted_iota(jnp.int32, shape, 1) % 8
    back = (line == step * REQ_DEV + by_arrival(shape, 1, 8)) & (step < STEPS)
    placed = jnp.dot(jnp.where(back, 1.0, 0.0).astype(BF16), fixed, preferred_element_type=F32)
    line = lax.broadcasted_iota(jnp.int32, (STEP_ROWS, own_cols), 0) % REQ_DEV
    here = line == requests[0]
    for at in range(1, 4):
        here = here | (line == requests[at])
    mine, theirs = own_ref[...], other_ref[...]
    low = jnp.where(par_ref[0] == 0, mine, theirs)
    high = jnp.where(par_ref[0] == 0, theirs, mine)
    base = jnp.concatenate(
        [
            part[s * HALF_REQ : (s + 1) * HALF_REQ].astype(F32)
            for s in range(STEPS)
            for part in (low, high)
        ],
        axis=0,
    )
    out_ref[...] = jnp.where(here, placed, base).astype(BF16)


def arrived_attention(parity, own, other, steps, spread, arrived):
    return resident(
        arrived_kernel,
        "arrived_attention",
        [jax.ShapeDtypeStruct((STEP_ROWS, QCOLS // 2), BF16)],
        parity,
        (own, other, *steps, spread, *arrived),
        16,
        cost(500_000_000, 2_000_000, 100_000),
    )[0]


def body(
    prompt_tokens,
    norm_gain,
    q_weight,
    k_weight,
    v_weight,
    q_bias,
    k_bias,
    v_bias,
    decode_tokens,
    k_cache,
    v_cache,
    block_table,
    context_len,
    prompt_dest,
):
    tp_rank = lax.axis_index("tp")
    dp_rank = lax.axis_index("dp")
    parity = tp_rank % 2
    chip = tp_rank // 2
    y_at, x_at = chip // 2, chip % 2
    lengths = context_len[0]
    parity_ref = parity[None].astype(jnp.int32)
    barrier = lax.optimization_barrier

    def joined(own, other, axis):
        return jnp.where(
            parity == 0,
            jnp.concatenate([own, other], axis=axis),
            jnp.concatenate([other, own], axis=axis),
        )

    mine, theirs = split_rows(parity_ref, prompt_tokens[0], decode_tokens[0])
    held = joined(mine, send(theirs, CORE), 1)
    wide = held.astype(F32)
    squares = jnp.sum(wide * wide, axis=1)
    squares = squares + send(squares, XSWAP)
    squares = squares + sum(
        send(squares, [(i, (i + 4 * dy) % 16) for i in range(16)]) for dy in range(1, 4)
    )
    rstd = lax.rsqrt(squares * (1.0 / FEATURES) + NORM_EPSILON)[:, None]
    chip_cols = lambda array, width: lax.dynamic_slice_in_dim(array, chip * width, width, 0)[None, :]
    held = (wide * rstd * chip_cols(norm_gain, CHUNK)).astype(BF16)

    k_w, v_w, squares_done = barrier((k_weight.T, v_weight.T, squares))
    k_other, v_other = send(k_w, CORE), send(v_w, CORE)

    held, q_w, k_other, v_other = barrier((held, q_weight, k_other, v_other))
    side, up, down = send(held, XSWAP), send(held, YUP), send(held, YDOWN)
    wide_weights = (q_w, send(q_w, CORE))
    thin_weights = (k_w, k_other, v_w, v_other)
    weights = wide_weights + thin_weights

    table = block_table[0]
    turned = lambda cache: jnp.transpose(cache[0], (1, 2, 0)).reshape(BLOCK * HEAD_DIM // 2, NBLK)
    k_flat, v_flat = turned(k_cache), turned(v_cache)
    table, held = barrier((table.reshape(1, 2 * PAIRS), held))
    cache_theirs = arrange(1 - parity_ref, table, k_flat, v_flat)

    (cache_theirs, zero, lengths, q_bias, k_bias, v_bias) = barrier(
        (cache_theirs, jnp.int32(0), lengths, q_bias, k_bias, v_bias)
    )
    spread_row = lax.broadcasted_iota(jnp.int32, (QCOLS, QCOLS), 0) + zero
    spread_col = lax.broadcasted_iota(jnp.int32, (QCOLS, QCOLS), 1)
    spread = spread_col == (spread_row % HEAD_DIM) * GROUP + spread_row // HEAD_DIM
    spread = spread.astype(BF16)
    own_len = lax.dynamic_slice_in_dim(lengths, parity * HALF_REQ, HALF_REQ, 0)
    reach = jnp.repeat(own_len, MAXB)[None, :]

    exponent = jnp.arange(HEAD_DIM // 2, dtype=F32) * (2.0 / HEAD_DIM)
    frequency = jnp.power(F32(ROPE_BASE), -exponent)

    def angles(positions):
        angle = positions.astype(F32)[:, None] * frequency
        cosine, sine = jnp.cos(angle), jnp.sin(angle)
        return jnp.concatenate([cosine, cosine], axis=1), jnp.concatenate([-sine, sine], axis=1)

    prompt_angles = angles(jnp.arange(PROMPT, dtype=jnp.int32) + zero)
    step_angles = angles(
        (own_len[None, :] + jnp.arange(STEPS, dtype=jnp.int32)[:, None]).reshape(-1)
    )
    q_offset = chip_cols(q_bias, QCOLS)
    kv_offsets = (chip_cols(k_bias, HEAD_DIM), chip_cols(v_bias, HEAD_DIM))
    place = lambda dy, dx: ((y_at + dy) % 4) * 2 + (x_at + dx) % 2
    early = chunk_scalars([place(0, 0), place(0, 1), place(3, 0), place(1, 0)], parity)
    late = chunk_scalars([place(2, 0), place(3, 1), place(1, 1)], parity)
    final = chunk_scalars([place(2, 1)], parity)

    scalars = jnp.concatenate([prompt_dest[0], parity[None], dp_rank[None]]).astype(jnp.int32)
    (side, up, down, cache_theirs, reach, early, late, final, spread, offsets, both_angles, scalars) = barrier(
        (
            (side, up, down, cache_theirs, reach, early, late, final, spread)
            + ((q_offset, *kv_offsets), (*prompt_angles, *step_angles), scalars)
        )
    )
    side_up, far, side_down = send(side, YUP), send(down, YDOWN), send(down, XSWAP)
    cache_other = send(cache_theirs, CORE)
    table, side_sent = barrier((table, side))
    cache_own = arrange(parity_ref, table, k_flat, v_flat)
    totals = project(
        (held, side, up, down),
        tuple(((source, 0, ALL_ROWS),) for source in range(4)),
        ((0, 1), (1, 2), (2, 4)),
        early,
        weights,
    )

    side_up, far, side_down, totals, cache_own = barrier(
        (side_up, far, side_down, totals, cache_own)
    )
    cut_a, cut_b = 208, 416
    sent = take_parts(
        parity_ref, (side_up, side_down, far), ((0, cut_a), (cut_a, cut_b), (cut_b, ALL_ROWS))
    )
    sent, side_up, side_down, far = barrier((sent, side_up, side_down, far))
    last = (send(sent[0], YUP), send(sent[1], YDOWN), send(sent[2], XSWAP))
    q_total, kv_total = project(
        (far, side_up, side_down),
        tuple(((source, 0, ALL_ROWS),) for source in range(3)),
        ((0, 1), (1, 3)),
        late,
        weights,
        before=totals,
    )
    parts = ((0, 0, cut_a), (1, 0, cut_b - cut_a), (2, 0, ALL_ROWS - cut_b))
    kv, kv_steps = last_keys(
        last, parts, final, thin_weights, kv_total, (*offsets[1:], *both_angles)
    )

    kv_steps_other = send(kv_steps, CORE)
    blocks = handover(scalars, kv, send(kv, CORE))
    blocks, last, q_total, kv_steps_other = barrier((blocks, last, q_total, kv_steps_other))
    arrived = []
    for shift, block in enumerate(blocks):
        pairs = [(g * 4 + a, (1 - g) * 4 + (a + shift) % 4) for g in range(2) for a in range(4)]
        arrived.append(lax.ppermute(block, ("grp", "dp"), pairs))

    q, q_steps = last_queries(
        last, parts, final, wide_weights, q_total, (offsets[0], *both_angles)
    )
    q_steps_other = send(q_steps, CORE)
    decode_own, decode_sent = decode_attention(
        parity_ref,
        q_steps,
        kv_steps,
        reach,
        cache_own,
        cache_other,
        spread,
    )
    prefill_own, prefill_sent = prompt_attention(parity_ref, q, kv)
    arrived, prefill_sent, decode_sent = barrier((arrived, prefill_sent, decode_sent))
    decode_other = send(decode_sent, CORE)
    prefill_out = join_rows(parity_ref, prefill_own, send(prefill_sent, CORE))[None]
    steps = (q_steps, kv_steps, q_steps_other, kv_steps_other)
    decode_out = arrived_attention(parity_ref, decode_own, decode_other, steps, spread, arrived)
    return (prefill_out, decode_out.reshape(1, STEPS, REQ_DEV, -1))


def solution(mesh):
    placed = (
        P("grp", "dp", "tp"),
        P(),
        P(None, "tp"),
        P(None, "tp"),
        P(None, "tp"),
        P(),
        P(),
        P(),
        P("grp", None, "dp", "tp"),
        P("grp", "dp", None, "tp"),
        P("grp", "dp", None, "tp"),
        P("grp", "dp", None),
        P("grp", "dp"),
        P("grp", "dp"),
    )
    return jax.shard_map(
        body,
        mesh=mesh,
        in_specs=placed,
        out_specs=(P("grp", "dp", "tp"), P("grp", None, "dp", "tp")),
        check_vma=False,
    )
```

```python
import functools
import math

import jax
import jax.numpy as jnp
from jax import lax
from jax.experimental import pallas as pl
from jax.experimental.pallas import tpu as pltpu
from jax.sharding import PartitionSpec as P

HEAD_DIM = 128
GROUP = 8
BLOCK = 16
MAXB = 32
PROMPT = 256
REQ_DEV = 64
STEPS = 3
ROPE_BASE = 1000000.0
NORM_EPSILON = 1e-06
MASKED = -1e30
SCALE = 1.0 / math.sqrt(HEAD_DIM)
FEATURES = 8192
CHUNK = 1024
ROWS = 512
STEP_ROWS = STEPS * REQ_DEV
OWN_STEPS = STEP_ROWS // 2
ALL_ROWS = ROWS + OWN_STEPS
QCOLS = GROUP * HEAD_DIM
KVCOLS = 2 * HEAD_DIM
COLS = QCOLS + KVCOLS
HALF_REQ = REQ_DEV // 2
NBLK = 2048
PAIRS = HALF_REQ * MAXB
POWER = SCALE * math.log2(math.e)
WHOLE_VMEM = 58

CORE = [(i, i ^ 1) for i in range(16)]
XSWAP = [(i, i ^ 2) for i in range(16)]
YFAR = [(i, i ^ 8) for i in range(16)]
YUP = [(i, (i + 4) % 16) for i in range(16)]
YDOWN = [(i, (i + 12) % 16) for i in range(16)]

NT = (((1,), (1,)), ((), ()))
F32 = jnp.float32
BF16 = jnp.bfloat16


def send(array, pairs):
    return lax.ppermute(array, "tp", pairs)


def cost(*_):
    return pl.CostEstimate(flops=1, bytes_accessed=1, transcendentals=0)


def params(mebibytes):
    return pltpu.CompilerParams(vmem_limit_bytes=mebibytes * 1024 * 1024)


VMEM = pl.BlockSpec(memory_space=pltpu.VMEM)
SMEM = pl.BlockSpec(memory_space=pltpu.SMEM)


def resident(kernel, name, outs, scalars, operands, mebibytes, estimate, scratch=()):
    return pl.pallas_call(
        kernel,
        in_specs=[SMEM] + [VMEM] * len(operands),
        out_specs=[VMEM] * len(outs),
        out_shape=outs,
        scratch_shapes=list(scratch),
        compiler_params=params(mebibytes),
        cost_estimate=estimate,
        name=name,
    )(scalars, *operands)


HBM = pl.BlockSpec(memory_space=pltpu.HBM)


def arrange_kernel(which_ref, table_ref, k_ref, v_ref, out_ref, pick):
    tile = pick.shape[2]
    half = k_ref.shape[0]
    block = lax.broadcasted_iota(jnp.int32, (NBLK, tile), 0)
    for at in range(PAIRS // tile):
        lanes = pl.ds(pl.multiple_of(which_ref[0] * PAIRS + at * tile, tile), tile)
        slot = at % 2
        pick[slot] = jnp.where(block == table_ref[:, lanes], 1.0, 0.0).astype(BF16)
        out_ref[at, :half] = jnp.dot(k_ref[...], pick[slot], preferred_element_type=F32).astype(BF16)
        out_ref[at, half:] = jnp.dot(v_ref[...], pick[slot], preferred_element_type=F32).astype(BF16)


def arrange(which, table, k_flat, v_flat):
    rows = k_flat.shape[0]
    return resident(
        arrange_kernel,
        "arrange_cache",
        [jax.ShapeDtypeStruct((PAIRS // 256, 2 * rows, 256), BF16)],
        which,
        (table, k_flat, v_flat),
        WHOLE_VMEM,
        cost(),
        [pltpu.VMEM((2, NBLK, 256), BF16)],
    )[0]


def parts_kernel(cuts, _, *refs):
    for (start, stop), source, out in zip(cuts, refs[:3], refs[3:]):
        out[...] = source[start:stop]


def take_parts(scalars, arrays, cuts):
    outs = [jax.ShapeDtypeStruct((stop - start, CHUNK), BF16) for start, stop in cuts]
    return resident(functools.partial(parts_kernel, cuts), "take_parts", outs, scalars, arrays, 8, cost())


def handover_kernel(scalar_ref, own_ref, other_ref, *outs):
    parity, rank = scalar_ref[4], scalar_ref[5]
    for shift in range(4):
        target = (rank + shift) % 4
        at = jnp.int32(0)
        request = jnp.int32(0)
        for prompt in range(4):
            chosen = scalar_ref[prompt] // REQ_DEV == target
            at = jnp.where(chosen, prompt, at)
            request = jnp.where(chosen, scalar_ref[prompt] % REQ_DEV, request)
        rows = pl.ds(pl.multiple_of((at % 2) * PROMPT, PROMPT), PROMPT)
        outs[shift][:PROMPT] = jnp.where(at // 2 == parity, own_ref[rows, :], other_ref[rows, :])
        outs[shift][PROMPT:] = jnp.full((16, 2 * HEAD_DIM), request.astype(F32), F32).astype(BF16)


def handover(scalars, own, other):
    shape = jax.ShapeDtypeStruct((PROMPT + 16, KVCOLS), BF16)
    return resident(
        handover_kernel, "sort_prompts", [shape] * 4, scalars, (own, other), WHOLE_VMEM, cost()
    )


def turn(rows, cosine, sine):
    return rows * cosine + pltpu.roll(rows, HEAD_DIM // 2, 1) * sine


class Copies:
    def __init__(self, sems):
        self.sems, self.made = sems, []

    def __call__(self, source, target):
        copy = pltpu.make_async_copy(source, target, self.sems.at[len(self.made)])
        copy.start()
        self.made.append(copy)
        return copy


def fetch_rows(copies, arrays, parts, lhs, at):
    cols = pl.ds(at * CHUNK, CHUNK)
    row, made = 0, []
    for source, start, stop in parts:
        target = lhs.at[pl.ds(row, stop - start), cols]
        made.append(copies(arrays[source].at[pl.ds(start, stop - start)], target))
        row += stop - start
    return made


def fetch_wide(copies, refs, chunk, parity, target, at):
    place = pl.ds(pl.multiple_of(chunk * CHUNK, CHUNK), CHUNK)
    half = QCOLS // 2
    made = []
    for ref, where in zip(refs, (parity, 1 - parity)):
        cols = pl.ds(pl.multiple_of(where * half, half), half)
        made.append(copies(ref.at[place, :], target.at[pl.ds(at * CHUNK, CHUNK), cols]))
    return made


def fetch_thin(copies, refs, chunk, parity, target, at):
    place = pl.ds(pl.multiple_of(chunk * CHUNK, CHUNK), CHUNK)
    half = HEAD_DIM // 2
    made = []
    for which, pair in enumerate((refs[:2], refs[2:])):
        for ref, where in zip(pair, (parity, 1 - parity)):
            rows = pl.ds(pl.multiple_of(which * HEAD_DIM + where * half, half), half)
            made.append(copies(ref.at[:, place], target.at[rows, pl.ds(at * CHUNK, CHUNK)]))
    return made


def project_kernel(chunks, order, count, first, idx_ref, *refs):
    wide_refs, thin_refs, refs = refs[:2], refs[2:6], refs[6:]
    arrays, refs = refs[:count], refs[count:]
    before, refs = ((), refs) if first else (refs[:2], refs[2:])
    q_total, kv_total, lhs, wide, thin, sems = refs[:6]
    parity = idx_ref[len(chunks)]
    copies = Copies(sems)
    groups = []
    for at, parts in enumerate(chunks):
        groups.append(
            fetch_rows(copies, arrays, parts, lhs, at)
            + fetch_wide(copies, wide_refs, idx_ref[at], parity, wide, at)
            + fetch_thin(copies, thin_refs, idx_ref[at], parity, thin, at)
        )
    if not first:
        groups[0] += [copies(before[0], refs[6]), copies(before[1], refs[7])]
        earlier = refs[6:8]
    for number, (start, stop) in enumerate(order):
        for group in groups[start:stop]:
            for copy in group:
                copy.wait()
        span = slice(start * CHUNK, stop * CHUNK)
        q_part = jnp.dot(lhs[:, span], wide[span, :], preferred_element_type=F32)
        kv_part = lax.dot_general(lhs[:, span], thin[:, span], NT, preferred_element_type=F32)
        if number:
            q_total[...] += q_part
            kv_total[...] += kv_part
        elif first:
            q_total[...] = q_part
            kv_total[...] = kv_part
        else:
            q_total[...] = earlier[0][...] + q_part
            kv_total[...] = earlier[1][...] + kv_part


def chunk_scalars(places, parity):
    return jnp.stack(list(places) + [parity]).astype(jnp.int32)


def from_hbm(kernel, name, outs, scalars, operands, resident_operands, scratch, limit=58):
    return pl.pallas_call(
        kernel,
        in_specs=[SMEM] + [HBM] * len(operands) + [VMEM] * len(resident_operands),
        out_specs=[VMEM] * len(outs),
        out_shape=outs,
        scratch_shapes=scratch,
        compiler_params=params(limit),
        cost_estimate=cost(),
        name=name,
    )(scalars, *operands, *resident_operands)


def project(arrays, chunks, order, scalars, weights, before=()):
    count = len(chunks)
    totals = [(ALL_ROWS, QCOLS), (ALL_ROWS, KVCOLS)]
    scratch = [
        pltpu.VMEM((ALL_ROWS, count * CHUNK), BF16),
        pltpu.VMEM((count * CHUNK, QCOLS), BF16),
        pltpu.VMEM((KVCOLS, count * CHUNK), BF16),
        pltpu.SemaphoreType.DMA((sum(len(parts) + 6 for parts in chunks) + 2,)),
    ]
    if before:
        scratch += [pltpu.VMEM(shape, F32) for shape in totals]
    return from_hbm(
        functools.partial(project_kernel, chunks, order, len(arrays), not before),
        "project_rows",
        [jax.ShapeDtypeStruct(shape, F32) for shape in totals],
        scalars,
        (*weights, *arrays, *before),
        (),
        scratch,
    )


def all_angles(first, second):
    return jnp.concatenate([first[...]] * (ROWS // PROMPT) + [second[...]], axis=0)


def keys_kernel(parts, count, idx_ref, *refs):
    thin_refs, before = refs[:4], refs[4]
    arrays, refs = refs[5 : 5 + count], refs[5 + count :]
    kb_ref, vb_ref, cos_ref, sin_ref, scos_ref, ssin_ref, out_ref, steps_out, lhs, thin, total, sems = refs
    copies = Copies(sems)
    made = fetch_rows(copies, arrays, parts, lhs, 0)
    made += fetch_thin(copies, thin_refs, idx_ref[0], idx_ref[1], thin, 0)
    made.append(copies(before, total))
    for copy in made:
        copy.wait()
    rows = total[...] + lax.dot_general(lhs[...], thin[...], NT, preferred_element_type=F32)
    cosine, sine = all_angles(cos_ref, scos_ref), all_angles(sin_ref, ssin_ref)
    keys = turn(rows[:, :HEAD_DIM] + kb_ref[...], cosine, sine).astype(BF16)
    values = (rows[:, HEAD_DIM:] + vb_ref[...]).astype(BF16)
    out_ref[:, :HEAD_DIM] = keys[:ROWS]
    out_ref[:, HEAD_DIM:] = values[:ROWS]
    steps_out[:, :HEAD_DIM] = keys[ROWS:].astype(F32)
    steps_out[:, HEAD_DIM:] = values[ROWS:].astype(F32)


def last_keys(arrays, parts, scalars, weights, before, ending):
    return from_hbm(
        functools.partial(keys_kernel, parts, len(arrays)),
        "project_keys",
        [jax.ShapeDtypeStruct((ROWS, KVCOLS), BF16), jax.ShapeDtypeStruct((OWN_STEPS, KVCOLS), F32)],
        scalars,
        (*weights, before, *arrays),
        ending,
        [
            pltpu.VMEM((ALL_ROWS, CHUNK), BF16),
            pltpu.VMEM((KVCOLS, CHUNK), BF16),
            pltpu.VMEM((ALL_ROWS, KVCOLS), F32),
            pltpu.SemaphoreType.DMA((len(parts) + 5,)),
        ],
    )


def split_kernel(par_ref, prompts_ref, steps_ref, own_out, other_out, sems):
    copies = Copies(sems)
    for out, which in ((other_out, 1 - par_ref[0]), (own_out, par_ref[0])):
        rows = pl.ds(pl.multiple_of(which * ROWS, ROWS), ROWS)
        copies(prompts_ref.at[rows], out.at[pl.ds(0, ROWS)])
        rows = pl.ds(pl.multiple_of(which * HALF_REQ, HALF_REQ), HALF_REQ)
        for s in range(STEPS):
            copies(steps_ref.at[s, rows], out.at[pl.ds(ROWS + s * HALF_REQ, HALF_REQ)])
    for copy in copies.made:
        copy.wait()


def split_rows(scalars, prompts, steps):
    half = jax.ShapeDtypeStruct((ALL_ROWS, prompts.shape[1]), BF16)
    return pl.pallas_call(
        split_kernel,
        in_specs=[SMEM, HBM, HBM],
        out_specs=[VMEM] * 2,
        out_shape=[half] * 2,
        scratch_shapes=[pltpu.SemaphoreType.DMA((2 + 2 * STEPS,))],
        compiler_params=params(WHOLE_VMEM),
        cost_estimate=cost(),
        name="split_rows",
    )(scalars, prompts, steps)


def halves(parity, wide, own_out, other_out):
    half = wide.shape[1] // 2
    own_out[...] = jnp.where(parity == 0, wide[:, :half], wide[:, half:])
    other_out[...] = jnp.where(parity == 0, wide[:, half:], wide[:, :half])


def attend_prompts(q, kv_ref, out):
    row = lax.broadcasted_iota(jnp.int32, (PROMPT, PROMPT), 0)
    col = lax.broadcasted_iota(jnp.int32, (PROMPT, PROMPT), 1)
    causal = row >= col
    for prompt in range(ROWS // PROMPT):
        rows = slice(prompt * PROMPT, (prompt + 1) * PROMPT)
        keys, values = kv_ref[rows, :HEAD_DIM], kv_ref[rows, HEAD_DIM:]
        for head in range(GROUP):
            cols = slice(head * HEAD_DIM, (head + 1) * HEAD_DIM)
            scores = lax.dot_general(q[rows, cols], keys, NT, preferred_element_type=F32)
            scores = jnp.where(causal, scores, MASKED)
            powers = jnp.exp2((scores - jnp.max(scores, axis=1, keepdims=True)) * POWER)
            weights = (powers * (1.0 / jnp.sum(powers, axis=1, keepdims=True))).astype(BF16)
            out[rows, cols] = jnp.dot(weights, values, preferred_element_type=F32).astype(BF16)


def attend_group(group, q_ref, kv_ref, len_ref, cache, scores, mixed):
    rows = GROUP * STEPS * 8
    lanes = GROUP * MAXB

    def step_rows(s):
        return slice(s * HALF_REQ + group * 8, s * HALF_REQ + group * 8 + 8)

    queries = jnp.concatenate(
        [
            q_ref[step_rows(s), m * HEAD_DIM : (m + 1) * HEAD_DIM]
            for m in range(GROUP)
            for s in range(STEPS)
        ],
        axis=0,
    ).astype(BF16)
    row = lax.broadcasted_iota(jnp.int32, (rows, 128), 0) % 8
    lane = lax.broadcasted_iota(jnp.int32, (rows, 128), 1)
    lower = row < 4
    reach = len_ref[:, group * lanes : (group + 1) * lanes]
    reach = jnp.where(lower, reach[:, :128], reach[:, 128:])
    place = jnp.where(row % 4 == lane // MAXB, (lane % MAXB) * BLOCK, MAXB * BLOCK * 2) - reach
    top = jnp.full((rows, 128), MASKED, F32)
    for slot in range(BLOCK):
        part = jnp.dot(queries, cache[slot], preferred_element_type=F32)
        part = jnp.where(lower, part[:, :128], part[:, 128:])
        part = jnp.where(place < -slot, part, MASKED)
        scores[slot] = part
        top = jnp.maximum(top, part)
    fresh = jnp.concatenate([kv_ref[step_rows(s), :] for s in range(STEPS)], axis=0)
    fresh = jnp.concatenate([fresh, jnp.zeros((128 - 8 * STEPS, KVCOLS), F32)], axis=0).astype(BF16)
    newer = lax.dot_general(queries, fresh[:, :HEAD_DIM], NT, preferred_element_type=F32)
    at_step = (lax.broadcasted_iota(jnp.int32, (rows, 128), 0) // 8) % STEPS
    newer = jnp.where((row == lane % 8) & (lane // 8 <= at_step), newer, MASKED)
    peak = jnp.max(jnp.maximum(top, newer), axis=1, keepdims=True)
    newer = jnp.exp2((newer - peak) * POWER)
    weight_sum = newer
    for slot in range(BLOCK):
        powers = jnp.exp2((scores[slot] - peak) * POWER)
        scores[slot] = powers
        weight_sum = weight_sum + powers
    share = 1.0 / jnp.sum(weight_sum, axis=1, keepdims=True)
    result = jnp.dot(
        (newer * share).astype(BF16), fresh[:, HEAD_DIM:], preferred_element_type=F32
    )
    for start in range(0, BLOCK, 8):
        slots = range(start, start + 8)
        pieces = []
        for slot in slots:
            weight = scores[slot] * share
            pieces += [jnp.where(lower, weight, 0.0), jnp.where(lower, 0.0, weight)]
        weights = jnp.concatenate([piece.astype(BF16) for piece in pieces], axis=1)
        values = jnp.concatenate([cache[BLOCK + slot] for slot in slots], axis=1)
        result = result + lax.dot_general(weights, values, NT, preferred_element_type=F32)
    for m in range(GROUP):
        for s in range(STEPS):
            at = (m * STEPS + s) * 8
            mixed[s, group * 8 : (group + 1) * 8, m * HEAD_DIM : (m + 1) * HEAD_DIM] = result[at : at + 8]


def attention_kernel(parts, count, idx_ref, *refs):
    wide_refs, before, own_ref, other_ref, spread_ref = refs[:2], refs[2], refs[3], refs[4], refs[5]
    arrays, refs = refs[6 : 6 + count], refs[6 + count :]
    kv_ref, kv_steps_ref, len_ref, qbias_ref, cos_ref, sin_ref, scos_ref, ssin_ref = refs[:8]
    prompts_own, prompts_other, steps_own, steps_other, q_steps = refs[8:13]
    lhs, wide, total, q, prompts, scores, mixed, steps, cache, spread, sems = refs[13:]
    parity = idx_ref[1]
    half_dim = HEAD_DIM // 2
    copies = Copies(sems)
    made = fetch_rows(copies, arrays, parts, lhs, 0)
    made += fetch_wide(copies, wide_refs, idx_ref[0], parity, wide, 0)
    total_copy = copies(before, total)
    loads = []
    for group in range(HALF_REQ // 8):
        for ref, where in ((own_ref, parity), (other_ref, 1 - parity)):
            dims = pl.ds(pl.multiple_of(where * half_dim, half_dim), half_dim)
            loads.append(copies(ref.at[group], cache.at[group, :, dims]))
    spread_copy = copies(spread_ref, spread)
    for copy in made:
        copy.wait()
    rows = jnp.dot(lhs[...], wide[...], preferred_element_type=F32)
    total_copy.wait()
    total[...] += rows
    cosine, sine = all_angles(cos_ref, scos_ref), all_angles(sin_ref, ssin_ref)
    for head in range(GROUP):
        cols = slice(head * HEAD_DIM, (head + 1) * HEAD_DIM)
        rows = turn(total[:, cols] + qbias_ref[:, cols], cosine, sine).astype(BF16)
        q[:, cols] = rows[:ROWS]
        q_steps[:, cols] = rows[ROWS:].astype(F32)
    attend_prompts(q, kv_ref, prompts)
    halves(parity, prompts, prompts_own, prompts_other)
    for group in range(HALF_REQ // 8):
        for copy in loads[2 * group : 2 * group + 2]:
            copy.wait()
        attend_group(group, q_steps, kv_steps_ref, len_ref, cache.at[group], scores.at[group % 2], mixed)
    spread_copy.wait()
    rounded = mixed[...].reshape(OWN_STEPS, QCOLS).astype(BF16)
    steps[...] = jnp.dot(rounded, spread[...], preferred_element_type=F32).astype(BF16)
    halves(parity, steps, steps_own, steps_other)


def attention(arrays, parts, scalars, weights, before, caches, spread, operands):
    groups = HALF_REQ // 8
    split = (groups, 2 * BLOCK, HEAD_DIM // 2, GROUP * MAXB)
    prompts = jax.ShapeDtypeStruct((ROWS, QCOLS // 2), BF16)
    steps = jax.ShapeDtypeStruct((OWN_STEPS, QCOLS // 2), BF16)
    q_steps = jax.ShapeDtypeStruct((OWN_STEPS, QCOLS), F32)
    return from_hbm(
        functools.partial(attention_kernel, parts, len(arrays)),
        "attention",
        [prompts, prompts, steps, steps, q_steps],
        scalars,
        (*weights, before, *(cache.reshape(split) for cache in caches), spread, *arrays),
        operands,
        [
            pltpu.VMEM((ALL_ROWS, CHUNK), BF16),
            pltpu.VMEM((CHUNK, QCOLS), BF16),
            pltpu.VMEM((ALL_ROWS, QCOLS), F32),
            pltpu.VMEM((ROWS, QCOLS), BF16),
            pltpu.VMEM((ROWS, QCOLS), BF16),
            pltpu.VMEM((2, BLOCK, GROUP * STEPS * 8, 128), F32),
            pltpu.VMEM((STEPS, HALF_REQ, QCOLS), F32),
            pltpu.VMEM((OWN_STEPS, QCOLS), BF16),
            pltpu.VMEM((groups, 2 * BLOCK, HEAD_DIM, GROUP * MAXB), BF16),
            pltpu.VMEM((QCOLS, QCOLS), BF16),
            pltpu.SemaphoreType.DMA((len(parts) + 4 + 2 * groups,)),
        ],
    )


def arrived_kernel(
    par_ref, prompts_own_ref, prompts_other_ref, own_ref, other_ref,
    q_ref, kv_ref, q_other_ref, kv_other_ref, spread_ref, *refs,
):
    arrived, prompts_out, out_ref = refs[:4], refs[4], refs[5]
    for at, which in ((0, 0), (1, 1)):
        prompts_out[at * ROWS : (at + 1) * ROWS] = jnp.where(
            par_ref[0] == which, prompts_own_ref[...], prompts_other_ref[...]
        )
    own_cols = QCOLS // 2
    rows = 4 * GROUP * 8

    def by_arrival(shape, axis, size):
        which = lax.broadcasted_iota(jnp.int32, shape, axis) // size
        picked = jnp.zeros(shape, jnp.int32)
        for at in range(4):
            picked = jnp.where(which == at, requests[at], picked)
        return picked

    requests = [arrived[at][PROMPT : PROMPT + 16, :128].astype(jnp.int32)[:1, :1] for at in range(4)]
    shape = (32, OWN_STEPS)
    step = lax.broadcasted_iota(jnp.int32, shape, 0) % 8
    col = lax.broadcasted_iota(jnp.int32, shape, 1)
    parity = par_ref[0]

    def picked_rows(half, ref):
        request = col % HALF_REQ + half * HALF_REQ
        pick = (col // HALF_REQ == step) & (request == by_arrival(shape, 0, 8))
        pick = jnp.where(pick, 1.0, 0.0).astype(BF16)
        return jnp.dot(pick, ref[...].astype(BF16), preferred_element_type=F32)

    own = picked_rows(parity, q_ref) + picked_rows(1 - parity, q_other_ref)
    fresh = picked_rows(parity, kv_ref) + picked_rows(1 - parity, kv_other_ref)
    queries = jnp.concatenate(
        [
            own[at * 8 : (at + 1) * 8, m * HEAD_DIM : (m + 1) * HEAD_DIM]
            for at in range(4)
            for m in range(GROUP)
        ],
        axis=0,
    ).astype(BF16)
    fresh = jnp.concatenate([fresh, jnp.zeros((96, KVCOLS), F32)], axis=0).astype(BF16)
    part = GROUP * 8
    scores = jnp.concatenate(
        [
            lax.dot_general(
                queries[at * part : (at + 1) * part],
                arrived[at][:PROMPT, :HEAD_DIM],
                NT,
                preferred_element_type=F32,
            )
            for at in range(4)
        ],
        axis=0,
    )
    newer = lax.dot_general(queries, fresh[:, :HEAD_DIM], NT, preferred_element_type=F32)
    nrow = lax.broadcasted_iota(jnp.int32, (rows, 128), 0)
    nlane = lax.broadcasted_iota(jnp.int32, (rows, 128), 1)
    seen = (nlane // 8 == nrow // part) & (nlane % 8 < STEPS) & (nlane % 8 <= nrow % 8)
    newer = jnp.where(seen, newer, MASKED)
    peak = jnp.maximum(jnp.max(scores, axis=1, keepdims=True), jnp.max(newer, axis=1, keepdims=True))
    scores = jnp.exp2((scores - peak) * POWER)
    newer = jnp.exp2((newer - peak) * POWER)
    share = 1.0 / (jnp.sum(scores, axis=1, keepdims=True) + jnp.sum(newer, axis=1, keepdims=True))
    scores = (scores * share).astype(BF16)
    result = jnp.concatenate(
        [
            jnp.dot(
                scores[at * part : (at + 1) * part],
                arrived[at][:PROMPT, HEAD_DIM:],
                preferred_element_type=F32,
            )
            for at in range(4)
        ],
        axis=0,
    )
    result = result + jnp.dot(
        (newer * share).astype(BF16), fresh[:, HEAD_DIM:], preferred_element_type=F32
    )
    wide = jnp.concatenate(
        [
            jnp.concatenate(
                [result[at * part + m * 8 : at * part + (m + 1) * 8] for m in range(GROUP)], axis=1
            )
            for at in range(4)
        ],
        axis=0,
    )
    spread = spread_ref[:, pl.ds(pl.multiple_of(par_ref[0] * own_cols, own_cols), own_cols)]
    fixed = jnp.dot(wide.astype(BF16), spread, preferred_element_type=F32).astype(BF16)
    shape = (STEP_ROWS, 32)
    line = lax.broadcasted_iota(jnp.int32, shape, 0)
    step = lax.broadcasted_iota(jnp.int32, shape, 1) % 8
    back = (line == step * REQ_DEV + by_arrival(shape, 1, 8)) & (step < STEPS)
    placed = jnp.dot(jnp.where(back, 1.0, 0.0).astype(BF16), fixed, preferred_element_type=F32)
    line = lax.broadcasted_iota(jnp.int32, (STEP_ROWS, own_cols), 0) % REQ_DEV
    here = line == requests[0]
    for at in range(1, 4):
        here = here | (line == requests[at])
    mine, theirs = own_ref[...], other_ref[...]
    low = jnp.where(par_ref[0] == 0, mine, theirs)
    high = jnp.where(par_ref[0] == 0, theirs, mine)
    base = jnp.concatenate(
        [
            part[s * HALF_REQ : (s + 1) * HALF_REQ].astype(F32)
            for s in range(STEPS)
            for part in (low, high)
        ],
        axis=0,
    )
    out_ref[...] = jnp.where(here, placed, base).astype(BF16)


def arrived_attention(parity, halves_got, steps, spread, arrived):
    return resident(
        arrived_kernel,
        "arrived_attention",
        [
            jax.ShapeDtypeStruct((2 * ROWS, QCOLS // 2), BF16),
            jax.ShapeDtypeStruct((STEP_ROWS, QCOLS // 2), BF16),
        ],
        parity,
        (*halves_got, *steps, spread, *arrived),
        WHOLE_VMEM,
        cost(),
    )


def body(
    prompt_tokens,
    norm_gain,
    q_weight,
    k_weight,
    v_weight,
    q_bias,
    k_bias,
    v_bias,
    decode_tokens,
    k_cache,
    v_cache,
    block_table,
    context_len,
    prompt_dest,
):
    tp_rank = lax.axis_index("tp")
    dp_rank = lax.axis_index("dp")
    parity = tp_rank % 2
    chip = tp_rank // 2
    y_at, x_at = chip // 2, chip % 2
    lengths = context_len[0]
    parity_ref = parity[None].astype(jnp.int32)
    barrier = lax.optimization_barrier

    def joined(own, other, axis):
        return jnp.where(
            parity == 0,
            jnp.concatenate([own, other], axis=axis),
            jnp.concatenate([other, own], axis=axis),
        )

    mine, theirs = split_rows(parity_ref, prompt_tokens[0], decode_tokens[0])
    held = joined(mine, send(theirs, CORE), 1)
    wide = held.astype(F32)
    squares = jnp.sum(wide * wide, axis=1)
    squares = squares + send(squares, XSWAP)
    squares = squares + sum(
        send(squares, [(i, (i + 4 * dy) % 16) for i in range(16)]) for dy in range(1, 4)
    )
    rstd = lax.rsqrt(squares * (1.0 / FEATURES) + NORM_EPSILON)[:, None]
    chip_cols = lambda array, width: lax.dynamic_slice_in_dim(array, chip * width, width, 0)[None, :]
    held = (wide * rstd * chip_cols(norm_gain, CHUNK)).astype(BF16)

    k_w, v_w, squares_done = barrier((k_weight.T, v_weight.T, squares))
    k_other, v_other = send(k_w, CORE), send(v_w, CORE)

    held, q_w, k_other, v_other = barrier((held, q_weight, k_other, v_other))
    side, up, down = send(held, XSWAP), send(held, YUP), send(held, YDOWN)
    wide_weights = (q_w, send(q_w, CORE))
    thin_weights = (k_w, k_other, v_w, v_other)
    weights = wide_weights + thin_weights

    table = block_table[0]
    turned = lambda cache: jnp.transpose(cache[0], (1, 2, 0)).reshape(BLOCK * HEAD_DIM // 2, NBLK)
    k_flat, v_flat = turned(k_cache), turned(v_cache)
    table, held = barrier((table.reshape(1, 2 * PAIRS), held))
    cache_theirs = arrange(1 - parity_ref, table, k_flat, v_flat)

    (cache_theirs, zero, lengths, q_bias, k_bias, v_bias) = barrier(
        (cache_theirs, jnp.int32(0), lengths, q_bias, k_bias, v_bias)
    )
    spread_row = lax.broadcasted_iota(jnp.int32, (QCOLS, QCOLS), 0) + zero
    spread_col = lax.broadcasted_iota(jnp.int32, (QCOLS, QCOLS), 1)
    spread = spread_col == (spread_row % HEAD_DIM) * GROUP + spread_row // HEAD_DIM
    spread = spread.astype(BF16)
    own_len = lax.dynamic_slice_in_dim(lengths, parity * HALF_REQ, HALF_REQ, 0)
    reach = jnp.repeat(own_len, MAXB)[None, :]

    exponent = jnp.arange(HEAD_DIM // 2, dtype=F32) * (2.0 / HEAD_DIM)
    frequency = jnp.power(F32(ROPE_BASE), -exponent)

    def angles(positions):
        angle = positions.astype(F32)[:, None] * frequency
        cosine, sine = jnp.cos(angle), jnp.sin(angle)
        return jnp.concatenate([cosine, cosine], axis=1), jnp.concatenate([-sine, sine], axis=1)

    prompt_angles = angles(jnp.arange(PROMPT, dtype=jnp.int32) + zero)
    step_angles = angles(
        (own_len[None, :] + jnp.arange(STEPS, dtype=jnp.int32)[:, None]).reshape(-1)
    )
    q_offset = chip_cols(q_bias, QCOLS)
    kv_offsets = (chip_cols(k_bias, HEAD_DIM), chip_cols(v_bias, HEAD_DIM))
    place = lambda dy, dx: ((y_at + dy) % 4) * 2 + (x_at + dx) % 2
    early = chunk_scalars([place(0, 0), place(0, 1), place(3, 0), place(1, 0)], parity)
    late = chunk_scalars([place(2, 0), place(3, 1), place(1, 1)], parity)
    final = chunk_scalars([place(2, 1)], parity)

    scalars = jnp.concatenate([prompt_dest[0], parity[None], dp_rank[None]]).astype(jnp.int32)
    (side, up, down, cache_theirs, reach, early, late, final, spread, offsets, both_angles, scalars) = barrier(
        (
            (side, up, down, cache_theirs, reach, early, late, final, spread)
            + ((q_offset, *kv_offsets), (*prompt_angles, *step_angles), scalars)
        )
    )
    side_up, far, side_down = send(side, YUP), send(down, YDOWN), send(down, XSWAP)
    cache_other = send(cache_theirs, CORE)
    table, side_sent = barrier((table, side))
    cache_own = arrange(parity_ref, table, k_flat, v_flat)
    totals = project(
        (held, side, up, down),
        tuple(((source, 0, ALL_ROWS),) for source in range(4)),
        ((0, 1), (1, 2), (2, 4)),
        early,
        weights,
    )

    side_up, far, side_down, totals, cache_own = barrier(
        (side_up, far, side_down, totals, cache_own)
    )
    cut_a, cut_b = 208, 416
    sent = take_parts(
        parity_ref, (side_up, side_down, far), ((0, cut_a), (cut_a, cut_b), (cut_b, ALL_ROWS))
    )
    sent, side_up, side_down, far = barrier((sent, side_up, side_down, far))
    last = (send(sent[0], YUP), send(sent[1], YDOWN), send(sent[2], XSWAP))
    q_total, kv_total = project(
        (far, side_up, side_down),
        tuple(((source, 0, ALL_ROWS),) for source in range(3)),
        ((0, 3),),
        late,
        weights,
        before=totals,
    )
    parts = ((0, 0, cut_a), (1, 0, cut_b - cut_a), (2, 0, ALL_ROWS - cut_b))
    kv, kv_steps = last_keys(
        last, parts, final, thin_weights, kv_total, (*offsets[1:], *both_angles)
    )

    kv_steps_other = send(kv_steps, CORE)
    blocks = handover(scalars, kv, send(kv, CORE))
    blocks, last, q_total, kv_steps_other = barrier((blocks, last, q_total, kv_steps_other))
    arrived = []
    for shift, block in enumerate(blocks):
        pairs = [(g * 4 + a, (1 - g) * 4 + (a + shift) % 4) for g in range(2) for a in range(4)]
        arrived.append(lax.ppermute(block, ("grp", "dp"), pairs))

    prefill_own, prefill_sent, decode_own, decode_sent, q_steps = attention(
        last,
        parts,
        final,
        wide_weights,
        q_total,
        (cache_own, cache_other),
        spread,
        (kv, kv_steps, reach, offsets[0], *both_angles),
    )
    arrived, prefill_sent, decode_sent, q_steps_sent = lax.optimization_barrier(
        (arrived, prefill_sent, decode_sent, q_steps)
    )
    steps = (q_steps, kv_steps, send(q_steps_sent, CORE), kv_steps_other)
    prefill_out, decode_out = arrived_attention(
        parity_ref,
        (prefill_own, send(prefill_sent, CORE), decode_own, send(decode_sent, CORE)),
        steps,
        spread,
        arrived,
    )
    prefill_out = prefill_out[None]
    return (prefill_out, decode_out.reshape(1, STEPS, REQ_DEV, -1))


def solution(mesh):
    placed = (
        P("grp", "dp", "tp"),
        P(),
        P(None, "tp"),
        P(None, "tp"),
        P(None, "tp"),
        P(),
        P(),
        P(),
        P("grp", None, "dp", "tp"),
        P("grp", "dp", None, "tp"),
        P("grp", "dp", None, "tp"),
        P("grp", "dp", None),
        P("grp", "dp"),
        P("grp", "dp"),
    )
    return jax.shard_map(
        body,
        mesh=mesh,
        in_specs=placed,
        out_specs=(P("grp", "dp", "tp"), P("grp", None, "dp", "tp")),
        check_vma=False,
    )
```

```python
import functools
import math

import jax
import jax.numpy as jnp
from jax import lax
from jax.experimental import pallas as pl
from jax.experimental.pallas import tpu as pltpu
from jax.sharding import PartitionSpec as P

HEAD_DIM = 128
GROUP = 8
BLOCK = 16
MAXB = 32
PROMPT = 256
REQ_DEV = 64
STEPS = 3
ROPE_BASE = 1000000.0
NORM_EPSILON = 1e-06
MASKED = -1e30
SCALE = 1.0 / math.sqrt(HEAD_DIM)
FEATURES = 8192
CHUNK = 1024
ROWS = 512
STEP_ROWS = STEPS * REQ_DEV
OWN_STEPS = STEP_ROWS // 2
ALL_ROWS = ROWS + OWN_STEPS
QCOLS = GROUP * HEAD_DIM
KVCOLS = 2 * HEAD_DIM
COLS = QCOLS + KVCOLS
HALF_REQ = REQ_DEV // 2
NBLK = 2048
PAIRS = HALF_REQ * MAXB
POWER = SCALE * math.log2(math.e)
WHOLE_VMEM = 58
LAST_AT = 7
CORE_AT = 8

CORE = [(i, i ^ 1) for i in range(16)]
XSWAP = [(i, i ^ 2) for i in range(16)]
YFAR = [(i, i ^ 8) for i in range(16)]
YUP = [(i, (i + 4) % 16) for i in range(16)]
YDOWN = [(i, (i + 12) % 16) for i in range(16)]

NT = (((1,), (1,)), ((), ()))
F32 = jnp.float32
BF16 = jnp.bfloat16


def send(array, pairs):
    return lax.ppermute(array, "tp", pairs)


def cost(*_):
    return pl.CostEstimate(flops=1, bytes_accessed=1, transcendentals=0)


def params(mebibytes):
    return pltpu.CompilerParams(vmem_limit_bytes=mebibytes * 1024 * 1024)


VMEM = pl.BlockSpec(memory_space=pltpu.VMEM)
SMEM = pl.BlockSpec(memory_space=pltpu.SMEM)


def resident(kernel, name, outs, scalars, operands, mebibytes, estimate, scratch=()):
    return pl.pallas_call(
        kernel,
        in_specs=[SMEM] + [VMEM] * len(operands),
        out_specs=[VMEM] * len(outs),
        out_shape=outs,
        scratch_shapes=list(scratch),
        compiler_params=params(mebibytes),
        cost_estimate=estimate,
        name=name,
    )(scalars, *operands)


HBM = pl.BlockSpec(memory_space=pltpu.HBM)


def arrange_kernel(which_ref, table_ref, k_ref, v_ref, out_ref, pick):
    tile = pick.shape[2]
    half = k_ref.shape[0]
    block = lax.broadcasted_iota(jnp.int32, (NBLK, tile), 0)
    for at in range(PAIRS // tile):
        lanes = pl.ds(pl.multiple_of(which_ref[0] * PAIRS + at * tile, tile), tile)
        slot = at % 2
        pick[slot] = jnp.where(block == table_ref[:, lanes], 1.0, 0.0).astype(BF16)
        out_ref[at, :half] = jnp.dot(k_ref[...], pick[slot], preferred_element_type=F32).astype(BF16)
        out_ref[at, half:] = jnp.dot(v_ref[...], pick[slot], preferred_element_type=F32).astype(BF16)


def arrange(which, table, k_flat, v_flat):
    rows = k_flat.shape[0]
    return resident(
        arrange_kernel,
        "arrange_cache",
        [jax.ShapeDtypeStruct((PAIRS // 256, 2 * rows, 256), BF16)],
        which,
        (table, k_flat, v_flat),
        WHOLE_VMEM,
        cost(),
        [pltpu.VMEM((2, NBLK, 256), BF16)],
    )[0]


def parts_kernel(cuts, _, *refs):
    for (start, stop), source, out in zip(cuts, refs[:3], refs[3:]):
        out[...] = source[start:stop]


def take_parts(scalars, arrays, cuts):
    outs = [jax.ShapeDtypeStruct((stop - start, CHUNK), BF16) for start, stop in cuts]
    return resident(functools.partial(parts_kernel, cuts), "take_parts", outs, scalars, arrays, 8, cost())


def handover_kernel(scalar_ref, own_ref, other_ref, *outs):
    parity, rank = scalar_ref[CORE_AT], scalar_ref[CORE_AT + 1]
    for shift in range(4):
        target = (rank + shift) % 4
        at = jnp.int32(0)
        request = jnp.int32(0)
        for prompt in range(4):
            chosen = scalar_ref[CORE_AT + 2 + prompt] // REQ_DEV == target
            at = jnp.where(chosen, prompt, at)
            request = jnp.where(chosen, scalar_ref[CORE_AT + 2 + prompt] % REQ_DEV, request)
        rows = pl.ds(pl.multiple_of((at % 2) * PROMPT, PROMPT), PROMPT)
        outs[shift][:PROMPT] = jnp.where(at // 2 == parity, own_ref[rows, :], other_ref[rows, :])
        outs[shift][PROMPT:] = jnp.full((16, 2 * HEAD_DIM), request.astype(F32), F32).astype(BF16)


def handover(scalars, own, other):
    shape = jax.ShapeDtypeStruct((PROMPT + 16, KVCOLS), BF16)
    return resident(
        handover_kernel, "sort_prompts", [shape] * 4, scalars, (own, other), WHOLE_VMEM, cost()
    )


def turn(rows, cosine, sine):
    return rows * cosine + pltpu.roll(rows, HEAD_DIM // 2, 1) * sine


class Copies:
    def __init__(self, sems):
        self.sems, self.made = sems, []

    def __call__(self, source, target):
        copy = pltpu.make_async_copy(source, target, self.sems.at[len(self.made)])
        copy.start()
        self.made.append(copy)
        return copy


def fetch_rows(copies, arrays, parts, lhs, at):
    cols = pl.ds(at * CHUNK, CHUNK)
    row, made = 0, []
    for source, start, stop in parts:
        target = lhs.at[pl.ds(row, stop - start), cols]
        made.append(copies(arrays[source].at[pl.ds(start, stop - start)], target))
        row += stop - start
    return made


def fetch_wide(copies, refs, chunk, parity, target, at):
    place = pl.ds(pl.multiple_of(chunk * CHUNK, CHUNK), CHUNK)
    half = QCOLS // 2
    made = []
    for ref, where in zip(refs, (parity, 1 - parity)):
        cols = pl.ds(pl.multiple_of(where * half, half), half)
        made.append(copies(ref.at[place, :], target.at[pl.ds(at * CHUNK, CHUNK), cols]))
    return made


def fetch_thin(copies, refs, chunk, parity, target, at):
    place = pl.ds(pl.multiple_of(chunk * CHUNK, CHUNK), CHUNK)
    half = HEAD_DIM // 2
    made = []
    for which, pair in enumerate((refs[:2], refs[2:])):
        for ref, where in zip(pair, (parity, 1 - parity)):
            rows = pl.ds(pl.multiple_of(which * HEAD_DIM + where * half, half), half)
            made.append(copies(ref.at[:, place], target.at[rows, pl.ds(at * CHUNK, CHUNK)]))
    return made


def project_kernel(chunks, order, base, count, first, idx_ref, *refs):
    wide_refs, thin_refs, refs = refs[:2], refs[2:6], refs[6:]
    arrays, refs = refs[:count], refs[count:]
    before, refs = ((), refs) if first else (refs[:2], refs[2:])
    q_total, kv_total, lhs, wide, thin, sems = refs[:6]
    parity = idx_ref[CORE_AT]
    copies = Copies(sems)
    groups = []
    for at, parts in enumerate(chunks):
        groups.append(
            fetch_rows(copies, arrays, parts, lhs, at)
            + fetch_wide(copies, wide_refs, idx_ref[base + at], parity, wide, at)
            + fetch_thin(copies, thin_refs, idx_ref[base + at], parity, thin, at)
        )
    if not first:
        groups[0] += [copies(before[0], refs[6]), copies(before[1], refs[7])]
        earlier = refs[6:8]
    for number, (start, stop) in enumerate(order):
        for group in groups[start:stop]:
            for copy in group:
                copy.wait()
        span = slice(start * CHUNK, stop * CHUNK)
        q_part = jnp.dot(lhs[:, span], wide[span, :], preferred_element_type=F32)
        kv_part = lax.dot_general(lhs[:, span], thin[:, span], NT, preferred_element_type=F32)
        if number:
            q_total[...] += q_part
            kv_total[...] += kv_part
        elif first:
            q_total[...] = q_part
            kv_total[...] = kv_part
        else:
            q_total[...] = earlier[0][...] + q_part
            kv_total[...] = earlier[1][...] + kv_part


def from_hbm(kernel, name, outs, scalars, operands, resident_operands, scratch, limit=58):
    return pl.pallas_call(
        kernel,
        in_specs=[SMEM] + [HBM] * len(operands) + [VMEM] * len(resident_operands),
        out_specs=[VMEM] * len(outs),
        out_shape=outs,
        scratch_shapes=scratch,
        compiler_params=params(limit),
        cost_estimate=cost(),
        name=name,
    )(scalars, *operands, *resident_operands)


def project(arrays, chunks, order, base, scalars, weights, before=()):
    count = len(chunks)
    totals = [(ALL_ROWS, QCOLS), (ALL_ROWS, KVCOLS)]
    scratch = [
        pltpu.VMEM((ALL_ROWS, count * CHUNK), BF16),
        pltpu.VMEM((count * CHUNK, QCOLS), BF16),
        pltpu.VMEM((KVCOLS, count * CHUNK), BF16),
        pltpu.SemaphoreType.DMA((sum(len(parts) + 6 for parts in chunks) + 2,)),
    ]
    if before:
        scratch += [pltpu.VMEM(shape, F32) for shape in totals]
    return from_hbm(
        functools.partial(project_kernel, chunks, order, base, len(arrays), not before),
        "project_rows",
        [jax.ShapeDtypeStruct(shape, F32) for shape in totals],
        scalars,
        (*weights, *arrays, *before),
        (),
        scratch,
    )


def all_angles(first, second):
    return jnp.concatenate([first[...]] * (ROWS // PROMPT) + [second[...]], axis=0)


def keys_kernel(parts, count, idx_ref, *refs):
    thin_refs, before = refs[:4], refs[4]
    arrays, refs = refs[5 : 5 + count], refs[5 + count :]
    kb_ref, vb_ref, cos_ref, sin_ref, scos_ref, ssin_ref, out_ref, steps_out, lhs, thin, total, sems = refs
    copies = Copies(sems)
    made = fetch_rows(copies, arrays, parts, lhs, 0)
    made += fetch_thin(copies, thin_refs, idx_ref[LAST_AT], idx_ref[CORE_AT], thin, 0)
    made.append(copies(before, total))
    for copy in made:
        copy.wait()
    rows = total[...] + lax.dot_general(lhs[...], thin[...], NT, preferred_element_type=F32)
    cosine, sine = all_angles(cos_ref, scos_ref), all_angles(sin_ref, ssin_ref)
    keys = turn(rows[:, :HEAD_DIM] + kb_ref[...], cosine, sine).astype(BF16)
    values = (rows[:, HEAD_DIM:] + vb_ref[...]).astype(BF16)
    out_ref[:, :HEAD_DIM] = keys[:ROWS]
    out_ref[:, HEAD_DIM:] = values[:ROWS]
    steps_out[:, :HEAD_DIM] = keys[ROWS:].astype(F32)
    steps_out[:, HEAD_DIM:] = values[ROWS:].astype(F32)


def last_keys(arrays, parts, scalars, weights, before, ending):
    return from_hbm(
        functools.partial(keys_kernel, parts, len(arrays)),
        "project_keys",
        [jax.ShapeDtypeStruct((ROWS, KVCOLS), BF16), jax.ShapeDtypeStruct((OWN_STEPS, KVCOLS), F32)],
        scalars,
        (*weights, before, *arrays),
        ending,
        [
            pltpu.VMEM((ALL_ROWS, CHUNK), BF16),
            pltpu.VMEM((KVCOLS, CHUNK), BF16),
            pltpu.VMEM((ALL_ROWS, KVCOLS), F32),
            pltpu.SemaphoreType.DMA((len(parts) + 5,)),
        ],
    )


def split_kernel(par_ref, prompts_ref, steps_ref, own_out, other_out, sems):
    copies = Copies(sems)
    for out, which in ((other_out, 1 - par_ref[0]), (own_out, par_ref[0])):
        rows = pl.ds(pl.multiple_of(which * ROWS, ROWS), ROWS)
        copies(prompts_ref.at[rows], out.at[pl.ds(0, ROWS)])
        rows = pl.ds(pl.multiple_of(which * HALF_REQ, HALF_REQ), HALF_REQ)
        for s in range(STEPS):
            copies(steps_ref.at[s, rows], out.at[pl.ds(ROWS + s * HALF_REQ, HALF_REQ)])
    for copy in copies.made:
        copy.wait()


def split_rows(scalars, prompts, steps):
    half = jax.ShapeDtypeStruct((ALL_ROWS, prompts.shape[1]), BF16)
    return pl.pallas_call(
        split_kernel,
        in_specs=[SMEM, HBM, HBM],
        out_specs=[VMEM] * 2,
        out_shape=[half] * 2,
        scratch_shapes=[pltpu.SemaphoreType.DMA((2 + 2 * STEPS,))],
        compiler_params=params(8),
        cost_estimate=cost(),
        name="split_rows",
    )(scalars, prompts, steps)


def join_kernel(par_ref, own_ref, other_ref, out_ref):
    half = own_ref.shape[1]
    own, other = own_ref[...], other_ref[...]
    out_ref[:, :half] = jnp.where(par_ref[0] == 0, own, other)
    out_ref[:, half:] = jnp.where(par_ref[0] == 0, other, own)


def join_features(parity, own, other):
    out = jax.ShapeDtypeStruct((own.shape[0], 2 * own.shape[1]), BF16)
    return resident(join_kernel, "join_features", [out], parity, (own, other), 8, cost())[0]


def halves(parity, wide, own_out, other_out):
    half = wide.shape[1] // 2
    own_out[...] = jnp.where(parity == 0, wide[:, :half], wide[:, half:])
    other_out[...] = jnp.where(parity == 0, wide[:, half:], wide[:, :half])


def attend_prompts(q, kv_ref, out):
    row = lax.broadcasted_iota(jnp.int32, (PROMPT, PROMPT), 0)
    col = lax.broadcasted_iota(jnp.int32, (PROMPT, PROMPT), 1)
    causal = row >= col
    for prompt in range(ROWS // PROMPT):
        rows = slice(prompt * PROMPT, (prompt + 1) * PROMPT)
        keys, values = kv_ref[rows, :HEAD_DIM], kv_ref[rows, HEAD_DIM:]
        for head in range(GROUP):
            cols = slice(head * HEAD_DIM, (head + 1) * HEAD_DIM)
            scores = lax.dot_general(q[rows, cols], keys, NT, preferred_element_type=F32)
            scores = jnp.where(causal, scores, MASKED)
            powers = jnp.exp2((scores - jnp.max(scores, axis=1, keepdims=True)) * POWER)
            weights = (powers * (1.0 / jnp.sum(powers, axis=1, keepdims=True))).astype(BF16)
            out[rows, cols] = jnp.dot(weights, values, preferred_element_type=F32).astype(BF16)


def attend_group(group, q_ref, kv_ref, len_ref, cache, scores, mixed):
    rows = GROUP * STEPS * 8
    lanes = GROUP * MAXB

    def step_rows(s):
        return slice(s * HALF_REQ + group * 8, s * HALF_REQ + group * 8 + 8)

    queries = jnp.concatenate(
        [
            q_ref[step_rows(s), m * HEAD_DIM : (m + 1) * HEAD_DIM]
            for m in range(GROUP)
            for s in range(STEPS)
        ],
        axis=0,
    ).astype(BF16)
    row = lax.broadcasted_iota(jnp.int32, (rows, 128), 0) % 8
    lane = lax.broadcasted_iota(jnp.int32, (rows, 128), 1)
    lower = row < 4
    reach = len_ref[:, group * lanes : (group + 1) * lanes]
    reach = jnp.where(lower, reach[:, :128], reach[:, 128:])
    place = jnp.where(row % 4 == lane // MAXB, (lane % MAXB) * BLOCK, MAXB * BLOCK * 2) - reach
    top = jnp.full((rows, 128), MASKED, F32)
    for slot in range(BLOCK):
        part = jnp.dot(queries, cache[slot], preferred_element_type=F32)
        part = jnp.where(lower, part[:, :128], part[:, 128:])
        part = jnp.where(place < -slot, part, MASKED)
        scores[slot] = part
        top = jnp.maximum(top, part)
    fresh = jnp.concatenate([kv_ref[step_rows(s), :] for s in range(STEPS)], axis=0)
    fresh = jnp.concatenate([fresh, jnp.zeros((128 - 8 * STEPS, KVCOLS), F32)], axis=0).astype(BF16)
    newer = lax.dot_general(queries, fresh[:, :HEAD_DIM], NT, preferred_element_type=F32)
    at_step = (lax.broadcasted_iota(jnp.int32, (rows, 128), 0) // 8) % STEPS
    newer = jnp.where((row == lane % 8) & (lane // 8 <= at_step), newer, MASKED)
    peak = jnp.max(jnp.maximum(top, newer), axis=1, keepdims=True)
    newer = jnp.exp2((newer - peak) * POWER)
    weight_sum = newer
    for slot in range(BLOCK):
        powers = jnp.exp2((scores[slot] - peak) * POWER)
        scores[slot] = powers
        weight_sum = weight_sum + powers
    share = 1.0 / jnp.sum(weight_sum, axis=1, keepdims=True)
    result = jnp.dot(
        (newer * share).astype(BF16), fresh[:, HEAD_DIM:], preferred_element_type=F32
    )
    for start in range(0, BLOCK, 8):
        slots = range(start, start + 8)
        pieces = []
        for slot in slots:
            weight = scores[slot] * share
            pieces += [jnp.where(lower, weight, 0.0), jnp.where(lower, 0.0, weight)]
        weights = jnp.concatenate([piece.astype(BF16) for piece in pieces], axis=1)
        values = jnp.concatenate([cache[BLOCK + slot] for slot in slots], axis=1)
        result = result + lax.dot_general(weights, values, NT, preferred_element_type=F32)
    for m in range(GROUP):
        for s in range(STEPS):
            at = (m * STEPS + s) * 8
            mixed[s, group * 8 : (group + 1) * 8, m * HEAD_DIM : (m + 1) * HEAD_DIM] = result[at : at + 8]


def attention_kernel(parts, count, idx_ref, *refs):
    wide_refs, before, own_ref, other_ref, spread_ref = refs[:2], refs[2], refs[3], refs[4], refs[5]
    arrays, refs = refs[6 : 6 + count], refs[6 + count :]
    kv_ref, kv_steps_ref, len_ref, qbias_ref, cos_ref, sin_ref, scos_ref, ssin_ref = refs[:8]
    prompts_own, prompts_other, steps_own, steps_other, q_steps = refs[8:13]
    lhs, wide, total, q, prompts, scores, mixed, steps, cache, spread, sems = refs[13:]
    parity = idx_ref[CORE_AT]
    half_dim = HEAD_DIM // 2
    copies = Copies(sems)
    made = fetch_rows(copies, arrays, parts, lhs, 0)
    made += fetch_wide(copies, wide_refs, idx_ref[LAST_AT], parity, wide, 0)
    total_copy = copies(before, total)
    loads = []
    for group in range(HALF_REQ // 8):
        for ref, where in ((own_ref, parity), (other_ref, 1 - parity)):
            dims = pl.ds(pl.multiple_of(where * half_dim, half_dim), half_dim)
            loads.append(copies(ref.at[group], cache.at[group, :, dims]))
    spread_copy = copies(spread_ref, spread)
    for copy in made:
        copy.wait()
    rows = jnp.dot(lhs[...], wide[...], preferred_element_type=F32)
    total_copy.wait()
    total[...] += rows
    cosine, sine = all_angles(cos_ref, scos_ref), all_angles(sin_ref, ssin_ref)
    for head in range(GROUP):
        cols = slice(head * HEAD_DIM, (head + 1) * HEAD_DIM)
        rows = turn(total[:, cols] + qbias_ref[:, cols], cosine, sine).astype(BF16)
        q[:, cols] = rows[:ROWS]
        q_steps[:, cols] = rows[ROWS:].astype(F32)
    attend_prompts(q, kv_ref, prompts)
    halves(parity, prompts, prompts_own, prompts_other)
    for group in range(HALF_REQ // 8):
        for copy in loads[2 * group : 2 * group + 2]:
            copy.wait()
        attend_group(group, q_steps, kv_steps_ref, len_ref, cache.at[group], scores.at[group % 2], mixed)
    spread_copy.wait()
    rounded = mixed[...].reshape(OWN_STEPS, QCOLS).astype(BF16)
    steps[...] = jnp.dot(rounded, spread[...], preferred_element_type=F32).astype(BF16)
    halves(parity, steps, steps_own, steps_other)


def attention(arrays, parts, scalars, weights, before, caches, spread, operands):
    groups = HALF_REQ // 8
    split = (groups, 2 * BLOCK, HEAD_DIM // 2, GROUP * MAXB)
    prompts = jax.ShapeDtypeStruct((ROWS, QCOLS // 2), BF16)
    steps = jax.ShapeDtypeStruct((OWN_STEPS, QCOLS // 2), BF16)
    q_steps = jax.ShapeDtypeStruct((OWN_STEPS, QCOLS), F32)
    return from_hbm(
        functools.partial(attention_kernel, parts, len(arrays)),
        "attention",
        [prompts, prompts, steps, steps, q_steps],
        scalars,
        (*weights, before, *(cache.reshape(split) for cache in caches), spread, *arrays),
        operands,
        [
            pltpu.VMEM((ALL_ROWS, CHUNK), BF16),
            pltpu.VMEM((CHUNK, QCOLS), BF16),
            pltpu.VMEM((ALL_ROWS, QCOLS), F32),
            pltpu.VMEM((ROWS, QCOLS), BF16),
            pltpu.VMEM((ROWS, QCOLS), BF16),
            pltpu.VMEM((2, BLOCK, GROUP * STEPS * 8, 128), F32),
            pltpu.VMEM((STEPS, HALF_REQ, QCOLS), F32),
            pltpu.VMEM((OWN_STEPS, QCOLS), BF16),
            pltpu.VMEM((groups, 2 * BLOCK, HEAD_DIM, GROUP * MAXB), BF16),
            pltpu.VMEM((QCOLS, QCOLS), BF16),
            pltpu.SemaphoreType.DMA((len(parts) + 4 + 2 * groups,)),
        ],
    )


def arrived_kernel(
    par_ref, prompts_own_ref, prompts_other_ref, own_ref, other_ref,
    q_ref, kv_ref, q_other_ref, kv_other_ref, spread_ref, *refs,
):
    arrived, prompts_out, out_ref = refs[:4], refs[4], refs[5]
    for at, which in ((0, 0), (1, 1)):
        prompts_out[at * ROWS : (at + 1) * ROWS] = jnp.where(
            par_ref[0] == which, prompts_own_ref[...], prompts_other_ref[...]
        )
    own_cols = QCOLS // 2
    rows = 4 * GROUP * 8

    def by_arrival(shape, axis, size):
        which = lax.broadcasted_iota(jnp.int32, shape, axis) // size
        picked = jnp.zeros(shape, jnp.int32)
        for at in range(4):
            picked = jnp.where(which == at, requests[at], picked)
        return picked

    requests = [arrived[at][PROMPT : PROMPT + 16, :128].astype(jnp.int32)[:1, :1] for at in range(4)]
    shape = (32, OWN_STEPS)
    step = lax.broadcasted_iota(jnp.int32, shape, 0) % 8
    col = lax.broadcasted_iota(jnp.int32, shape, 1)
    parity = par_ref[0]

    def picked_rows(half, ref):
        request = col % HALF_REQ + half * HALF_REQ
        pick = (col // HALF_REQ == step) & (request == by_arrival(shape, 0, 8))
        pick = jnp.where(pick, 1.0, 0.0).astype(BF16)
        return jnp.dot(pick, ref[...].astype(BF16), preferred_element_type=F32)

    own = picked_rows(parity, q_ref) + picked_rows(1 - parity, q_other_ref)
    fresh = picked_rows(parity, kv_ref) + picked_rows(1 - parity, kv_other_ref)
    queries = jnp.concatenate(
        [
            own[at * 8 : (at + 1) * 8, m * HEAD_DIM : (m + 1) * HEAD_DIM]
            for at in range(4)
            for m in range(GROUP)
        ],
        axis=0,
    ).astype(BF16)
    fresh = jnp.concatenate([fresh, jnp.zeros((96, KVCOLS), F32)], axis=0).astype(BF16)
    part = GROUP * 8
    scores = jnp.concatenate(
        [
            lax.dot_general(
                queries[at * part : (at + 1) * part],
                arrived[at][:PROMPT, :HEAD_DIM],
                NT,
                preferred_element_type=F32,
            )
            for at in range(4)
        ],
        axis=0,
    )
    newer = lax.dot_general(queries, fresh[:, :HEAD_DIM], NT, preferred_element_type=F32)
    nrow = lax.broadcasted_iota(jnp.int32, (rows, 128), 0)
    nlane = lax.broadcasted_iota(jnp.int32, (rows, 128), 1)
    seen = (nlane // 8 == nrow // part) & (nlane % 8 < STEPS) & (nlane % 8 <= nrow % 8)
    newer = jnp.where(seen, newer, MASKED)
    peak = jnp.maximum(jnp.max(scores, axis=1, keepdims=True), jnp.max(newer, axis=1, keepdims=True))
    scores = jnp.exp2((scores - peak) * POWER)
    newer = jnp.exp2((newer - peak) * POWER)
    share = 1.0 / (jnp.sum(scores, axis=1, keepdims=True) + jnp.sum(newer, axis=1, keepdims=True))
    scores = (scores * share).astype(BF16)
    result = jnp.concatenate(
        [
            jnp.dot(
                scores[at * part : (at + 1) * part],
                arrived[at][:PROMPT, HEAD_DIM:],
                preferred_element_type=F32,
            )
            for at in range(4)
        ],
        axis=0,
    )
    result = result + jnp.dot(
        (newer * share).astype(BF16), fresh[:, HEAD_DIM:], preferred_element_type=F32
    )
    wide = jnp.concatenate(
        [
            jnp.concatenate(
                [result[at * part + m * 8 : at * part + (m + 1) * 8] for m in range(GROUP)], axis=1
            )
            for at in range(4)
        ],
        axis=0,
    )
    spread = spread_ref[:, pl.ds(pl.multiple_of(par_ref[0] * own_cols, own_cols), own_cols)]
    fixed = jnp.dot(wide.astype(BF16), spread, preferred_element_type=F32).astype(BF16)
    shape = (STEP_ROWS, 32)
    line = lax.broadcasted_iota(jnp.int32, shape, 0)
    step = lax.broadcasted_iota(jnp.int32, shape, 1) % 8
    back = (line == step * REQ_DEV + by_arrival(shape, 1, 8)) & (step < STEPS)
    placed = jnp.dot(jnp.where(back, 1.0, 0.0).astype(BF16), fixed, preferred_element_type=F32)
    line = lax.broadcasted_iota(jnp.int32, (STEP_ROWS, own_cols), 0) % REQ_DEV
    here = line == requests[0]
    for at in range(1, 4):
        here = here | (line == requests[at])
    mine, theirs = own_ref[...], other_ref[...]
    low = jnp.where(par_ref[0] == 0, mine, theirs)
    high = jnp.where(par_ref[0] == 0, theirs, mine)
    base = jnp.concatenate(
        [
            part[s * HALF_REQ : (s + 1) * HALF_REQ].astype(F32)
            for s in range(STEPS)
            for part in (low, high)
        ],
        axis=0,
    )
    out_ref[...] = jnp.where(here, placed, base).astype(BF16)


def arrived_attention(parity, halves_got, steps, spread, arrived):
    return resident(
        arrived_kernel,
        "arrived_attention",
        [
            jax.ShapeDtypeStruct((2 * ROWS, QCOLS // 2), BF16),
            jax.ShapeDtypeStruct((STEP_ROWS, QCOLS // 2), BF16),
        ],
        parity,
        (*halves_got, *steps, spread, *arrived),
        WHOLE_VMEM,
        cost(),
    )


def body(
    prompt_tokens,
    norm_gain,
    q_weight,
    k_weight,
    v_weight,
    q_bias,
    k_bias,
    v_bias,
    decode_tokens,
    k_cache,
    v_cache,
    block_table,
    context_len,
    prompt_dest,
):
    tp_rank = lax.axis_index("tp")
    dp_rank = lax.axis_index("dp")
    parity = tp_rank % 2
    chip = tp_rank // 2
    y_at, x_at = chip // 2, chip % 2
    lengths = context_len[0]
    parity_ref = parity[None].astype(jnp.int32)
    barrier = lax.optimization_barrier

    mine, theirs = split_rows(parity_ref, prompt_tokens[0], decode_tokens[0])
    held = join_features(parity_ref, mine, send(theirs, CORE))
    wide = held.astype(F32)
    squares = jnp.sum(wide * wide, axis=1)
    squares = squares + send(squares, XSWAP)
    squares = squares + sum(
        send(squares, [(i, (i + 4 * dy) % 16) for i in range(16)]) for dy in range(1, 4)
    )
    rstd = lax.rsqrt(squares * (1.0 / FEATURES) + NORM_EPSILON)[:, None]
    chip_cols = lambda array, width: lax.dynamic_slice_in_dim(array, chip * width, width, 0)[None, :]
    held = (wide * rstd * chip_cols(norm_gain, CHUNK)).astype(BF16)

    k_w, v_w, squares_done = barrier((k_weight.T, v_weight.T, squares))
    k_other, v_other = send(k_w, CORE), send(v_w, CORE)

    held, q_w, k_other, v_other = barrier((held, q_weight, k_other, v_other))
    side, up, down = send(held, XSWAP), send(held, YUP), send(held, YDOWN)
    wide_weights = (q_w, send(q_w, CORE))
    thin_weights = (k_w, k_other, v_w, v_other)
    weights = wide_weights + thin_weights

    table = block_table[0]
    turned = lambda cache: jnp.transpose(cache[0], (1, 2, 0)).reshape(BLOCK * HEAD_DIM // 2, NBLK)
    k_flat, v_flat = turned(k_cache), turned(v_cache)
    table, held = barrier((table.reshape(1, 2 * PAIRS), held))
    cache_theirs = arrange(1 - parity_ref, table, k_flat, v_flat)

    (cache_theirs, zero, lengths, q_bias, k_bias, v_bias) = barrier(
        (cache_theirs, jnp.int32(0), lengths, q_bias, k_bias, v_bias)
    )
    spread_row = lax.broadcasted_iota(jnp.int32, (QCOLS, QCOLS), 0) + zero
    spread_col = lax.broadcasted_iota(jnp.int32, (QCOLS, QCOLS), 1)
    spread = spread_col == (spread_row % HEAD_DIM) * GROUP + spread_row // HEAD_DIM
    spread = spread.astype(BF16)
    own_len = lax.dynamic_slice_in_dim(lengths, parity * HALF_REQ, HALF_REQ, 0)
    reach = jnp.repeat(own_len, MAXB)[None, :]

    exponent = jnp.arange(HEAD_DIM // 2, dtype=F32) * (2.0 / HEAD_DIM)
    frequency = jnp.power(F32(ROPE_BASE), -exponent)

    def angles(positions):
        angle = positions.astype(F32)[:, None] * frequency
        cosine, sine = jnp.cos(angle), jnp.sin(angle)
        return jnp.concatenate([cosine, cosine], axis=1), jnp.concatenate([-sine, sine], axis=1)

    prompt_angles = angles(jnp.arange(PROMPT, dtype=jnp.int32) + zero)
    step_angles = angles(
        (own_len[None, :] + jnp.arange(STEPS, dtype=jnp.int32)[:, None]).reshape(-1)
    )
    q_offset = chip_cols(q_bias, QCOLS)
    kv_offsets = (chip_cols(k_bias, HEAD_DIM), chip_cols(v_bias, HEAD_DIM))
    place = lambda dy, dx: ((y_at + dy) % 4) * 2 + (x_at + dx) % 2
    places = ((0, 0), (0, 1), (3, 0), (1, 0), (2, 0), (3, 1), (1, 1), (2, 1))
    scalars = jnp.concatenate(
        [jnp.stack([place(*at) for at in places] + [parity, dp_rank]).astype(jnp.int32), prompt_dest[0]]
    )

    (side, up, down, cache_theirs, reach, spread, offsets, both_angles, scalars) = barrier(
        (
            (side, up, down, cache_theirs, reach, spread)
            + ((q_offset, *kv_offsets), (*prompt_angles, *step_angles), scalars)
        )
    )
    side_up, far, side_down = send(side, YUP), send(down, YDOWN), send(down, XSWAP)
    cache_other = send(cache_theirs, CORE)
    table, side_sent = barrier((table, side))
    cache_own = arrange(parity_ref, table, k_flat, v_flat)
    totals = project(
        (held, side, up, down),
        tuple(((source, 0, ALL_ROWS),) for source in range(4)),
        ((0, 1), (1, 2), (2, 4)),
        0,
        scalars,
        weights,
    )

    side_up, far, side_down, totals, cache_own = barrier(
        (side_up, far, side_down, totals, cache_own)
    )
    cut_a, cut_b = 208, 416
    sent = take_parts(
        parity_ref, (side_up, side_down, far), ((0, cut_a), (cut_a, cut_b), (cut_b, ALL_ROWS))
    )
    sent, side_up, side_down, far = barrier((sent, side_up, side_down, far))
    last = (send(sent[0], YUP), send(sent[1], YDOWN), send(sent[2], XSWAP))
    q_total, kv_total = project(
        (far, side_up, side_down),
        tuple(((source, 0, ALL_ROWS),) for source in range(3)),
        ((0, 3),),
        4,
        scalars,
        weights,
        before=totals,
    )
    parts = ((0, 0, cut_a), (1, 0, cut_b - cut_a), (2, 0, ALL_ROWS - cut_b))
    kv, kv_steps = last_keys(
        last, parts, scalars, thin_weights, kv_total, (*offsets[1:], *both_angles)
    )

    kv_steps_other = send(kv_steps, CORE)
    blocks = handover(scalars, kv, send(kv, CORE))
    blocks, last, q_total, kv_steps_other = barrier((blocks, last, q_total, kv_steps_other))
    arrived = []
    for shift, block in enumerate(blocks):
        pairs = [(g * 4 + a, (1 - g) * 4 + (a + shift) % 4) for g in range(2) for a in range(4)]
        arrived.append(lax.ppermute(block, ("grp", "dp"), pairs))

    prefill_own, prefill_sent, decode_own, decode_sent, q_steps = attention(
        last,
        parts,
        scalars,
        wide_weights,
        q_total,
        (cache_own, cache_other),
        spread,
        (kv, kv_steps, reach, offsets[0], *both_angles),
    )
    arrived, prefill_sent, decode_sent, q_steps_sent = lax.optimization_barrier(
        (arrived, prefill_sent, decode_sent, q_steps)
    )
    steps = (q_steps, kv_steps, send(q_steps_sent, CORE), kv_steps_other)
    prefill_out, decode_out = arrived_attention(
        parity_ref,
        (prefill_own, send(prefill_sent, CORE), decode_own, send(decode_sent, CORE)),
        steps,
        spread,
        arrived,
    )
    prefill_out = prefill_out[None]
    return (prefill_out, decode_out.reshape(1, STEPS, REQ_DEV, -1))


def solution(mesh):
    placed = (
        P("grp", "dp", "tp"),
        P(),
        P(None, "tp"),
        P(None, "tp"),
        P(None, "tp"),
        P(),
        P(),
        P(),
        P("grp", None, "dp", "tp"),
        P("grp", "dp", None, "tp"),
        P("grp", "dp", None, "tp"),
        P("grp", "dp", None),
        P("grp", "dp"),
        P("grp", "dp"),
    )
    return jax.shard_map(
        body,
        mesh=mesh,
        in_specs=placed,
        out_specs=(P("grp", "dp", "tp"), P("grp", None, "dp", "tp")),
        check_vma=False,
    )
```

```python
import functools
import math

import jax
import jax.numpy as jnp
from jax import lax
from jax.experimental import pallas as pl
from jax.experimental.pallas import tpu as pltpu
from jax.sharding import PartitionSpec as P

HEAD_DIM = 128
GROUP = 8
BLOCK = 16
MAXB = 32
PROMPT = 256
REQ_DEV = 64
STEPS = 3
ROPE_BASE = 1000000.0
NORM_EPSILON = 1e-06
MASKED = -1e30
SCALE = 1.0 / math.sqrt(HEAD_DIM)
FEATURES = 8192
CHUNK = 1024
ROWS = 512
STEP_ROWS = STEPS * REQ_DEV
OWN_STEPS = STEP_ROWS // 2
ALL_ROWS = ROWS + OWN_STEPS
QCOLS = GROUP * HEAD_DIM
KVCOLS = 2 * HEAD_DIM
COLS = QCOLS + KVCOLS
HALF_REQ = REQ_DEV // 2
NBLK = 2048
PAIRS = HALF_REQ * MAXB
POWER = SCALE * math.log2(math.e)
WHOLE_VMEM = 58
LAST_AT = 7
CORE_AT = 8

CORE = [(i, i ^ 1) for i in range(16)]
XSWAP = [(i, i ^ 2) for i in range(16)]
YFAR = [(i, i ^ 8) for i in range(16)]
YUP = [(i, (i + 4) % 16) for i in range(16)]
YDOWN = [(i, (i + 12) % 16) for i in range(16)]

NT = (((1,), (1,)), ((), ()))
F32 = jnp.float32
BF16 = jnp.bfloat16


def send(array, pairs):
    return lax.ppermute(array, "tp", pairs)


def cost(*_):
    return pl.CostEstimate(flops=1, bytes_accessed=1, transcendentals=0)


def params(mebibytes):
    return pltpu.CompilerParams(vmem_limit_bytes=mebibytes * 1024 * 1024)


VMEM = pl.BlockSpec(memory_space=pltpu.VMEM)
SMEM = pl.BlockSpec(memory_space=pltpu.SMEM)


def resident(kernel, name, outs, scalars, operands, mebibytes, estimate, scratch=()):
    return pl.pallas_call(
        kernel,
        in_specs=[SMEM] + [VMEM] * len(operands),
        out_specs=[VMEM] * len(outs),
        out_shape=outs,
        scratch_shapes=list(scratch),
        compiler_params=params(mebibytes),
        cost_estimate=estimate,
        name=name,
    )(scalars, *operands)


HBM = pl.BlockSpec(memory_space=pltpu.HBM)


def arrange_kernel(which_ref, table_ref, k_ref, v_ref, out_ref, pick):
    tile = pick.shape[2]
    half = k_ref.shape[0]
    block = lax.broadcasted_iota(jnp.int32, (NBLK, tile), 0)
    for at in range(PAIRS // tile):
        lanes = pl.ds(pl.multiple_of(which_ref[0] * PAIRS + at * tile, tile), tile)
        slot = at % 2
        pick[slot] = jnp.where(block == table_ref[:, lanes], 1.0, 0.0).astype(BF16)
        out_ref[at, :half] = jnp.dot(k_ref[...], pick[slot], preferred_element_type=F32).astype(BF16)
        out_ref[at, half:] = jnp.dot(v_ref[...], pick[slot], preferred_element_type=F32).astype(BF16)


def arrange(which, table, k_flat, v_flat):
    rows = k_flat.shape[0]
    return resident(
        arrange_kernel,
        "arrange_cache",
        [jax.ShapeDtypeStruct((PAIRS // 256, 2 * rows, 256), BF16)],
        which,
        (table, k_flat, v_flat),
        WHOLE_VMEM,
        cost(),
        [pltpu.VMEM((2, NBLK, 256), BF16)],
    )[0]


def parts_kernel(cuts, _, *refs):
    for (start, stop), source, out in zip(cuts, refs[:3], refs[3:]):
        out[...] = source[start:stop]


def take_parts(scalars, arrays, cuts):
    outs = [jax.ShapeDtypeStruct((stop - start, CHUNK), BF16) for start, stop in cuts]
    return resident(functools.partial(parts_kernel, cuts), "take_parts", outs, scalars, arrays, 8, cost())


def handover_kernel(scalar_ref, own_ref, other_ref, *outs):
    parity, rank = scalar_ref[CORE_AT], scalar_ref[CORE_AT + 1]
    for shift in range(4):
        target = (rank + shift) % 4
        at = jnp.int32(0)
        request = jnp.int32(0)
        for prompt in range(4):
            chosen = scalar_ref[CORE_AT + 2 + prompt] // REQ_DEV == target
            at = jnp.where(chosen, prompt, at)
            request = jnp.where(chosen, scalar_ref[CORE_AT + 2 + prompt] % REQ_DEV, request)
        rows = pl.ds(pl.multiple_of((at % 2) * PROMPT, PROMPT), PROMPT)
        outs[shift][:PROMPT] = jnp.where(at // 2 == parity, own_ref[rows, :], other_ref[rows, :])
        outs[shift][PROMPT:] = jnp.full((16, 2 * HEAD_DIM), request.astype(F32), F32).astype(BF16)


def handover(scalars, own, other):
    shape = jax.ShapeDtypeStruct((PROMPT + 16, KVCOLS), BF16)
    return resident(
        handover_kernel, "sort_prompts", [shape] * 4, scalars, (own, other), 8, cost()
    )


def turn(rows, cosine, sine):
    return rows * cosine + pltpu.roll(rows, HEAD_DIM // 2, 1) * sine


class Copies:
    def __init__(self, sems):
        self.sems, self.made = sems, []

    def __call__(self, source, target):
        copy = pltpu.make_async_copy(source, target, self.sems.at[len(self.made)])
        copy.start()
        self.made.append(copy)
        return copy


def fetch_rows(copies, arrays, parts, lhs, at):
    cols = pl.ds(at * CHUNK, CHUNK)
    row, made = 0, []
    for source, start, stop in parts:
        target = lhs.at[pl.ds(row, stop - start), cols]
        made.append(copies(arrays[source].at[pl.ds(start, stop - start)], target))
        row += stop - start
    return made


def fetch_wide(copies, refs, chunk, parity, target, at):
    place = pl.ds(pl.multiple_of(chunk * CHUNK, CHUNK), CHUNK)
    half = QCOLS // 2
    made = []
    for ref, where in zip(refs, (parity, 1 - parity)):
        cols = pl.ds(pl.multiple_of(where * half, half), half)
        made.append(copies(ref.at[place, :], target.at[pl.ds(at * CHUNK, CHUNK), cols]))
    return made


def fetch_thin(copies, refs, chunk, parity, target, at):
    place = pl.ds(pl.multiple_of(chunk * CHUNK, CHUNK), CHUNK)
    half = HEAD_DIM // 2
    made = []
    for which, pair in enumerate((refs[:2], refs[2:])):
        for ref, where in zip(pair, (parity, 1 - parity)):
            rows = pl.ds(pl.multiple_of(which * HEAD_DIM + where * half, half), half)
            made.append(copies(ref.at[:, place], target.at[rows, pl.ds(at * CHUNK, CHUNK)]))
    return made


def project_kernel(chunks, order, base, count, first, idx_ref, *refs):
    wide_refs, thin_refs, refs = refs[:2], refs[2:6], refs[6:]
    arrays, refs = refs[:count], refs[count:]
    before, refs = ((), refs) if first else (refs[:2], refs[2:])
    q_total, kv_total, lhs, wide, thin, sems = refs[:6]
    parity = idx_ref[CORE_AT]
    copies = Copies(sems)
    groups = []
    for at, parts in enumerate(chunks):
        groups.append(
            fetch_rows(copies, arrays, parts, lhs, at)
            + fetch_wide(copies, wide_refs, idx_ref[base + at], parity, wide, at)
            + fetch_thin(copies, thin_refs, idx_ref[base + at], parity, thin, at)
        )
    if not first:
        groups[0] += [copies(before[0], refs[6]), copies(before[1], refs[7])]
        earlier = refs[6:8]
    for number, (start, stop) in enumerate(order):
        for group in groups[start:stop]:
            for copy in group:
                copy.wait()
        span = slice(start * CHUNK, stop * CHUNK)
        q_part = jnp.dot(lhs[:, span], wide[span, :], preferred_element_type=F32)
        kv_part = lax.dot_general(lhs[:, span], thin[:, span], NT, preferred_element_type=F32)
        if number:
            q_total[...] += q_part
            kv_total[...] += kv_part
        elif first:
            q_total[...] = q_part
            kv_total[...] = kv_part
        else:
            q_total[...] = earlier[0][...] + q_part
            kv_total[...] = earlier[1][...] + kv_part


def from_hbm(kernel, name, outs, scalars, operands, resident_operands, scratch, limit=58):
    return pl.pallas_call(
        kernel,
        in_specs=[SMEM] + [HBM] * len(operands) + [VMEM] * len(resident_operands),
        out_specs=[VMEM] * len(outs),
        out_shape=outs,
        scratch_shapes=scratch,
        compiler_params=params(limit),
        cost_estimate=cost(),
        name=name,
    )(scalars, *operands, *resident_operands)


def project(arrays, chunks, order, base, scalars, weights, before=()):
    count = len(chunks)
    totals = [(ALL_ROWS, QCOLS), (ALL_ROWS, KVCOLS)]
    scratch = [
        pltpu.VMEM((ALL_ROWS, count * CHUNK), BF16),
        pltpu.VMEM((count * CHUNK, QCOLS), BF16),
        pltpu.VMEM((KVCOLS, count * CHUNK), BF16),
        pltpu.SemaphoreType.DMA((sum(len(parts) + 6 for parts in chunks) + 2,)),
    ]
    if before:
        scratch += [pltpu.VMEM(shape, F32) for shape in totals]
    return from_hbm(
        functools.partial(project_kernel, chunks, order, base, len(arrays), not before),
        "project_rows",
        [jax.ShapeDtypeStruct(shape, F32) for shape in totals],
        scalars,
        (*weights, *arrays, *before),
        (),
        scratch,
    )


def all_angles(first, second):
    return jnp.concatenate([first[...]] * (ROWS // PROMPT) + [second[...]], axis=0)


def keys_kernel(parts, count, idx_ref, *refs):
    thin_refs, before = refs[:4], refs[4]
    arrays, refs = refs[5 : 5 + count], refs[5 + count :]
    kb_ref, vb_ref, cos_ref, sin_ref, scos_ref, ssin_ref, out_ref, steps_out, lhs, thin, total, sems = refs
    copies = Copies(sems)
    made = fetch_rows(copies, arrays, parts, lhs, 0)
    made += fetch_thin(copies, thin_refs, idx_ref[LAST_AT], idx_ref[CORE_AT], thin, 0)
    made.append(copies(before, total))
    for copy in made:
        copy.wait()
    rows = total[...] + lax.dot_general(lhs[...], thin[...], NT, preferred_element_type=F32)
    cosine, sine = all_angles(cos_ref, scos_ref), all_angles(sin_ref, ssin_ref)
    keys = turn(rows[:, :HEAD_DIM] + kb_ref[...], cosine, sine).astype(BF16)
    values = (rows[:, HEAD_DIM:] + vb_ref[...]).astype(BF16)
    out_ref[:, :HEAD_DIM] = keys[:ROWS]
    out_ref[:, HEAD_DIM:] = values[:ROWS]
    steps_out[:, :HEAD_DIM] = keys[ROWS:].astype(F32)
    steps_out[:, HEAD_DIM:] = values[ROWS:].astype(F32)


def last_keys(arrays, parts, scalars, weights, before, ending):
    return from_hbm(
        functools.partial(keys_kernel, parts, len(arrays)),
        "project_keys",
        [jax.ShapeDtypeStruct((ROWS, KVCOLS), BF16), jax.ShapeDtypeStruct((OWN_STEPS, KVCOLS), F32)],
        scalars,
        (*weights, before, *arrays),
        ending,
        [
            pltpu.VMEM((ALL_ROWS, CHUNK), BF16),
            pltpu.VMEM((KVCOLS, CHUNK), BF16),
            pltpu.VMEM((ALL_ROWS, KVCOLS), F32),
            pltpu.SemaphoreType.DMA((len(parts) + 5,)),
        ],
    )


def split_kernel(par_ref, prompts_ref, steps_ref, own_out, other_out, sems):
    copies = Copies(sems)
    for out, which in ((other_out, 1 - par_ref[0]), (own_out, par_ref[0])):
        rows = pl.ds(pl.multiple_of(which * ROWS, ROWS), ROWS)
        copies(prompts_ref.at[rows], out.at[pl.ds(0, ROWS)])
        rows = pl.ds(pl.multiple_of(which * HALF_REQ, HALF_REQ), HALF_REQ)
        for s in range(STEPS):
            copies(steps_ref.at[s, rows], out.at[pl.ds(ROWS + s * HALF_REQ, HALF_REQ)])
    for copy in copies.made:
        copy.wait()


def split_rows(scalars, prompts, steps):
    half = jax.ShapeDtypeStruct((ALL_ROWS, prompts.shape[1]), BF16)
    return pl.pallas_call(
        split_kernel,
        in_specs=[SMEM, HBM, HBM],
        out_specs=[VMEM] * 2,
        out_shape=[half] * 2,
        scratch_shapes=[pltpu.SemaphoreType.DMA((2 + 2 * STEPS,))],
        compiler_params=params(8),
        cost_estimate=cost(),
        name="split_rows",
    )(scalars, prompts, steps)


def join_kernel(par_ref, own_ref, other_ref, out_ref):
    half = own_ref.shape[1]
    own, other = own_ref[...], other_ref[...]
    out_ref[:, :half] = jnp.where(par_ref[0] == 0, own, other)
    out_ref[:, half:] = jnp.where(par_ref[0] == 0, other, own)


def join_features(parity, own, other):
    out = jax.ShapeDtypeStruct((own.shape[0], 2 * own.shape[1]), BF16)
    return resident(join_kernel, "join_features", [out], parity, (own, other), 8, cost())[0]


def halves(parity, wide, own_out, other_out):
    half = wide.shape[1] // 2
    own_out[...] = jnp.where(parity == 0, wide[:, :half], wide[:, half:])
    other_out[...] = jnp.where(parity == 0, wide[:, half:], wide[:, :half])


def attend_prompts(q, kv_ref, out):
    row = lax.broadcasted_iota(jnp.int32, (PROMPT, PROMPT), 0)
    col = lax.broadcasted_iota(jnp.int32, (PROMPT, PROMPT), 1)
    causal = row >= col
    for prompt in range(ROWS // PROMPT):
        rows = slice(prompt * PROMPT, (prompt + 1) * PROMPT)
        keys, values = kv_ref[rows, :HEAD_DIM], kv_ref[rows, HEAD_DIM:]
        for head in range(GROUP):
            cols = slice(head * HEAD_DIM, (head + 1) * HEAD_DIM)
            scores = lax.dot_general(q[rows, cols], keys, NT, preferred_element_type=F32)
            scores = jnp.where(causal, scores, MASKED)
            powers = jnp.exp2((scores - jnp.max(scores, axis=1, keepdims=True)) * POWER)
            weights = (powers * (1.0 / jnp.sum(powers, axis=1, keepdims=True))).astype(BF16)
            out[rows, cols] = jnp.dot(weights, values, preferred_element_type=F32).astype(BF16)


def attend_group(group, q_ref, kv_ref, len_ref, cache, scores, mixed):
    rows = GROUP * STEPS * 8
    lanes = GROUP * MAXB

    def step_rows(s):
        return slice(s * HALF_REQ + group * 8, s * HALF_REQ + group * 8 + 8)

    queries = jnp.concatenate(
        [
            q_ref[step_rows(s), m * HEAD_DIM : (m + 1) * HEAD_DIM]
            for m in range(GROUP)
            for s in range(STEPS)
        ],
        axis=0,
    ).astype(BF16)
    row = lax.broadcasted_iota(jnp.int32, (rows, 128), 0) % 8
    lane = lax.broadcasted_iota(jnp.int32, (rows, 128), 1)
    lower = row < 4
    reach = len_ref[:, group * lanes : (group + 1) * lanes]
    reach = jnp.where(lower, reach[:, :128], reach[:, 128:])
    place = jnp.where(row % 4 == lane // MAXB, (lane % MAXB) * BLOCK, MAXB * BLOCK * 2) - reach
    top = jnp.full((rows, 128), MASKED, F32)
    for slot in range(BLOCK):
        part = jnp.dot(queries, cache[slot], preferred_element_type=F32)
        part = jnp.where(lower, part[:, :128], part[:, 128:])
        part = jnp.where(place < -slot, part, MASKED)
        scores[slot] = part
        top = jnp.maximum(top, part)
    fresh = jnp.concatenate([kv_ref[step_rows(s), :] for s in range(STEPS)], axis=0)
    fresh = jnp.concatenate([fresh, jnp.zeros((128 - 8 * STEPS, KVCOLS), F32)], axis=0).astype(BF16)
    newer = lax.dot_general(queries, fresh[:, :HEAD_DIM], NT, preferred_element_type=F32)
    at_step = (lax.broadcasted_iota(jnp.int32, (rows, 128), 0) // 8) % STEPS
    newer = jnp.where((row == lane % 8) & (lane // 8 <= at_step), newer, MASKED)
    peak = jnp.max(jnp.maximum(top, newer), axis=1, keepdims=True)
    newer = jnp.exp2((newer - peak) * POWER)
    weight_sum = newer
    for slot in range(BLOCK):
        powers = jnp.exp2((scores[slot] - peak) * POWER)
        scores[slot] = powers
        weight_sum = weight_sum + powers
    share = 1.0 / jnp.sum(weight_sum, axis=1, keepdims=True)
    result = jnp.dot(
        (newer * share).astype(BF16), fresh[:, HEAD_DIM:], preferred_element_type=F32
    )
    for start in range(0, BLOCK, BLOCK):
        slots = range(start, start + BLOCK)
        pieces = []
        for slot in slots:
            weight = scores[slot] * share
            pieces += [jnp.where(lower, weight, 0.0), jnp.where(lower, 0.0, weight)]
        weights = jnp.concatenate([piece.astype(BF16) for piece in pieces], axis=1)
        values = jnp.concatenate([cache[BLOCK + slot] for slot in slots], axis=1)
        result = result + lax.dot_general(weights, values, NT, preferred_element_type=F32)
    for m in range(GROUP):
        for s in range(STEPS):
            at = (m * STEPS + s) * 8
            mixed[s, group * 8 : (group + 1) * 8, m * HEAD_DIM : (m + 1) * HEAD_DIM] = result[at : at + 8]


def attention_kernel(parts, count, idx_ref, *refs):
    wide_refs, before, own_ref, other_ref, spread_ref = refs[:2], refs[2], refs[3], refs[4], refs[5]
    arrays, refs = refs[6 : 6 + count], refs[6 + count :]
    kv_ref, kv_steps_ref, len_ref, qbias_ref, cos_ref, sin_ref, scos_ref, ssin_ref = refs[:8]
    prompts_own, prompts_other, steps_own, steps_other, q_steps = refs[8:13]
    lhs, wide, total, q, prompts, scores, mixed, steps, cache, spread, sems = refs[13:]
    parity = idx_ref[CORE_AT]
    half_dim = HEAD_DIM // 2
    copies = Copies(sems)
    made = fetch_rows(copies, arrays, parts, lhs, 0)
    made += fetch_wide(copies, wide_refs, idx_ref[LAST_AT], parity, wide, 0)
    total_copy = copies(before, total)
    loads = []
    for group in range(HALF_REQ // 8):
        for ref, where in ((own_ref, parity), (other_ref, 1 - parity)):
            dims = pl.ds(pl.multiple_of(where * half_dim, half_dim), half_dim)
            loads.append(copies(ref.at[group], cache.at[group, :, dims]))
    spread_copy = copies(spread_ref, spread)
    for copy in made:
        copy.wait()
    rows = jnp.dot(lhs[...], wide[...], preferred_element_type=F32)
    total_copy.wait()
    total[...] += rows
    cosine, sine = all_angles(cos_ref, scos_ref), all_angles(sin_ref, ssin_ref)
    for head in range(GROUP):
        cols = slice(head * HEAD_DIM, (head + 1) * HEAD_DIM)
        rows = turn(total[:, cols] + qbias_ref[:, cols], cosine, sine).astype(BF16)
        q[:, cols] = rows[:ROWS]
        q_steps[:, cols] = rows[ROWS:].astype(F32)
    attend_prompts(q, kv_ref, prompts)
    halves(parity, prompts, prompts_own, prompts_other)
    for group in range(HALF_REQ // 8):
        for copy in loads[2 * group : 2 * group + 2]:
            copy.wait()
        attend_group(group, q_steps, kv_steps_ref, len_ref, cache.at[group], scores.at[group % 2], mixed)
    spread_copy.wait()
    rounded = mixed[...].reshape(OWN_STEPS, QCOLS).astype(BF16)
    steps[...] = jnp.dot(rounded, spread[...], preferred_element_type=F32).astype(BF16)
    halves(parity, steps, steps_own, steps_other)


def attention(arrays, parts, scalars, weights, before, caches, spread, operands):
    groups = HALF_REQ // 8
    split = (groups, 2 * BLOCK, HEAD_DIM // 2, GROUP * MAXB)
    prompts = jax.ShapeDtypeStruct((ROWS, QCOLS // 2), BF16)
    steps = jax.ShapeDtypeStruct((OWN_STEPS, QCOLS // 2), BF16)
    q_steps = jax.ShapeDtypeStruct((OWN_STEPS, QCOLS), F32)
    return from_hbm(
        functools.partial(attention_kernel, parts, len(arrays)),
        "attention",
        [prompts, prompts, steps, steps, q_steps],
        scalars,
        (*weights, before, *(cache.reshape(split) for cache in caches), spread, *arrays),
        operands,
        [
            pltpu.VMEM((ALL_ROWS, CHUNK), BF16),
            pltpu.VMEM((CHUNK, QCOLS), BF16),
            pltpu.VMEM((ALL_ROWS, QCOLS), F32),
            pltpu.VMEM((ROWS, QCOLS), BF16),
            pltpu.VMEM((ROWS, QCOLS), BF16),
            pltpu.VMEM((2, BLOCK, GROUP * STEPS * 8, 128), F32),
            pltpu.VMEM((STEPS, HALF_REQ, QCOLS), F32),
            pltpu.VMEM((OWN_STEPS, QCOLS), BF16),
            pltpu.VMEM((groups, 2 * BLOCK, HEAD_DIM, GROUP * MAXB), BF16),
            pltpu.VMEM((QCOLS, QCOLS), BF16),
            pltpu.SemaphoreType.DMA((len(parts) + 4 + 2 * groups,)),
        ],
    )


def arrived_kernel(
    par_ref, prompts_own_ref, prompts_other_ref, own_ref, other_ref,
    q_ref, kv_ref, q_other_ref, kv_other_ref, spread_ref, *refs,
):
    arrived, prompts_out, out_ref = refs[:4], refs[4], refs[5]
    for at, which in ((0, 0), (1, 1)):
        prompts_out[at * ROWS : (at + 1) * ROWS] = jnp.where(
            par_ref[0] == which, prompts_own_ref[...], prompts_other_ref[...]
        )
    own_cols = QCOLS // 2
    rows = 4 * GROUP * 8

    def by_arrival(shape, axis, size):
        which = lax.broadcasted_iota(jnp.int32, shape, axis) // size
        picked = jnp.zeros(shape, jnp.int32)
        for at in range(4):
            picked = jnp.where(which == at, requests[at], picked)
        return picked

    requests = [arrived[at][PROMPT : PROMPT + 16, :128].astype(jnp.int32)[:1, :1] for at in range(4)]
    shape = (32, OWN_STEPS)
    step = lax.broadcasted_iota(jnp.int32, shape, 0) % 8
    col = lax.broadcasted_iota(jnp.int32, shape, 1)
    parity = par_ref[0]

    def picked_rows(half, ref):
        request = col % HALF_REQ + half * HALF_REQ
        pick = (col // HALF_REQ == step) & (request == by_arrival(shape, 0, 8))
        pick = jnp.where(pick, 1.0, 0.0).astype(BF16)
        return jnp.dot(pick, ref[...].astype(BF16), preferred_element_type=F32)

    own = picked_rows(parity, q_ref) + picked_rows(1 - parity, q_other_ref)
    fresh = picked_rows(parity, kv_ref) + picked_rows(1 - parity, kv_other_ref)
    queries = jnp.concatenate(
        [
            own[at * 8 : (at + 1) * 8, m * HEAD_DIM : (m + 1) * HEAD_DIM]
            for at in range(4)
            for m in range(GROUP)
        ],
        axis=0,
    ).astype(BF16)
    fresh = jnp.concatenate([fresh, jnp.zeros((96, KVCOLS), F32)], axis=0).astype(BF16)
    part = GROUP * 8
    scores = jnp.concatenate(
        [
            lax.dot_general(
                queries[at * part : (at + 1) * part],
                arrived[at][:PROMPT, :HEAD_DIM],
                NT,
                preferred_element_type=F32,
            )
            for at in range(4)
        ],
        axis=0,
    )
    newer = lax.dot_general(queries, fresh[:, :HEAD_DIM], NT, preferred_element_type=F32)
    nrow = lax.broadcasted_iota(jnp.int32, (rows, 128), 0)
    nlane = lax.broadcasted_iota(jnp.int32, (rows, 128), 1)
    seen = (nlane // 8 == nrow // part) & (nlane % 8 < STEPS) & (nlane % 8 <= nrow % 8)
    newer = jnp.where(seen, newer, MASKED)
    peak = jnp.maximum(jnp.max(scores, axis=1, keepdims=True), jnp.max(newer, axis=1, keepdims=True))
    scores = jnp.exp2((scores - peak) * POWER)
    newer = jnp.exp2((newer - peak) * POWER)
    share = 1.0 / (jnp.sum(scores, axis=1, keepdims=True) + jnp.sum(newer, axis=1, keepdims=True))
    scores = (scores * share).astype(BF16)
    result = jnp.concatenate(
        [
            jnp.dot(
                scores[at * part : (at + 1) * part],
                arrived[at][:PROMPT, HEAD_DIM:],
                preferred_element_type=F32,
            )
            for at in range(4)
        ],
        axis=0,
    )
    result = result + jnp.dot(
        (newer * share).astype(BF16), fresh[:, HEAD_DIM:], preferred_element_type=F32
    )
    wide = jnp.concatenate(
        [
            jnp.concatenate(
                [result[at * part + m * 8 : at * part + (m + 1) * 8] for m in range(GROUP)], axis=1
            )
            for at in range(4)
        ],
        axis=0,
    )
    spread = spread_ref[:, pl.ds(pl.multiple_of(par_ref[0] * own_cols, own_cols), own_cols)]
    fixed = jnp.dot(wide.astype(BF16), spread, preferred_element_type=F32).astype(BF16)
    shape = (STEP_ROWS, 32)
    line = lax.broadcasted_iota(jnp.int32, shape, 0)
    step = lax.broadcasted_iota(jnp.int32, shape, 1) % 8
    back = (line == step * REQ_DEV + by_arrival(shape, 1, 8)) & (step < STEPS)
    placed = jnp.dot(jnp.where(back, 1.0, 0.0).astype(BF16), fixed, preferred_element_type=F32)
    line = lax.broadcasted_iota(jnp.int32, (STEP_ROWS, own_cols), 0) % REQ_DEV
    here = line == requests[0]
    for at in range(1, 4):
        here = here | (line == requests[at])
    mine, theirs = own_ref[...], other_ref[...]
    low = jnp.where(par_ref[0] == 0, mine, theirs)
    high = jnp.where(par_ref[0] == 0, theirs, mine)
    base = jnp.concatenate(
        [
            part[s * HALF_REQ : (s + 1) * HALF_REQ].astype(F32)
            for s in range(STEPS)
            for part in (low, high)
        ],
        axis=0,
    )
    out_ref[...] = jnp.where(here, placed, base).astype(BF16)


def arrived_attention(parity, halves_got, steps, spread, arrived):
    return resident(
        arrived_kernel,
        "arrived_attention",
        [
            jax.ShapeDtypeStruct((2 * ROWS, QCOLS // 2), BF16),
            jax.ShapeDtypeStruct((STEP_ROWS, QCOLS // 2), BF16),
        ],
        parity,
        (*halves_got, *steps, spread, *arrived),
        WHOLE_VMEM,
        cost(),
    )


def body(
    prompt_tokens,
    norm_gain,
    q_weight,
    k_weight,
    v_weight,
    q_bias,
    k_bias,
    v_bias,
    decode_tokens,
    k_cache,
    v_cache,
    block_table,
    context_len,
    prompt_dest,
):
    tp_rank = lax.axis_index("tp")
    dp_rank = lax.axis_index("dp")
    parity = tp_rank % 2
    chip = tp_rank // 2
    y_at, x_at = chip // 2, chip % 2
    lengths = context_len[0]
    parity_ref = parity[None].astype(jnp.int32)
    barrier = lax.optimization_barrier

    mine, theirs = split_rows(parity_ref, prompt_tokens[0], decode_tokens[0])
    held = join_features(parity_ref, mine, send(theirs, CORE))
    wide = held.astype(F32)
    squares = jnp.sum(wide * wide, axis=1)
    squares = squares + send(squares, XSWAP)
    squares = squares + sum(
        send(squares, [(i, (i + 4 * dy) % 16) for i in range(16)]) for dy in range(1, 4)
    )
    rstd = lax.rsqrt(squares * (1.0 / FEATURES) + NORM_EPSILON)[:, None]
    chip_cols = lambda array, width: lax.dynamic_slice_in_dim(array, chip * width, width, 0)[None, :]
    held = (wide * rstd * chip_cols(norm_gain, CHUNK)).astype(BF16)

    k_w, v_w, squares_done = barrier((k_weight.T, v_weight.T, squares))
    k_other, v_other = send(k_w, CORE), send(v_w, CORE)

    held, q_w, k_other, v_other = barrier((held, q_weight, k_other, v_other))
    side, up, down = send(held, XSWAP), send(held, YUP), send(held, YDOWN)
    wide_weights = (q_w, send(q_w, CORE))
    thin_weights = (k_w, k_other, v_w, v_other)
    weights = wide_weights + thin_weights

    table = block_table[0]
    turned = lambda cache: jnp.transpose(cache[0], (1, 2, 0)).reshape(BLOCK * HEAD_DIM // 2, NBLK)
    k_flat, v_flat = turned(k_cache), turned(v_cache)
    table, held = barrier((table.reshape(1, 2 * PAIRS), held))
    cache_theirs = arrange(1 - parity_ref, table, k_flat, v_flat)

    (cache_theirs, zero, lengths, q_bias, k_bias, v_bias) = barrier(
        (cache_theirs, jnp.int32(0), lengths, q_bias, k_bias, v_bias)
    )
    spread_row = lax.broadcasted_iota(jnp.int32, (QCOLS, QCOLS), 0) + zero
    spread_col = lax.broadcasted_iota(jnp.int32, (QCOLS, QCOLS), 1)
    spread = spread_col == (spread_row % HEAD_DIM) * GROUP + spread_row // HEAD_DIM
    spread = spread.astype(BF16)
    own_len = lax.dynamic_slice_in_dim(lengths, parity * HALF_REQ, HALF_REQ, 0)
    reach = jnp.repeat(own_len, MAXB)[None, :]

    exponent = jnp.arange(HEAD_DIM // 2, dtype=F32) * (2.0 / HEAD_DIM)
    frequency = jnp.power(F32(ROPE_BASE), -exponent)

    def angles(positions):
        angle = positions.astype(F32)[:, None] * frequency
        cosine, sine = jnp.cos(angle), jnp.sin(angle)
        return jnp.concatenate([cosine, cosine], axis=1), jnp.concatenate([-sine, sine], axis=1)

    prompt_angles = angles(jnp.arange(PROMPT, dtype=jnp.int32) + zero)
    step_angles = angles(
        (own_len[None, :] + jnp.arange(STEPS, dtype=jnp.int32)[:, None]).reshape(-1)
    )
    q_offset = chip_cols(q_bias, QCOLS)
    kv_offsets = (chip_cols(k_bias, HEAD_DIM), chip_cols(v_bias, HEAD_DIM))
    place = lambda dy, dx: ((y_at + dy) % 4) * 2 + (x_at + dx) % 2
    places = ((0, 0), (0, 1), (3, 0), (1, 0), (2, 0), (3, 1), (1, 1), (2, 1))
    scalars = jnp.concatenate(
        [jnp.stack([place(*at) for at in places] + [parity, dp_rank]).astype(jnp.int32), prompt_dest[0]]
    )

    (side, up, down, cache_theirs, reach, spread, offsets, both_angles, scalars) = barrier(
        (
            (side, up, down, cache_theirs, reach, spread)
            + ((q_offset, *kv_offsets), (*prompt_angles, *step_angles), scalars)
        )
    )
    side_up, far, side_down = send(side, YUP), send(down, YDOWN), send(down, XSWAP)
    cache_other = send(cache_theirs, CORE)
    table, side_sent = barrier((table, side))
    cache_own = arrange(parity_ref, table, k_flat, v_flat)
    totals = project(
        (held, side, up, down),
        tuple(((source, 0, ALL_ROWS),) for source in range(4)),
        ((0, 1), (1, 2), (2, 4)),
        0,
        scalars,
        weights,
    )

    side_up, far, side_down, totals, cache_own = barrier(
        (side_up, far, side_down, totals, cache_own)
    )
    cut_a, cut_b = 208, 416
    sent = take_parts(
        parity_ref, (side_up, side_down, far), ((0, cut_a), (cut_a, cut_b), (cut_b, ALL_ROWS))
    )
    sent, side_up, side_down, far = barrier((sent, side_up, side_down, far))
    last = (send(sent[0], YUP), send(sent[1], YDOWN), send(sent[2], XSWAP))
    q_total, kv_total = project(
        (far, side_up, side_down),
        tuple(((source, 0, ALL_ROWS),) for source in range(3)),
        ((0, 3),),
        4,
        scalars,
        weights,
        before=totals,
    )
    parts = ((0, 0, cut_a), (1, 0, cut_b - cut_a), (2, 0, ALL_ROWS - cut_b))
    kv, kv_steps = last_keys(
        last, parts, scalars, thin_weights, kv_total, (*offsets[1:], *both_angles)
    )

    kv_steps_other = send(kv_steps, CORE)
    blocks = handover(scalars, kv, send(kv, CORE))
    blocks, last, q_total, kv_steps_other = barrier((blocks, last, q_total, kv_steps_other))
    arrived = []
    for shift, block in enumerate(blocks):
        pairs = [(g * 4 + a, (1 - g) * 4 + (a + shift) % 4) for g in range(2) for a in range(4)]
        arrived.append(lax.ppermute(block, ("grp", "dp"), pairs))

    prefill_own, prefill_sent, decode_own, decode_sent, q_steps = attention(
        last,
        parts,
        scalars,
        wide_weights,
        q_total,
        (cache_own, cache_other),
        spread,
        (kv, kv_steps, reach, offsets[0], *both_angles),
    )
    arrived, prefill_sent, decode_sent, q_steps_sent = lax.optimization_barrier(
        (arrived, prefill_sent, decode_sent, q_steps)
    )
    steps = (q_steps, kv_steps, send(q_steps_sent, CORE), kv_steps_other)
    prefill_out, decode_out = arrived_attention(
        parity_ref,
        (prefill_own, send(prefill_sent, CORE), decode_own, send(decode_sent, CORE)),
        steps,
        spread,
        arrived,
    )
    prefill_out = prefill_out[None]
    return (prefill_out, decode_out.reshape(1, STEPS, REQ_DEV, -1))


def solution(mesh):
    placed = (
        P("grp", "dp", "tp"),
        P(),
        P(None, "tp"),
        P(None, "tp"),
        P(None, "tp"),
        P(),
        P(),
        P(),
        P("grp", None, "dp", "tp"),
        P("grp", "dp", None, "tp"),
        P("grp", "dp", None, "tp"),
        P("grp", "dp", None),
        P("grp", "dp"),
        P("grp", "dp"),
    )
    return jax.shard_map(
        body,
        mesh=mesh,
        in_specs=placed,
        out_specs=(P("grp", "dp", "tp"), P("grp", None, "dp", "tp")),
        check_vma=False,
    )
```
